32 devices in a mesh: hours: 2 (over x), chan: 2 (over core), freq: 8 (over z, y).
Axes of the slice: x: 2, y: 2, z: 4, core: 2. Of those that a mesh axis runs over, the one named last changes fastest.
Arguments:
- samples: bfloat16 [1152, 32, 1024], P('chan', ('hours', 'freq')), parts along dimension 1, may hold values from -18 to 18
Outputs:
- cross_spectra: bfloat16 [2, 256, 1152, 1152], P(None, ('hours', 'freq'), None, 'chan'), parts along dimension 1
The draws below stay inside these ranges and needn't reach their ends.
There are 2 independent parts, one for each index of `hours`. The reference program is written for one: setup_inputs(seed, part) draws one part's arguments, and reference() takes and returns one part's arrays. A program takes and returns all parts, laid end to end along the dimension named above; each array names one. Nothing has to cross between parts.
All inputs are finite; a program needn't handle non-finite values.
Results may differ from the reference program's by a relative error of at most 0.008.
Values may be sent and summed in bfloat16 or wider, within the bound.
No kernel may reach another device: no remote copies, remote signals or barrier semaphores. Data moves between devices by JAX's collectives and lax.ppermute only.
A program may use at most 192 MiB of HBM per device.

```python
import math
import jax
import jax.numpy as jnp
from jax import lax

CHANNELS = 1152
SAMPLES = 1024
BINS = 128
WINDOWS = 16


def draw_samples(key, part):
    first, second = jax.random.split(jax.random.fold_in(key, 7), 2)
    gains = jnp.exp(jax.random.uniform(first, (CHANNELS, 1, 1), jnp.float32, math.log(0.1), math.log(3.0)))
    values = jnp.clip(jax.random.normal(second, (CHANNELS, WINDOWS, SAMPLES), jnp.float32), -6.0, 6.0)
    return (gains * values).astype(jnp.bfloat16)


def setup_inputs(seed: int = 0, part: int = 0) -> dict:
    arg_keys = jax.random.split(jax.random.key(seed), 2)
    part_keys = jax.random.split(jax.random.fold_in(arg_keys[1], part), 2)
    samples = draw_samples(jax.random.fold_in(jax.random.fold_in(arg_keys[1], part), 71), part)
    return dict(samples=samples)


def bin_table(length, bins):
    position = lax.broadcasted_iota(jnp.int32, (length, bins), 0)
    number = lax.broadcasted_iota(jnp.int32, (length, bins), 1) + 1
    phase = (position * number % length).astype(jnp.float32) * (2.0 * math.pi / length)
    taper = 0.5 - 0.5 * jnp.cos(position.astype(jnp.float32) * (2.0 * math.pi / length))
    factor = math.sqrt(8.0 / (3.0 * length))
    table = jnp.concatenate([taper * jnp.cos(phase), -(taper * jnp.sin(phase))], axis=1) * factor
    return table.astype(jnp.bfloat16)

def whiten(padded, first_bin, total_bins):
    count_bins = padded.shape[1] - 4
    values = padded.astype(jnp.float32)
    power = values[0] * values[0] + values[1] * values[1]
    summed = power[0:count_bins] + power[1:count_bins + 1]
    summed = summed + power[2:count_bins + 2]
    summed = summed + power[3:count_bins + 3]
    summed = summed + power[4:count_bins + 4]
    which = first_bin + jnp.arange(count_bins, dtype=jnp.int32)
    upper = jnp.minimum(which + 2, total_bins - 1)
    lower = jnp.maximum(which - 2, 0)
    count = (upper - lower + 1).astype(jnp.float32)
    level = jnp.maximum(summed / count[:, None, None], 0.1)
    return (values[:, 2:count_bins + 2] / jnp.sqrt(level)[None]).astype(jnp.bfloat16)

def reference(samples):
    channels, windows, length = samples.shape
    table = bin_table(length, BINS)
    flat = jnp.dot(samples.reshape(channels * windows, length), table, preferred_element_type=jnp.float32)
    spectrum = flat.reshape(channels, windows, 2, BINS).transpose(2, 3, 1, 0).astype(jnp.bfloat16)
    padded = jnp.pad(spectrum, ((0, 0), (2, 2), (0, 0), (0, 0)))
    whitened = whiten(padded, 0, BINS)

    def one_bin(index):
        single = lax.dynamic_index_in_dim(whitened, index, 1, keepdims=False).astype(jnp.float32)
        real_part = jnp.einsum('pwa,pwb->ab', single, single)
        rotated = jnp.stack([-single[1], single[0]])
        imag_part = jnp.einsum('pwa,pwb->ab', single, rotated)
        return (jnp.stack([real_part, imag_part]) / windows).astype(jnp.bfloat16)
    stacked = lax.map(one_bin, jnp.arange(BINS, dtype=jnp.int32))
    return jnp.transpose(stacked, (1, 0, 3, 2))
```

```python
import functools
import math

import jax
import jax.numpy as jnp
import ml_dtypes
import numpy as np
from jax import lax
from jax.experimental import pallas as pl
from jax.experimental.pallas import tpu as pltpu
from jax.sharding import PartitionSpec as P

BINS = 128
LANES = 128
VMEM_BYTES = 56 * 1024 * 1024


def bin_table(length, bins, group):
    position = np.arange(length)[None, :]
    number = np.arange(1, bins + 1)[:, None]
    phase = (position * number % length).astype(np.float32) * np.float32(2.0 * math.pi / length)
    taper = np.float32(0.5) - np.float32(0.5) * np.cos(
        position.astype(np.float32) * np.float32(2.0 * math.pi / length)
    )
    factor = np.float32(math.sqrt(8.0 / (3.0 * length)))
    table = np.stack([taper * np.cos(phase), -(taper * np.sin(phase))]) * factor
    table = table.reshape(2, bins // group, group, length).transpose(1, 0, 2, 3)
    return table.reshape(2 * bins, length).astype(ml_dtypes.bfloat16)


def channel_blocks(channels):
    return [
        (first, min(LANES, channels - first), 2 * first) for first in range(0, channels, LANES)
    ]


def whiten_kernel(group, samples_ref, table_ref, out_ref):
    channels, windows, _ = samples_ref.shape
    bins = table_ref.shape[0] // 2
    table = table_ref[...]
    row = lax.broadcasted_iota(jnp.int32, (bins, 1), 0)
    count = jnp.minimum(row + 2, bins - 1) - jnp.maximum(row - 2, 0) + 1
    share = 1.0 / count.astype(jnp.float32)

    for first, width, lane in channel_blocks(channels):
        blocks = [
            lax.dot_general(
                table,
                samples_ref[first : first + width, w, :],
                (((1,), (1,)), ((), ())),
                preferred_element_type=jnp.float32,
            )
            for w in range(windows)
        ]
        spectrum = jnp.concatenate(blocks, axis=1).astype(jnp.bfloat16).astype(jnp.float32)
        cols = windows * width
        parts = spectrum.reshape(bins // group, 2, group, cols)
        power = (parts[:, 0] * parts[:, 0] + parts[:, 1] * parts[:, 1]).reshape(bins, cols)
        summed = power
        for step in (1, 2):
            summed = summed + jnp.where(row >= step, pltpu.roll(power, step, axis=0), 0.0)
            summed = summed + jnp.where(
                row < bins - step, pltpu.roll(power, bins - step, axis=0), 0.0
            )
        level = jnp.maximum(summed * share, 0.1)
        inverse = lax.rsqrt(level).reshape(bins // group, 1, group, cols)
        whitened = (parts * inverse).reshape(2 * bins, cols).astype(jnp.bfloat16)
        out_ref[:, lane : lane + cols] = whitened


def swap_halves(tile):
    return pltpu.roll(tile, LANES // 2, axis=1)


def outer_kernel(bins, scale, own_ref, other_ref, out_ref, right, left):
    half = LANES // 2
    channels = out_ref.shape[2]
    full = channels // LANES
    step = pl.program_id(1)

    @pl.when(step == 0)
    def _():
        me = lax.axis_index("chan")
        which = pl.program_id(0)
        own = own_ref[:, which].astype(jnp.float32)
        other = other_ref[:, which].astype(jnp.float32)
        rows = own.shape[0] * own.shape[1]
        own = own.reshape(rows, own.shape[2])
        other = other.reshape(rows, other.shape[2])
        block0 = jnp.where(me == 0, own, other)
        block1 = jnp.where(me == 0, other, own)
        row = lax.broadcasted_iota(jnp.int32, (rows, 1), 0)
        first_part = (row // bins) % 2 == 0
        low = lax.broadcasted_iota(jnp.int32, (rows, LANES), 1) < half

        def tiles_of(block, w):
            tiles = [
                block[:, (2 * j + w) * LANES : (2 * j + w + 1) * LANES] for j in range(full)
            ]
            last = block[:, 2 * full * LANES :]
            turned = swap_halves(last)
            both = jnp.where(low, last, turned) if w == 0 else jnp.where(low, turned, last)
            return tiles, both

        for w in range(2):
            at = pl.ds(w * rows, rows)
            tiles, last0 = tiles_of(block0, w)
            tiles1, last1 = tiles_of(block1, w)
            turned = [swap_halves(tile) for tile in tiles1]
            chain = [last0] + turned + [last1]
            tiles = tiles + [
                jnp.where(low, chain[j], chain[j + 1]) for j in range(len(chain) - 1)
            ]
            for j, tile in enumerate(tiles):
                rotated = jnp.where(
                    first_part,
                    -pltpu.roll(tile, rows - bins, axis=0),
                    pltpu.roll(tile, bins, axis=0),
                )
                right[at, j * LANES : (j + 1) * LANES] = tile.astype(jnp.bfloat16)
                right[at, 2 * channels + j * LANES : 2 * channels + (j + 1) * LANES] = (
                    rotated.astype(jnp.bfloat16)
                )
        scaled = own * scale
        for j in range(full):
            for w in range(2):
                lanes = (2 * j + w) * LANES
                left[j * LANES : (j + 1) * LANES, w * rows : (w + 1) * rows] = scaled[
                    :, lanes : lanes + LANES
                ].T
        last = scaled[:, 2 * full * LANES :].T
        for w in range(2):
            left[full * LANES :, w * rows : (w + 1) * rows] = last[w * half : (w + 1) * half]

    depth = left.shape[1]
    lane = lax.broadcasted_iota(jnp.int32, (channels, depth), 1)
    chosen = jnp.where(lane % bins == step, left[...], 0.0).astype(jnp.bfloat16)
    width = 2 * LANES
    for tile in range(4 * channels // width):
        product = jnp.dot(
            chosen,
            right[:, tile * width : (tile + 1) * width],
            preferred_element_type=jnp.float32,
        ).astype(jnp.bfloat16)
        for piece in range(2):
            lanes = tile * width + piece * LANES
            part, lanes = lanes // (2 * channels), lanes % (2 * channels)
            out_ref[part, 0, :, lanes : lanes + LANES] = product[
                :, piece * LANES : (piece + 1) * LANES
            ]


def local(samples):
    local_channels, local_windows, length = samples.shape
    devices = lax.axis_size("freq")
    local_bins = BINS // devices
    windows = local_windows * devices
    bins = min(local_bins, 128 // (2 * devices))
    groups = local_bins // bins
    aligned = bins % 8 == 0
    group = bins if aligned else BINS
    table = jnp.asarray(bin_table(length, BINS, group))
    lanes = local_windows * local_channels
    vmem = pl.BlockSpec(memory_space=pltpu.VMEM)
    params = pltpu.CompilerParams(vmem_limit_bytes=VMEM_BYTES)

    with jax.named_scope("whiten"):
        whitened = pl.pallas_call(
            functools.partial(whiten_kernel, group),
            out_shape=jax.ShapeDtypeStruct((2 * BINS, lanes), jnp.bfloat16),
            in_specs=[vmem, vmem],
            out_specs=vmem,
            compiler_params=params,
            cost_estimate=pl.CostEstimate(
                flops=4 * BINS * lanes * length, bytes_accessed=3 << 20, transcendentals=BINS * lanes
            ),
        )(samples, table)
    if aligned:
        whitened = whitened.reshape(devices, groups, 2 * bins, lanes)
    else:
        whitened = whitened.reshape(2, devices, groups, bins, lanes).transpose(1, 2, 0, 3, 4)
        whitened = whitened.reshape(devices, groups, 2 * bins, lanes)
    own = lax.all_to_all(whitened, "freq", split_axis=0, concat_axis=0, tiled=True)
    if not aligned:
        own = own.transpose(1, 0, 2, 3).reshape(1, groups, devices * 2 * bins, lanes)
    other = lax.ppermute(own, "chan", [(0, 1), (1, 0)])
    depth = local_windows * devices * 2 * bins
    with jax.named_scope("outer_products"):
        out = pl.pallas_call(
            functools.partial(outer_kernel, bins, 1.0 / windows),
            out_shape=jax.ShapeDtypeStruct(
                (2, local_bins, local_channels, 2 * local_channels), jnp.bfloat16
            ),
            grid=(groups, bins),
            in_specs=[vmem, vmem],
            out_specs=pl.BlockSpec(
                (2, 1, local_channels, 2 * local_channels),
                lambda g, k: (0, g * bins + k, 0, 0),
            ),
            scratch_shapes=[
                pltpu.VMEM((depth, 4 * local_channels), jnp.bfloat16),
                pltpu.VMEM((local_channels, depth), jnp.float32),
            ],
            compiler_params=params,
            cost_estimate=pl.CostEstimate(
                flops=8 * local_bins * depth * local_channels * local_channels,
                bytes_accessed=8 * local_bins * local_channels * local_channels,
                transcendentals=0,
            ),
        )(own, other)
    return jnp.transpose(out, (0, 1, 3, 2))


def solution(mesh):
    placed = (P("chan", ("hours", "freq"), None),)
    return jax.shard_map(
        local,
        mesh=mesh,
        in_specs=placed,
        out_specs=P(None, ("hours", "freq"), None, "chan"),
        check_vma=False,
    )
```

```python
import functools
import math

import jax
import jax.numpy as jnp
import ml_dtypes
import numpy as np
from jax import lax
from jax.experimental import pallas as pl
from jax.experimental.pallas import tpu as pltpu
from jax.sharding import PartitionSpec as P

BINS = 128
LANES = 128
MIB = 1024 * 1024


def bin_table(length, bins, group):
    position = np.arange(length)[None, :]
    number = np.arange(1, bins + 1)[:, None]
    phase = (position * number % length).astype(np.float32) * np.float32(2.0 * math.pi / length)
    taper = np.float32(0.5) - np.float32(0.5) * np.cos(
        position.astype(np.float32) * np.float32(2.0 * math.pi / length)
    )
    factor = np.float32(math.sqrt(8.0 / (3.0 * length)))
    table = np.stack([taper * np.cos(phase), -(taper * np.sin(phase))]) * factor
    table = table.reshape(2, bins // group, group, length).transpose(3, 1, 0, 2)
    return table.reshape(length, 2 * bins).astype(ml_dtypes.bfloat16)


def channel_blocks(channels):
    return [
        (first, min(LANES, channels - first), 2 * first) for first in range(0, channels, LANES)
    ]


def whiten_kernel(group, spectrum_ref, *refs):
    pieces, rows_ref = refs[:-1], refs[-1]
    windows, channels, columns = spectrum_ref.shape
    bins = columns // 2
    row = lax.broadcasted_iota(jnp.int32, (bins, 1), 0)
    count = jnp.minimum(row + 2, bins - 1) - jnp.maximum(row - 2, 0) + 1
    share = 1.0 / count.astype(jnp.float32)

    for first, width, lane in channel_blocks(channels):
        blocks = [
            spectrum_ref[w, first : first + width, :].astype(jnp.float32).T
            for w in range(windows)
        ]
        spectrum = jnp.concatenate(blocks, axis=1)
        cols = windows * width
        parts = spectrum.reshape(bins // group, 2, group, cols)
        power = (parts[:, 0] * parts[:, 0] + parts[:, 1] * parts[:, 1]).reshape(bins, cols)
        summed = power
        for step in (1, 2):
            summed = summed + jnp.where(row >= step, pltpu.roll(power, step, axis=0), 0.0)
            summed = summed + jnp.where(
                row < bins - step, pltpu.roll(power, bins - step, axis=0), 0.0
            )
        level = jnp.maximum(summed * share, 0.1)
        inverse = lax.rsqrt(level).reshape(bins // group, 1, group, cols)
        whitened = (parts * inverse).astype(jnp.bfloat16)
        rows_ref[..., lane : lane + cols] = whitened.reshape(rows_ref.shape[:-1] + (cols,))

    if len(pieces) == 1:
        pieces[0][...] = rows_ref[...]
    else:
        me = lax.axis_index("freq")
        for m, piece in enumerate(pieces):
            piece[...] = rows_ref[me ^ m]


def swap_halves(tile):
    return pltpu.roll(tile, LANES // 2, axis=1)


def outer_kernel(bins, scale, *refs):
    out_ref, right, left = refs[-3:]
    count = (len(refs) - 3) // 2
    own_refs, other_refs = refs[:count], refs[count:-3]
    half = LANES // 2
    channels = out_ref.shape[2]
    full = channels // LANES
    step = pl.program_id(1)

    @pl.when(step == 0)
    def _():
        me = lax.axis_index("chan")
        which = pl.program_id(0)
        own = jnp.concatenate([ref[which].astype(jnp.float32) for ref in own_refs])
        other = jnp.concatenate([ref[which].astype(jnp.float32) for ref in other_refs])
        rows = own.shape[0]
        block0 = jnp.where(me == 0, own, other)
        block1 = jnp.where(me == 0, other, own)
        row = lax.broadcasted_iota(jnp.int32, (rows, 1), 0)
        first_part = (row // bins) % 2 == 0
        low = lax.broadcasted_iota(jnp.int32, (rows, LANES), 1) < half

        def tiles_of(block, w):
            tiles = [
                block[:, (2 * j + w) * LANES : (2 * j + w + 1) * LANES] for j in range(full)
            ]
            last = block[:, 2 * full * LANES :]
            turned = swap_halves(last)
            both = jnp.where(low, last, turned) if w == 0 else jnp.where(low, turned, last)
            return tiles, both

        for w in range(2):
            at = pl.ds(w * rows, rows)
            tiles, last0 = tiles_of(block0, w)
            tiles1, last1 = tiles_of(block1, w)
            turned = [swap_halves(tile) for tile in tiles1]
            chain = [last0] + turned + [last1]
            tiles = tiles + [
                jnp.where(low, chain[j], chain[j + 1]) for j in range(len(chain) - 1)
            ]
            for j, tile in enumerate(tiles):
                rotated = jnp.where(
                    first_part,
                    -pltpu.roll(tile, rows - bins, axis=0),
                    pltpu.roll(tile, bins, axis=0),
                )
                right[at, j * LANES : (j + 1) * LANES] = tile.astype(jnp.bfloat16)
                right[at, 2 * channels + j * LANES : 2 * channels + (j + 1) * LANES] = (
                    rotated.astype(jnp.bfloat16)
                )
        scaled = own * scale
        for j in range(full):
            for w in range(2):
                lanes = (2 * j + w) * LANES
                left[j * LANES : (j + 1) * LANES, w * rows : (w + 1) * rows] = scaled[
                    :, lanes : lanes + LANES
                ].T
        last = scaled[:, 2 * full * LANES :].T
        for w in range(2):
            left[full * LANES :, w * rows : (w + 1) * rows] = last[w * half : (w + 1) * half]

    depth = left.shape[1]
    lane = lax.broadcasted_iota(jnp.int32, (1, depth), 1)
    chosen = jnp.where((lane & (bins - 1)) == step, left[...], 0.0).astype(jnp.bfloat16)
    product = jnp.dot(chosen, right[...], preferred_element_type=jnp.float32)
    for part in range(2):
        lanes = part * 2 * channels
        out_ref[part, 0] = product[:, lanes : lanes + 2 * channels].astype(jnp.bfloat16)


def local(samples):
    local_channels, local_windows, length = samples.shape
    devices = lax.axis_size("freq")
    local_bins = BINS // devices
    windows = local_windows * devices
    bins = min(local_bins, 128 // (2 * devices))
    groups = local_bins // bins
    aligned = bins % 8 == 0
    group = bins if aligned else BINS
    table = jnp.asarray(bin_table(length, BINS, group))
    lanes = local_windows * local_channels
    vmem = pl.BlockSpec(memory_space=pltpu.VMEM)

    spectrum = jnp.einsum("cws,sj->wcj", samples, table, preferred_element_type=jnp.float32)
    spectrum = spectrum.astype(jnp.bfloat16)
    pieces = devices if aligned else 1
    rows = (devices, groups, 2 * bins, lanes) if aligned else (2 * BINS, lanes)
    piece = rows[1:] if aligned else rows
    with jax.named_scope("whiten"):
        whitened = pl.pallas_call(
            functools.partial(whiten_kernel, group),
            out_shape=[jax.ShapeDtypeStruct(piece, jnp.bfloat16)] * pieces,
            in_specs=[vmem],
            out_specs=[vmem] * pieces,
            scratch_shapes=[pltpu.VMEM(rows, jnp.bfloat16)],
            compiler_params=pltpu.CompilerParams(vmem_limit_bytes=16 * MIB),
            cost_estimate=pl.CostEstimate(
                flops=40 * BINS * lanes, bytes_accessed=12 * BINS * lanes, transcendentals=BINS * lanes
            ),
        )(spectrum)
    if aligned:
        own = [whitened[0]] + [None] * (devices - 1)
        for m in reversed(range(1, devices)):
            pairs = [(source, source ^ m) for source in range(devices)]
            own[m] = lax.ppermute(whitened[m], "freq", pairs)
    else:
        rows = whitened[0].reshape(2, devices, groups, bins, lanes).transpose(1, 2, 0, 3, 4)
        rows = rows.reshape(devices, groups, 2 * bins, lanes)
        rows = lax.all_to_all(rows, "freq", split_axis=0, concat_axis=0, tiled=True)
        own = [rows.transpose(1, 0, 2, 3).reshape(groups, devices * 2 * bins, lanes)]
    other = [lax.ppermute(value, "chan", [(0, 1), (1, 0)]) for value in own]
    depth = local_windows * devices * 2 * bins
    with jax.named_scope("outer_products"):
        out = pl.pallas_call(
            functools.partial(outer_kernel, bins, 1.0 / windows),
            out_shape=jax.ShapeDtypeStruct(
                (2, local_bins, local_channels, 2 * local_channels), jnp.bfloat16
            ),
            grid=(groups, bins),
            in_specs=[vmem] * (2 * pieces),
            out_specs=pl.BlockSpec(
                (2, 1, local_channels, 2 * local_channels),
                lambda g, k: (0, g * bins + k, 0, 0),
            ),
            scratch_shapes=[
                pltpu.VMEM((depth, 4 * local_channels), jnp.bfloat16),
                pltpu.VMEM((local_channels, depth), jnp.float32),
            ],
            compiler_params=pltpu.CompilerParams(vmem_limit_bytes=32 * MIB),
            cost_estimate=pl.CostEstimate(
                flops=8 * local_bins * depth * local_channels * local_channels,
                bytes_accessed=8 * local_bins * local_channels * local_channels,
                transcendentals=0,
            ),
        )(*own, *other)
    return jnp.transpose(out, (0, 1, 3, 2))


def solution(mesh):
    placed = (P("chan", ("hours", "freq"), None),)
    return jax.shard_map(
        local,
        mesh=mesh,
        in_specs=placed,
        out_specs=P(None, ("hours", "freq"), None, "chan"),
        check_vma=False,
    )
```

```python
import functools
import math

import jax
import jax.numpy as jnp
import ml_dtypes
import numpy as np
from jax import lax
from jax.experimental import pallas as pl
from jax.experimental.pallas import tpu as pltpu
from jax.sharding import PartitionSpec as P

BINS = 128
LANES = 128
MIB = 1024 * 1024


def bin_table(length, bins, group):
    position = np.arange(length)[None, :]
    number = np.arange(1, bins + 1)[:, None]
    phase = (position * number % length).astype(np.float32) * np.float32(2.0 * math.pi / length)
    taper = np.float32(0.5) - np.float32(0.5) * np.cos(
        position.astype(np.float32) * np.float32(2.0 * math.pi / length)
    )
    factor = np.float32(math.sqrt(8.0 / (3.0 * length)))
    table = np.stack([taper * np.cos(phase), -(taper * np.sin(phase))]) * factor
    table = table.reshape(2, bins // group, group, length).transpose(3, 1, 0, 2)
    return table.reshape(length, 2 * bins).astype(ml_dtypes.bfloat16)


def channel_blocks(channels):
    return [
        (first, min(LANES, channels - first), 2 * first) for first in range(0, channels, LANES)
    ]


def whiten_kernel(group, masks, spectrum_ref, *refs):
    pieces, rows_ref = refs[:-1], refs[-1]
    windows, channels, columns = spectrum_ref.shape
    bins = columns // 2
    row = lax.broadcasted_iota(jnp.int32, (bins, 1), 0)
    count = jnp.minimum(row + 2, bins - 1) - jnp.maximum(row - 2, 0) + 1
    share = 1.0 / count.astype(jnp.float32)

    for first, width, lane in channel_blocks(channels):
        blocks = [
            spectrum_ref[w, first : first + width, :].astype(jnp.float32).T
            for w in range(windows)
        ]
        spectrum = jnp.concatenate(blocks, axis=1)
        cols = windows * width
        parts = spectrum.reshape(bins // group, 2, group, cols)
        power = (parts[:, 0] * parts[:, 0] + parts[:, 1] * parts[:, 1]).reshape(bins, cols)
        summed = power
        for step in (1, 2):
            summed = summed + jnp.where(row >= step, pltpu.roll(power, step, axis=0), 0.0)
            summed = summed + jnp.where(
                row < bins - step, pltpu.roll(power, bins - step, axis=0), 0.0
            )
        level = jnp.maximum(summed * share, 0.1)
        inverse = lax.rsqrt(level).reshape(bins // group, 1, group, cols)
        whitened = (parts * inverse).astype(jnp.bfloat16)
        rows_ref[..., lane : lane + cols] = whitened.reshape(rows_ref.shape[:-1] + (cols,))

    if len(pieces) == 1:
        pieces[0][...] = rows_ref[...]
    else:
        me = lax.axis_index("freq")
        for mask, piece in zip(masks, pieces):
            piece[...] = rows_ref[me ^ mask]


def swap_halves(tile):
    return pltpu.roll(tile, LANES // 2, axis=1)


def outer_kernel(bins, scale, *refs):
    out_ref, right, left, slots, sems = refs[-5:]
    count = (len(refs) - 5) // 2
    own_refs, other_refs = refs[:count], refs[count:-5]
    half = LANES // 2
    channels = out_ref.shape[2]
    full = channels // LANES
    step = pl.program_id(1)
    now = pl.program_id(0) * bins + step
    steps = pl.num_programs(0) * bins
    depth_of_slots, cuts = sems.shape[:2]
    size = channels // cuts

    def copy(when, cut, part):
        slot = lax.rem(when, depth_of_slots)
        at = pl.ds(cut * size, size)
        return pltpu.make_async_copy(
            slots.at[slot, part, at], out_ref.at[part, when, at], sems.at[slot, cut, part]
        )

    def wait_for(when):
        for cut in range(cuts):
            for part in range(2):
                copy(when, cut, part).wait()

    @pl.when(step == 0)
    def _():
        me = lax.axis_index("chan")
        which = pl.program_id(0)
        own = jnp.concatenate([ref[which].astype(jnp.float32) for ref in own_refs])
        other = jnp.concatenate([ref[which].astype(jnp.float32) for ref in other_refs])
        rows = own.shape[0]
        block0 = jnp.where(me == 0, own, other)
        block1 = jnp.where(me == 0, other, own)
        row = lax.broadcasted_iota(jnp.int32, (rows, 1), 0)
        first_part = (row // bins) % 2 == 0
        low = lax.broadcasted_iota(jnp.int32, (rows, LANES), 1) < half

        def tiles_of(block, w):
            tiles = [
                block[:, (2 * j + w) * LANES : (2 * j + w + 1) * LANES] for j in range(full)
            ]
            last = block[:, 2 * full * LANES :]
            turned = swap_halves(last)
            both = jnp.where(low, last, turned) if w == 0 else jnp.where(low, turned, last)
            return tiles, both

        for w in range(2):
            at = pl.ds(w * rows, rows)
            tiles, last0 = tiles_of(block0, w)
            tiles1, last1 = tiles_of(block1, w)
            turned = [swap_halves(tile) for tile in tiles1]
            chain = [last0] + turned + [last1]
            tiles = tiles + [
                jnp.where(low, chain[j], chain[j + 1]) for j in range(len(chain) - 1)
            ]
            for j, tile in enumerate(tiles):
                rotated = jnp.where(
                    first_part,
                    -pltpu.roll(tile, rows - bins, axis=0),
                    pltpu.roll(tile, bins, axis=0),
                )
                right[at, j * LANES : (j + 1) * LANES] = tile.astype(jnp.bfloat16)
                right[at, 2 * channels + j * LANES : 2 * channels + (j + 1) * LANES] = (
                    rotated.astype(jnp.bfloat16)
                )
        scaled = own * scale
        for j in range(full):
            for w in range(2):
                lanes = (2 * j + w) * LANES
                left[j * LANES : (j + 1) * LANES, w * rows : (w + 1) * rows] = scaled[
                    :, lanes : lanes + LANES
                ].T
        last = scaled[:, 2 * full * LANES :].T
        for w in range(2):
            left[full * LANES :, w * rows : (w + 1) * rows] = last[w * half : (w + 1) * half]

    depth = left.shape[1]
    lane = lax.broadcasted_iota(jnp.int32, (1, depth), 1)
    chosen = jnp.where((lane & (bins - 1)) == step, left[...], 0.0).astype(jnp.bfloat16)
    @pl.when(now >= depth_of_slots)
    def _():
        wait_for(now - depth_of_slots)

    slot = lax.rem(now, depth_of_slots)
    for cut in range(cuts):
        at = slice(cut * size, (cut + 1) * size)
        product = jnp.dot(chosen[at], right[...], preferred_element_type=jnp.float32)
        for part in range(2):
            lanes = part * 2 * channels
            slots[slot, part, at] = product[:, lanes : lanes + 2 * channels].astype(jnp.bfloat16)
            copy(now, cut, part).start()

    @pl.when(now == steps - 1)
    def _():
        for back in reversed(range(depth_of_slots)):
            wait_for(now - back)


def local(samples):
    local_channels, local_windows, length = samples.shape
    devices = lax.axis_size("freq")
    local_bins = BINS // devices
    windows = local_windows * devices
    bins = min(local_bins, 128 // (2 * devices))
    groups = local_bins // bins
    aligned = bins % 8 == 0
    group = bins if aligned else BINS
    table = jnp.asarray(bin_table(length, BINS, group))
    lanes = local_windows * local_channels
    vmem = pl.BlockSpec(memory_space=pltpu.VMEM)

    memory = pl.BlockSpec(memory_space=pl.ANY)
    spectrum = jnp.einsum("cws,sj->wcj", samples, table, preferred_element_type=jnp.float32)
    spectrum = spectrum.astype(jnp.bfloat16)
    masks = [1, 2, *range(devices - 1, 2, -1), 0] if aligned else [0]
    pieces = len(masks)
    rows = (devices, groups, 2 * bins, lanes) if aligned else (2 * BINS, lanes)
    piece = rows[1:] if aligned else rows
    with jax.named_scope("whiten"):
        whitened = pl.pallas_call(
            functools.partial(whiten_kernel, group, masks),
            out_shape=[jax.ShapeDtypeStruct(piece, jnp.bfloat16)] * pieces,
            in_specs=[vmem],
            out_specs=[vmem] * pieces,
            scratch_shapes=[pltpu.VMEM(rows, jnp.bfloat16)],
            compiler_params=pltpu.CompilerParams(vmem_limit_bytes=16 * MIB),
            cost_estimate=pl.CostEstimate(
                flops=40 * BINS * lanes, bytes_accessed=12 * BINS * lanes, transcendentals=BINS * lanes
            ),
        )(spectrum)
    if aligned:
        own = []
        for mask, value in zip(masks, whitened):
            pairs = [(source, source ^ mask) for source in range(devices)]
            own.append(lax.ppermute(value, "freq", pairs) if mask else value)
    else:
        rows = whitened[0].reshape(2, devices, groups, bins, lanes).transpose(1, 2, 0, 3, 4)
        rows = rows.reshape(devices, groups, 2 * bins, lanes)
        rows = lax.all_to_all(rows, "freq", split_axis=0, concat_axis=0, tiled=True)
        own = [rows.transpose(1, 0, 2, 3).reshape(groups, devices * 2 * bins, lanes)]
    other = [lax.ppermute(value, "chan", [(0, 1), (1, 0)]) for value in own]
    depth = local_windows * devices * 2 * bins
    with jax.named_scope("outer_products"):
        out = pl.pallas_call(
            functools.partial(outer_kernel, bins, 1.0 / windows),
            out_shape=jax.ShapeDtypeStruct(
                (2, local_bins, local_channels, 2 * local_channels), jnp.bfloat16
            ),
            grid=(groups, bins),
            in_specs=[vmem] * (2 * pieces),
            out_specs=memory,
            scratch_shapes=[
                pltpu.VMEM((depth, 4 * local_channels), jnp.bfloat16),
                pltpu.VMEM((local_channels, depth), jnp.float32),
                pltpu.VMEM((3, 2, local_channels, 2 * local_channels), jnp.bfloat16),
                pltpu.SemaphoreType.DMA((3, 2, 2)),
            ],
            compiler_params=pltpu.CompilerParams(vmem_limit_bytes=32 * MIB),
            cost_estimate=pl.CostEstimate(
                flops=8 * local_bins * depth * local_channels * local_channels,
                bytes_accessed=8 * local_bins * local_channels * local_channels,
                transcendentals=0,
            ),
        )(*own, *other)
    return jnp.transpose(out, (0, 1, 3, 2))


def solution(mesh):
    placed = (P("chan", ("hours", "freq"), None),)
    return jax.shard_map(
        local,
        mesh=mesh,
        in_specs=placed,
        out_specs=P(None, ("hours", "freq"), None, "chan"),
        check_vma=False,
    )
```

```python
import functools
import math

import jax
import jax.numpy as jnp
import ml_dtypes
import numpy as np
from jax import lax
from jax.experimental import pallas as pl
from jax.experimental.pallas import tpu as pltpu
from jax.sharding import PartitionSpec as P

BINS = 128
LANES = 128
TILE = 256
BLOCK = 96
AHEAD = 3
MIB = 1024 * 1024


def bin_table(length, bins, group):
    position = np.arange(length)[None, :]
    number = np.arange(1, bins + 1)[:, None]
    phase = (position * number % length).astype(np.float32) * np.float32(2.0 * math.pi / length)
    taper = np.float32(0.5) - np.float32(0.5) * np.cos(
        position.astype(np.float32) * np.float32(2.0 * math.pi / length)
    )
    factor = np.float32(math.sqrt(8.0 / (3.0 * length)))
    table = np.stack([taper * np.cos(phase), -(taper * np.sin(phase))]) * factor
    table = table.reshape(2, bins // group, group, length).transpose(3, 1, 0, 2)
    return table.reshape(length, 2 * bins).astype(ml_dtypes.bfloat16)


def channel_blocks(channels):
    return [
        (first, min(LANES, channels - first), 2 * first) for first in range(0, channels, LANES)
    ]


def whiten_kernel(group, masks, spectrum_ref, *refs):
    pieces, rows_ref = refs[:-1], refs[-1]
    windows, channels, columns = spectrum_ref.shape
    bins = columns // 2
    row = lax.broadcasted_iota(jnp.int32, (bins, 1), 0)
    count = jnp.minimum(row + 2, bins - 1) - jnp.maximum(row - 2, 0) + 1
    share = 1.0 / count.astype(jnp.float32)

    for first, width, lane in channel_blocks(channels):
        blocks = [
            spectrum_ref[w, first : first + width, :].astype(jnp.float32).T
            for w in range(windows)
        ]
        spectrum = jnp.concatenate(blocks, axis=1)
        cols = windows * width
        parts = spectrum.reshape(bins // group, 2, group, cols)
        power = (parts[:, 0] * parts[:, 0] + parts[:, 1] * parts[:, 1]).reshape(bins, cols)
        summed = power
        for step in (1, 2):
            summed = summed + jnp.where(row >= step, pltpu.roll(power, step, axis=0), 0.0)
            summed = summed + jnp.where(
                row < bins - step, pltpu.roll(power, bins - step, axis=0), 0.0
            )
        level = jnp.maximum(summed * share, 0.1)
        inverse = lax.rsqrt(level).reshape(bins // group, 1, group, cols)
        whitened = (parts * inverse).astype(jnp.bfloat16)
        rows_ref[..., lane : lane + cols] = whitened.reshape(rows_ref.shape[:-1] + (cols,))

    if len(pieces) == 1:
        pieces[0][...] = rows_ref[...]
    else:
        me = lax.axis_index("freq")
        for mask, piece in zip(masks, pieces):
            piece[...] = rows_ref[me ^ mask]


def swap_halves(tile):
    return pltpu.roll(tile, LANES // 2, axis=1)


def outer_kernel(bins, scale, *refs):
    out_ref, right, left, slots, sems = refs[-5:]
    count = (len(refs) - 5) // 2
    own_refs, other_refs = refs[:count], refs[count:-5]
    half = LANES // 2
    channels = out_ref.shape[2]
    full = channels // LANES
    step = pl.program_id(1)
    now = pl.program_id(0) * bins + step
    steps = pl.num_programs(0) * bins
    depth_of_slots, cuts = sems.shape[:2]
    size = channels // cuts

    def copy(when, cut, part):
        slot = lax.rem(when, depth_of_slots)
        at = pl.ds(cut * size, size)
        return pltpu.make_async_copy(
            slots.at[slot, part, at], out_ref.at[part, when, at], sems.at[slot, cut, part]
        )

    def wait_for(when):
        for cut in range(cuts):
            for part in range(2):
                copy(when, cut, part).wait()

    @pl.when(step == 0)
    def _():
        me = lax.axis_index("chan")
        which = pl.program_id(0)
        own = jnp.concatenate([ref[which].astype(jnp.float32) for ref in own_refs])
        other = jnp.concatenate([ref[which].astype(jnp.float32) for ref in other_refs])
        rows = own.shape[0]
        block0 = jnp.where(me == 0, own, other)
        block1 = jnp.where(me == 0, other, own)
        row = lax.broadcasted_iota(jnp.int32, (rows, 1), 0)
        first_part = (row // bins) % 2 == 0
        low = lax.broadcasted_iota(jnp.int32, (rows, LANES), 1) < half

        def tiles_of(block, w):
            tiles = [
                block[:, (2 * j + w) * LANES : (2 * j + w + 1) * LANES] for j in range(full)
            ]
            last = block[:, 2 * full * LANES :]
            turned = swap_halves(last)
            both = jnp.where(low, last, turned) if w == 0 else jnp.where(low, turned, last)
            return tiles, both

        for w in range(2):
            at = pl.ds(w * rows, rows)
            tiles, last0 = tiles_of(block0, w)
            tiles1, last1 = tiles_of(block1, w)
            turned = [swap_halves(tile) for tile in tiles1]
            chain = [last0] + turned + [last1]
            tiles = tiles + [
                jnp.where(low, chain[j], chain[j + 1]) for j in range(len(chain) - 1)
            ]
            for j, tile in enumerate(tiles):
                rotated = jnp.where(
                    first_part,
                    -pltpu.roll(tile, rows - bins, axis=0),
                    pltpu.roll(tile, bins, axis=0),
                )
                right[at, j * LANES : (j + 1) * LANES] = tile.astype(jnp.bfloat16)
                right[at, 2 * channels + j * LANES : 2 * channels + (j + 1) * LANES] = (
                    rotated.astype(jnp.bfloat16)
                )
        scaled = own * scale
        for j in range(full):
            for w in range(2):
                lanes = (2 * j + w) * LANES
                left[j * LANES : (j + 1) * LANES, w * rows : (w + 1) * rows] = scaled[
                    :, lanes : lanes + LANES
                ].T
        last = scaled[:, 2 * full * LANES :].T
        for w in range(2):
            left[full * LANES :, w * rows : (w + 1) * rows] = last[w * half : (w + 1) * half]

    depth = left.shape[1]
    lane = lax.broadcasted_iota(jnp.int32, (1, depth), 1)
    chosen = jnp.where((lane & (bins - 1)) == step, left[...], 0.0).astype(jnp.bfloat16)
    @pl.when(now >= depth_of_slots)
    def _():
        wait_for(now - depth_of_slots)

    slot = lax.rem(now, depth_of_slots)

    def store(tile, first, product):
        for lane in range(tile * TILE, (tile + 1) * TILE, LANES):
            part, at = lane // (2 * channels), lane % (2 * channels)
            piece = product[:, lane - tile * TILE : lane - tile * TILE + LANES]
            slots[slot, part, first : first + BLOCK, at : at + LANES] = piece.astype(jnp.bfloat16)

    def multiply(*accumulators):
        units = [accumulators[:AHEAD], accumulators[AHEAD:]]
        blocks = channels // BLOCK
        tiles = 4 * channels // TILE
        middle = tiles // 2
        work = [[], []]
        for tile in range(tiles):
            split = tile == middle
            for block in range(blocks):
                if split:
                    unit = 0 if block < blocks // 2 else 1
                else:
                    unit = (tile if tile < middle else tile + 1) % 2
                work[unit].append((tile, block))
        pushed, issued = [0, 0], [0, 0]
        waiting = [[], []]
        left_to_store = [blocks * (2 * channels // LANES)] * 2

        def push(unit):
            order = list(dict.fromkeys(tile for tile, _ in work[unit]))
            if pushed[unit] < len(order):
                tile = order[pushed[unit]]
                pltpu.matmul_push_rhs(
                    right[:, tile * TILE : (tile + 1) * TILE], pushed[unit] % 2, unit
                )
                pushed[unit] += 1

        def pop(unit):
            tile, block, acc = waiting[unit].pop(0)
            store(tile, block * BLOCK, pltpu.matmul_pop(acc))
            for lane in range(tile * TILE, (tile + 1) * TILE, LANES):
                part = lane // (2 * channels)
                left_to_store[part] -= 1
                if left_to_store[part] == 0:
                    for cut in range(cuts):
                        copy(now, cut, part).start()

        for unit in range(2):
            push(unit)
        seen = [[], []]
        for index in range(max(len(items) for items in work)):
            for unit in range(2):
                if index >= len(work[unit]):
                    continue
                tile, block = work[unit][index]
                if len(waiting[unit]) == AHEAD:
                    pop(unit)
                acc = units[unit][index % AHEAD]
                fresh = tile not in seen[unit]
                staged = len(seen[unit]) % 2 if fresh else None
                pltpu.matmul_acc_lhs(acc, chosen[block * BLOCK : (block + 1) * BLOCK], staged)
                if fresh:
                    seen[unit].append(tile)
                    push(unit)
                waiting[unit].append((tile, block, acc))
        while waiting[0] or waiting[1]:
            for unit in range(2):
                if waiting[unit]:
                    pop(unit)

    pl.run_scoped(
        multiply,
        *[
            pltpu.ACC(unit)((BLOCK, TILE), jnp.float32)
            for unit in range(2)
            for _ in range(AHEAD)
        ],
    )

    @pl.when(now == steps - 1)
    def _():
        for back in reversed(range(depth_of_slots)):
            wait_for(now - back)


def copy_kernel(in_ref, out_ref):
    out_ref[...] = in_ref[...]


def exchange(value, mask):
    pairs = [(source, source ^ mask) for source in range(lax.axis_size("freq"))]
    return lax.ppermute(value, "freq", pairs)


def swap(value):
    return lax.ppermute(value, "chan", [(0, 1), (1, 0)])


def local(samples):
    local_channels, local_windows, length = samples.shape
    devices = lax.axis_size("freq")
    local_bins = BINS // devices
    windows = local_windows * devices
    bins = min(local_bins, 128 // (2 * devices))
    groups = local_bins // bins
    aligned = bins % 8 == 0
    group = bins if aligned else BINS
    table = jnp.asarray(bin_table(length, BINS, group))
    lanes = local_windows * local_channels
    vmem = pl.BlockSpec(memory_space=pltpu.VMEM)

    memory = pl.BlockSpec(memory_space=pl.ANY)
    with jax.named_scope("table"):
        table = pl.pallas_call(
            copy_kernel,
            out_shape=jax.ShapeDtypeStruct(table.shape, table.dtype),
            in_specs=[vmem],
            out_specs=vmem,
            compiler_params=pltpu.CompilerParams(vmem_limit_bytes=8 * MIB),
        )(table)
    spectrum = jnp.einsum("cws,sj->wcj", samples, table, preferred_element_type=jnp.float32)
    spectrum = spectrum.astype(jnp.bfloat16)
    masks = [*range(devices - 1, devices // 2 - 1, -1), *range(1, devices // 2), 0]
    masks = masks if aligned else [0]
    pieces = len(masks)
    rows = (devices, groups, 2 * bins, lanes) if aligned else (2 * BINS, lanes)
    piece = rows[1:] if aligned else rows
    with jax.named_scope("whiten"):
        whitened = pl.pallas_call(
            functools.partial(whiten_kernel, group, masks),
            out_shape=[jax.ShapeDtypeStruct(piece, jnp.bfloat16)] * pieces,
            in_specs=[vmem],
            out_specs=[vmem] * pieces,
            scratch_shapes=[pltpu.VMEM(rows, jnp.bfloat16)],
            compiler_params=pltpu.CompilerParams(vmem_limit_bytes=16 * MIB),
            cost_estimate=pl.CostEstimate(
                flops=40 * BINS * lanes, bytes_accessed=12 * BINS * lanes, transcendentals=BINS * lanes
            ),
        )(spectrum)
    if aligned:
        pieces_of = dict(zip(masks, whitened))
        own, other = {0: pieces_of[0]}, {}
        for mask in masks[: devices // 2]:
            own[mask] = exchange(pieces_of[mask], mask)
        latest = other[0] = swap(own[0])
        for mask in masks[devices // 2 : -1]:
            value, latest = lax.optimization_barrier((pieces_of[mask], latest))
            own[mask] = exchange(value, mask)
            latest = other[mask] = swap(own[mask])
        for mask in masks[: devices // 2]:
            other[mask] = swap(own[mask])
        own, other = [own[mask] for mask in masks], [other[mask] for mask in masks]
    else:
        rows = whitened[0].reshape(2, devices, groups, bins, lanes).transpose(1, 2, 0, 3, 4)
        rows = rows.reshape(devices, groups, 2 * bins, lanes)
        rows = lax.all_to_all(rows, "freq", split_axis=0, concat_axis=0, tiled=True)
        own = [rows.transpose(1, 0, 2, 3).reshape(groups, devices * 2 * bins, lanes)]
        other = [swap(own[0])]
    depth = local_windows * devices * 2 * bins
    with jax.named_scope("outer_products"):
        out = pl.pallas_call(
            functools.partial(outer_kernel, bins, 1.0 / windows),
            out_shape=jax.ShapeDtypeStruct(
                (2, local_bins, local_channels, 2 * local_channels), jnp.bfloat16
            ),
            grid=(groups, bins),
            in_specs=[vmem] * (2 * pieces),
            out_specs=memory,
            scratch_shapes=[
                pltpu.VMEM((depth, 4 * local_channels), jnp.bfloat16),
                pltpu.VMEM((local_channels, depth), jnp.float32),
                pltpu.VMEM((3, 2, local_channels, 2 * local_channels), jnp.bfloat16),
                pltpu.SemaphoreType.DMA((3, 2, 2)),
            ],
            compiler_params=pltpu.CompilerParams(vmem_limit_bytes=32 * MIB),
            cost_estimate=pl.CostEstimate(
                flops=8 * local_bins * depth * local_channels * local_channels,
                bytes_accessed=8 * local_bins * local_channels * local_channels,
                transcendentals=0,
            ),
        )(*own, *other)
    return jnp.transpose(out, (0, 1, 3, 2))


def solution(mesh):
    placed = (P("chan", ("hours", "freq"), None),)
    return jax.shard_map(
        local,
        mesh=mesh,
        in_specs=placed,
        out_specs=P(None, ("hours", "freq"), None, "chan"),
        check_vma=False,
    )
```

```python
import functools
import math

import jax
import jax.numpy as jnp
import ml_dtypes
import numpy as np
from jax import lax
from jax.experimental import pallas as pl
from jax.experimental.pallas import tpu as pltpu
from jax.sharding import PartitionSpec as P

BINS = 128
LANES = 128
MIB = 1024 * 1024


def bin_table(length, bins, group):
    position = np.arange(length)[None, :]
    number = np.arange(1, bins + 1)[:, None]
    phase = (position * number % length).astype(np.float32) * np.float32(2.0 * math.pi / length)
    taper = np.float32(0.5) - np.float32(0.5) * np.cos(
        position.astype(np.float32) * np.float32(2.0 * math.pi / length)
    )
    factor = np.float32(math.sqrt(8.0 / (3.0 * length)))
    table = np.stack([taper * np.cos(phase), -(taper * np.sin(phase))]) * factor
    table = table.reshape(2, bins // group, group, length).transpose(3, 1, 0, 2)
    return table.reshape(length, 2 * bins).astype(ml_dtypes.bfloat16)


def channel_blocks(channels):
    return [
        (first, min(LANES, channels - first), 2 * first) for first in range(0, channels, LANES)
    ]


def whiten_kernel(group, near, spectrum_ref, *refs):
    pieces, rows_ref = refs[:-1], refs[-1]
    windows, channels, columns = spectrum_ref.shape
    bins = columns // 2
    row = lax.broadcasted_iota(jnp.int32, (bins, 1), 0)
    count = jnp.minimum(row + 2, bins - 1) - jnp.maximum(row - 2, 0) + 1
    share = 1.0 / count.astype(jnp.float32)

    for first, width, lane in channel_blocks(channels):
        blocks = [
            spectrum_ref[w, first : first + width, :].astype(jnp.float32).T
            for w in range(windows)
        ]
        spectrum = jnp.concatenate(blocks, axis=1)
        cols = windows * width
        parts = spectrum.reshape(bins // group, 2, group, cols)
        power = (parts[:, 0] * parts[:, 0] + parts[:, 1] * parts[:, 1]).reshape(bins, cols)
        summed = power
        for step in (1, 2):
            summed = summed + jnp.where(row >= step, pltpu.roll(power, step, axis=0), 0.0)
            summed = summed + jnp.where(
                row < bins - step, pltpu.roll(power, bins - step, axis=0), 0.0
            )
        level = jnp.maximum(summed * share, 0.1)
        inverse = lax.rsqrt(level).reshape(bins // group, 1, group, cols)
        whitened = (parts * inverse).astype(jnp.bfloat16)
        rows_ref[..., lane : lane + cols] = whitened.reshape(rows_ref.shape[:-1] + (cols,))

    if near is None:
        pieces[0][...] = rows_ref[...]
    else:
        me = lax.axis_index("freq")
        first = (me // near) * near
        for i in range(near):
            pieces[0][i] = rows_ref[first + i]
        for mask, piece in enumerate(pieces[1:], near):
            piece[...] = rows_ref[me ^ mask]


def swap_halves(tile):
    return pltpu.roll(tile, LANES // 2, axis=1)


def rows_of(refs, which):
    for ref in refs:
        if len(ref.shape) == 3:
            yield ref[which]
        else:
            for i in range(ref.shape[0]):
                yield ref[i, which]


def outer_kernel(bins, scale, *refs):
    out_ref, right, left, slots, sems = refs[-5:]
    count = (len(refs) - 5) // 2
    own_refs, other_refs = refs[:count], refs[count:-5]
    half = LANES // 2
    channels = out_ref.shape[2]
    full = channels // LANES
    step = pl.program_id(1)
    now = pl.program_id(0) * bins + step
    steps = pl.num_programs(0) * bins
    depth_of_slots, cuts = sems.shape[:2]
    size = channels // cuts

    def copy(when, cut, part):
        slot = lax.rem(when, depth_of_slots)
        at = pl.ds(cut * size, size)
        return pltpu.make_async_copy(
            slots.at[slot, part, at], out_ref.at[part, when, at], sems.at[slot, cut, part]
        )

    def wait_for(when):
        for cut in range(cuts):
            for part in range(2):
                copy(when, cut, part).wait()

    @pl.when(step == 0)
    def _():
        me = lax.axis_index("chan")
        which = pl.program_id(0)
        own = jnp.concatenate([rows.astype(jnp.float32) for rows in rows_of(own_refs, which)])
        other = jnp.concatenate([rows.astype(jnp.float32) for rows in rows_of(other_refs, which)])
        rows = own.shape[0]
        block0 = jnp.where(me == 0, own, other)
        block1 = jnp.where(me == 0, other, own)
        row = lax.broadcasted_iota(jnp.int32, (rows, 1), 0)
        first_part = (row // bins) % 2 == 0
        low = lax.broadcasted_iota(jnp.int32, (rows, LANES), 1) < half

        def tiles_of(block, w):
            tiles = [
                block[:, (2 * j + w) * LANES : (2 * j + w + 1) * LANES] for j in range(full)
            ]
            last = block[:, 2 * full * LANES :]
            turned = swap_halves(last)
            both = jnp.where(low, last, turned) if w == 0 else jnp.where(low, turned, last)
            return tiles, both

        for w in range(2):
            at = pl.ds(w * rows, rows)
            tiles, last0 = tiles_of(block0, w)
            tiles1, last1 = tiles_of(block1, w)
            turned = [swap_halves(tile) for tile in tiles1]
            chain = [last0] + turned + [last1]
            tiles = tiles + [
                jnp.where(low, chain[j], chain[j + 1]) for j in range(len(chain) - 1)
            ]
            for j, tile in enumerate(tiles):
                rotated = jnp.where(
                    first_part,
                    -pltpu.roll(tile, rows - bins, axis=0),
                    pltpu.roll(tile, bins, axis=0),
                )
                right[at, j * LANES : (j + 1) * LANES] = tile.astype(jnp.bfloat16)
                right[at, 2 * channels + j * LANES : 2 * channels + (j + 1) * LANES] = (
                    rotated.astype(jnp.bfloat16)
                )
        scaled = own * scale
        for j in range(full):
            for w in range(2):
                lanes = (2 * j + w) * LANES
                left[j * LANES : (j + 1) * LANES, w * rows : (w + 1) * rows] = scaled[
                    :, lanes : lanes + LANES
                ].T
        last = scaled[:, 2 * full * LANES :].T
        for w in range(2):
            left[full * LANES :, w * rows : (w + 1) * rows] = last[w * half : (w + 1) * half]

    depth = left.shape[1]
    lane = lax.broadcasted_iota(jnp.int32, (1, depth), 1)
    chosen = jnp.where((lane & (bins - 1)) == step, left[...], 0.0).astype(jnp.bfloat16)
    @pl.when(now >= depth_of_slots)
    def _():
        wait_for(now - depth_of_slots)

    slot = lax.rem(now, depth_of_slots)

    whole = 2 * channels // (2 * LANES) * (2 * LANES)
    starts = [0, whole, 4 * channels - whole, 4 * channels]
    left_over = 2 * channels - whole

    def multiply(first, last):
        return jnp.dot(
            chosen, right[:, first:last], preferred_element_type=jnp.float32
        ).astype(jnp.bfloat16)

    def send(part):
        for cut in range(cuts):
            copy(now, cut, part).start()

    slots[slot, 0, :, :whole] = multiply(*starts[:2])
    if left_over:
        both = multiply(*starts[1:3])
        slots[slot, 0, :, whole:] = both[:, :left_over]
        slots[slot, 1, :, :left_over] = both[:, left_over:]
    send(0)
    slots[slot, 1, :, left_over:] = multiply(*starts[2:])
    send(1)

    @pl.when(now == steps - 1)
    def _():
        for back in reversed(range(depth_of_slots)):
            wait_for(now - back)


def copy_kernel(in_ref, out_ref):
    out_ref[...] = in_ref[...]


def exchange(value, mask):
    pairs = [(source, source ^ mask) for source in range(lax.axis_size("freq"))]
    return lax.ppermute(value, "freq", pairs)


def swap(value):
    return lax.ppermute(value, "chan", [(0, 1), (1, 0)])


def local(samples):
    local_channels, local_windows, length = samples.shape
    devices = lax.axis_size("freq")
    local_bins = BINS // devices
    windows = local_windows * devices
    bins = min(local_bins, 128 // (2 * devices))
    groups = local_bins // bins
    aligned = bins % 8 == 0
    group = bins if aligned else BINS
    table = jnp.asarray(bin_table(length, BINS, group))
    lanes = local_windows * local_channels
    vmem = pl.BlockSpec(memory_space=pltpu.VMEM)
    memory = pl.BlockSpec(memory_space=pl.ANY)
    near = devices // 2 if aligned else None
    pieces = devices - near + 1 if aligned else 1
    rows = (devices, groups, 2 * bins, lanes) if aligned else (2 * BINS, lanes)
    shapes = [(near,) + rows[1:]] + [rows[1:]] * (pieces - 1) if aligned else [rows]
    with jax.named_scope("table"):
        table = pl.pallas_call(
            copy_kernel,
            out_shape=jax.ShapeDtypeStruct(table.shape, table.dtype),
            in_specs=[vmem],
            out_specs=vmem,
            compiler_params=pltpu.CompilerParams(vmem_limit_bytes=8 * MIB),
        )(table)
    spectrum = jnp.einsum("cws,sj->wcj", samples, table, preferred_element_type=jnp.float32)
    spectrum = spectrum.astype(jnp.bfloat16)
    with jax.named_scope("whiten"):
        whitened = pl.pallas_call(
            functools.partial(whiten_kernel, group, near),
            out_shape=[jax.ShapeDtypeStruct(shape, jnp.bfloat16) for shape in shapes],
            in_specs=[vmem],
            out_specs=[vmem] * pieces,
            scratch_shapes=[pltpu.VMEM(rows, jnp.bfloat16)],
            compiler_params=pltpu.CompilerParams(vmem_limit_bytes=16 * MIB),
            cost_estimate=pl.CostEstimate(
                flops=40 * BINS * lanes, bytes_accessed=12 * BINS * lanes, transcendentals=BINS * lanes
            ),
        )(spectrum)
    if aligned:
        far = [exchange(value, mask) for mask, value in enumerate(whitened[1:], near)]
        grouped = [list(range(first, first + near)) for first in range(0, devices, near)]
        own = lax.all_to_all(
            whitened[0], "freq", split_axis=0, concat_axis=0, tiled=True, axis_index_groups=grouped
        )
        own = [own] + far
    else:
        rows = whitened[0].reshape(2, devices, groups, bins, lanes).transpose(1, 2, 0, 3, 4)
        rows = rows.reshape(devices, groups, 2 * bins, lanes)
        rows = lax.all_to_all(rows, "freq", split_axis=0, concat_axis=0, tiled=True)
        own = [rows.transpose(1, 0, 2, 3).reshape(groups, devices * 2 * bins, lanes)]
    other = [swap(value) for value in own]
    depth = local_windows * devices * 2 * bins
    with jax.named_scope("outer_products"):
        out = pl.pallas_call(
            functools.partial(outer_kernel, bins, 1.0 / windows),
            out_shape=jax.ShapeDtypeStruct(
                (2, local_bins, local_channels, 2 * local_channels), jnp.bfloat16
            ),
            grid=(groups, bins),
            in_specs=[vmem] * (2 * pieces),
            out_specs=memory,
            scratch_shapes=[
                pltpu.VMEM((depth, 4 * local_channels), jnp.bfloat16),
                pltpu.VMEM((local_channels, depth), jnp.float32),
                pltpu.VMEM((3, 2, local_channels, 2 * local_channels), jnp.bfloat16),
                pltpu.SemaphoreType.DMA((3, 2, 2)),
            ],
            compiler_params=pltpu.CompilerParams(vmem_limit_bytes=32 * MIB),
            cost_estimate=pl.CostEstimate(
                flops=8 * local_bins * depth * local_channels * local_channels,
                bytes_accessed=8 * local_bins * local_channels * local_channels,
                transcendentals=0,
            ),
        )(*own, *other)
    return jnp.transpose(out, (0, 1, 3, 2))


def solution(mesh):
    placed = (P("chan", ("hours", "freq"), None),)
    return jax.shard_map(
        local,
        mesh=mesh,
        in_specs=placed,
        out_specs=P(None, ("hours", "freq"), None, "chan"),
        check_vma=False,
    )
```

```python
import functools
import math

import jax
import jax.numpy as jnp
import ml_dtypes
import numpy as np
from jax import lax
from jax.experimental import pallas as pl
from jax.experimental.pallas import tpu as pltpu
from jax.sharding import PartitionSpec as P

BINS = 128
LANES = 128
CUTS = 6
MIB = 1024 * 1024


def bin_table(length, bins, group):
    position = np.arange(length)[None, :]
    number = np.arange(1, bins + 1)[:, None]
    phase = (position * number % length).astype(np.float32) * np.float32(2.0 * math.pi / length)
    taper = np.float32(0.5) - np.float32(0.5) * np.cos(
        position.astype(np.float32) * np.float32(2.0 * math.pi / length)
    )
    factor = np.float32(math.sqrt(8.0 / (3.0 * length)))
    table = np.stack([taper * np.cos(phase), -(taper * np.sin(phase))]) * factor
    table = table.reshape(2, bins // group, group, length).transpose(3, 1, 0, 2)
    return table.reshape(length, 2 * bins).astype(ml_dtypes.bfloat16)


def channel_blocks(channels):
    return [
        (first, min(LANES, channels - first), 2 * first) for first in range(0, channels, LANES)
    ]


def whiten_kernel(group, near, spectrum_ref, *refs):
    pieces, rows_ref = refs[:-1], refs[-1]
    windows, channels, columns = spectrum_ref.shape
    bins = columns // 2
    row = lax.broadcasted_iota(jnp.int32, (bins, 1), 0)
    count = jnp.minimum(row + 2, bins - 1) - jnp.maximum(row - 2, 0) + 1
    share = 1.0 / count.astype(jnp.float32)

    for first, width, lane in channel_blocks(channels):
        blocks = [
            spectrum_ref[w, first : first + width, :].astype(jnp.float32).T
            for w in range(windows)
        ]
        spectrum = jnp.concatenate(blocks, axis=1)
        cols = windows * width
        parts = spectrum.reshape(bins // group, 2, group, cols)
        power = (parts[:, 0] * parts[:, 0] + parts[:, 1] * parts[:, 1]).reshape(bins, cols)
        summed = power
        for step in (1, 2):
            summed = summed + jnp.where(row >= step, pltpu.roll(power, step, axis=0), 0.0)
            summed = summed + jnp.where(
                row < bins - step, pltpu.roll(power, bins - step, axis=0), 0.0
            )
        level = jnp.maximum(summed * share, 0.1)
        inverse = lax.rsqrt(level).reshape(bins // group, 1, group, cols)
        whitened = (parts * inverse).astype(jnp.bfloat16)
        rows_ref[..., lane : lane + cols] = whitened.reshape(rows_ref.shape[:-1] + (cols,))

    if near is None:
        pieces[0][...] = rows_ref[...]
    else:
        me = lax.axis_index("freq")
        for mask in range(near):
            pieces[mask][...] = rows_ref[me ^ mask]
        for i, piece in enumerate(pieces[near:]):
            mask, which = near + i % near, i // near
            piece[0] = rows_ref[me ^ mask, which]


def swap_halves(tile):
    return pltpu.roll(tile, LANES // 2, axis=1)


def rows_of(refs, which, kinds):
    for ref, kind in zip(refs, kinds):
        if kind == "groups":
            yield ref[which]
        elif kind == "pair":
            near = lax.axis_size("freq") // 2
            yield ref[1 - lax.axis_index("freq") // near]
        else:
            yield ref[0]


def outer_kernel(bins, scale, which, kinds, *refs):
    out_ref, right, left, slots, sems = refs[-5:]
    count = len(kinds)
    own_refs, other_refs = refs[:count], refs[count : 2 * count]
    half = LANES // 2
    channels = out_ref.shape[2]
    full = channels // LANES
    step = now = pl.program_id(0)
    steps = bins
    depth_of_slots, cuts = sems.shape[:2]
    size = channels // cuts

    def copy(when, cut, part):
        slot = lax.rem(when, depth_of_slots)
        at = pl.ds(cut * size, size)
        return pltpu.make_async_copy(
            slots.at[slot, part, at], out_ref.at[part, which * bins + when, at], sems.at[slot, cut, part]
        )

    def wait_for(when):
        for cut in range(cuts):
            for part in range(2):
                copy(when, cut, part).wait()

    @pl.when(step == 0)
    def _():
        me = lax.axis_index("chan")
        own, other = (
            jnp.concatenate([rows.astype(jnp.float32) for rows in rows_of(some, which, kinds)])
            for some in (own_refs, other_refs)
        )
        rows = own.shape[0]
        block0 = jnp.where(me == 0, own, other)
        block1 = jnp.where(me == 0, other, own)
        row = lax.broadcasted_iota(jnp.int32, (rows, 1), 0)
        first_part = (row // bins) % 2 == 0
        low = lax.broadcasted_iota(jnp.int32, (rows, LANES), 1) < half

        def tiles_of(block, w):
            tiles = [
                block[:, (2 * j + w) * LANES : (2 * j + w + 1) * LANES] for j in range(full)
            ]
            last = block[:, 2 * full * LANES :]
            turned = swap_halves(last)
            both = jnp.where(low, last, turned) if w == 0 else jnp.where(low, turned, last)
            return tiles, both

        for w in range(2):
            at = pl.ds(w * rows, rows)
            tiles, last0 = tiles_of(block0, w)
            tiles1, last1 = tiles_of(block1, w)
            turned = [swap_halves(tile) for tile in tiles1]
            chain = [last0] + turned + [last1]
            tiles = tiles + [
                jnp.where(low, chain[j], chain[j + 1]) for j in range(len(chain) - 1)
            ]
            for j, tile in enumerate(tiles):
                rotated = jnp.where(
                    first_part,
                    -pltpu.roll(tile, rows - bins, axis=0),
                    pltpu.roll(tile, bins, axis=0),
                )
                right[at, j * LANES : (j + 1) * LANES] = tile.astype(jnp.bfloat16)
                right[at, 2 * channels + j * LANES : 2 * channels + (j + 1) * LANES] = (
                    rotated.astype(jnp.bfloat16)
                )
        scaled = own * scale
        for j in range(full):
            for w in range(2):
                lanes = (2 * j + w) * LANES
                left[j * LANES : (j + 1) * LANES, w * rows : (w + 1) * rows] = scaled[
                    :, lanes : lanes + LANES
                ].T
        last = scaled[:, 2 * full * LANES :].T
        for w in range(2):
            left[full * LANES :, w * rows : (w + 1) * rows] = last[w * half : (w + 1) * half]

    depth = left.shape[1]
    lane = lax.broadcasted_iota(jnp.int32, (1, depth), 1)
    chosen = jnp.where((lane & (bins - 1)) == step, left[...], 0.0).astype(jnp.bfloat16)
    @pl.when(now >= depth_of_slots)
    def _():
        wait_for(now - depth_of_slots)

    slot = lax.rem(now, depth_of_slots)

    whole = 2 * channels // (2 * LANES) * (2 * LANES)
    starts = [0, whole, 4 * channels - whole, 4 * channels]
    left_over = 2 * channels - whole

    def multiply(first, last):
        return jnp.dot(
            chosen, right[:, first:last], preferred_element_type=jnp.float32
        ).astype(jnp.bfloat16)

    def send(part):
        for cut in range(cuts):
            copy(now, cut, part).start()

    slots[slot, 0, :, :whole] = multiply(*starts[:2])
    if left_over:
        both = multiply(*starts[1:3])
        slots[slot, 0, :, whole:] = both[:, :left_over]
        slots[slot, 1, :, :left_over] = both[:, left_over:]
    send(0)
    slots[slot, 1, :, left_over:] = multiply(*starts[2:])
    send(1)

    @pl.when(now == steps - 1)
    def _():
        for back in reversed(range(depth_of_slots)):
            wait_for(now - back)


def copy_kernel(in_ref, out_ref):
    out_ref[...] = in_ref[...]


def exchange(value, mask):
    pairs = [(source, source ^ mask) for source in range(lax.axis_size("freq"))]
    return lax.ppermute(value, "freq", pairs)


def gather_pair(value, mask):
    pairs = sorted({(min(i, i ^ mask), max(i, i ^ mask)) for i in range(lax.axis_size("freq"))})
    return lax.all_gather(
        value, "freq", axis_index_groups=[list(pair) for pair in pairs], tiled=True
    )


def swap(value):
    return lax.ppermute(value, "chan", [(0, 1), (1, 0)])


def local(samples):
    local_channels, local_windows, length = samples.shape
    devices = lax.axis_size("freq")
    local_bins = BINS // devices
    windows = local_windows * devices
    bins = min(local_bins, 128 // (2 * devices))
    groups = local_bins // bins
    aligned = bins % 8 == 0
    group = bins if aligned else BINS
    table = jnp.asarray(bin_table(length, BINS, group))
    lanes = local_windows * local_channels
    vmem = pl.BlockSpec(memory_space=pltpu.VMEM)
    memory = pl.BlockSpec(memory_space=pl.ANY)
    near = devices // 2 if aligned else None
    if aligned:
        rows = (devices, groups, 2 * bins, lanes)
        shapes = [rows[1:]] * near + [(1,) + rows[2:]] * (groups * near)
    else:
        rows = (2 * BINS, lanes)
        shapes = [rows]
    with jax.named_scope("table"):
        table = pl.pallas_call(
            copy_kernel,
            out_shape=jax.ShapeDtypeStruct(table.shape, table.dtype),
            in_specs=[vmem],
            out_specs=vmem,
            compiler_params=pltpu.CompilerParams(vmem_limit_bytes=8 * MIB),
        )(table)
    spectrum = jnp.einsum("cws,sj->wcj", samples, table, preferred_element_type=jnp.float32)
    spectrum = spectrum.astype(jnp.bfloat16)
    with jax.named_scope("whiten"):
        whitened = pl.pallas_call(
            functools.partial(whiten_kernel, group, near),
            out_shape=[jax.ShapeDtypeStruct(shape, jnp.bfloat16) for shape in shapes],
            in_specs=[vmem],
            out_specs=[vmem] * len(shapes),
            scratch_shapes=[pltpu.VMEM(rows, jnp.bfloat16)],
            compiler_params=pltpu.CompilerParams(vmem_limit_bytes=16 * MIB),
            cost_estimate=pl.CostEstimate(
                flops=40 * BINS * lanes, bytes_accessed=12 * BINS * lanes, transcendentals=BINS * lanes
            ),
        )(spectrum)
    if aligned:
        own = {mask: whitened[mask] for mask in range(near)}
        far = [whitened[near * (1 + g) : near * (2 + g)] for g in range(groups)]
        first = {}
        for mask in (1, 2, *range(devices - 1, near - 1, -1), *range(3, near)):
            if mask < near:
                own[mask] = exchange(own[mask], mask)
            else:
                first[mask] = exchange(far[0][mask - near], mask)
        sources = [[*own.values(), *first.values()]]
        kinds = [["groups"] * near + ["whole"] * near]
        for g in range(1, groups):
            later, held = lax.optimization_barrier((far[g], sources[-1][-2:]))
            sources[-1][-2:] = held
            gathered = [gather_pair(value, near + i) for i, value in enumerate(later)]
            sources.append([*own.values(), *gathered])
            kinds.append(["groups"] * near + ["pair"] * near)
        near_other = [swap(value) for value in own.values()]
    else:
        rows = whitened[0].reshape(2, devices, groups, bins, lanes).transpose(1, 2, 0, 3, 4)
        rows = rows.reshape(devices, groups, 2 * bins, lanes)
        rows = lax.all_to_all(rows, "freq", split_axis=0, concat_axis=0, tiled=True)
        own = rows.transpose(1, 0, 2, 3).reshape(groups, devices * 2 * bins, lanes)
        near, near_other = 1, [swap(own)]
        sources, kinds = [[own]] * groups, [["groups"]] * groups
    depth = local_windows * devices * 2 * bins
    out = None
    for g in range(groups):
        later = sources[g][near:]
        if out is not None and later:
            later, out = lax.optimization_barrier((later, out))
        operands = [*sources[g][:near], *later, *near_other, *map(swap, later)]
        specs = [vmem] * len(operands)
        aliases = {}
        if out is not None:
            aliases = {len(operands): 0}
            operands, specs = [*operands, out], [*specs, memory]
        with jax.named_scope("outer_products"):
            out = pl.pallas_call(
                functools.partial(outer_kernel, bins, 1.0 / windows, g, kinds[g]),
                out_shape=jax.ShapeDtypeStruct(
                    (2, local_bins, local_channels, 2 * local_channels), jnp.bfloat16
                ),
                grid=(bins,),
                in_specs=specs,
                out_specs=memory,
                input_output_aliases=aliases,
                scratch_shapes=[
                    pltpu.VMEM((depth, 4 * local_channels), jnp.bfloat16),
                    pltpu.VMEM((local_channels, depth), jnp.float32),
                    pltpu.VMEM((3, 2, local_channels, 2 * local_channels), jnp.bfloat16),
                    pltpu.SemaphoreType.DMA((3, CUTS, 2)),
                ],
                compiler_params=pltpu.CompilerParams(vmem_limit_bytes=32 * MIB),
                cost_estimate=pl.CostEstimate(
                    flops=8 * bins * depth * local_channels * local_channels,
                    bytes_accessed=8 * bins * local_channels * local_channels,
                    transcendentals=0,
                ),
            )(*operands)
    return jnp.transpose(out, (0, 1, 3, 2))


def solution(mesh):
    placed = (P("chan", ("hours", "freq"), None),)
    return jax.shard_map(
        local,
        mesh=mesh,
        in_specs=placed,
        out_specs=P(None, ("hours", "freq"), None, "chan"),
        check_vma=False,
    )
```

```python
import functools
import math

import jax
import jax.numpy as jnp
import ml_dtypes
import numpy as np
from jax import lax
from jax.experimental import pallas as pl
from jax.experimental.pallas import tpu as pltpu
from jax.sharding import PartitionSpec as P

BINS = 128
LANES = 128
CUTS = 2
MIB = 1024 * 1024


def bin_table(length, bins, group):
    position = np.arange(length)[None, :]
    number = np.arange(1, bins + 1)[:, None]
    phase = (position * number % length).astype(np.float32) * np.float32(2.0 * math.pi / length)
    taper = np.float32(0.5) - np.float32(0.5) * np.cos(
        position.astype(np.float32) * np.float32(2.0 * math.pi / length)
    )
    factor = np.float32(math.sqrt(8.0 / (3.0 * length)))
    table = np.stack([taper * np.cos(phase), -(taper * np.sin(phase))]) * factor
    table = table.reshape(2, bins // group, group, length).transpose(3, 1, 0, 2)
    return table.reshape(length, 2 * bins).astype(ml_dtypes.bfloat16)


def channel_blocks(channels):
    return [
        (first, min(LANES, channels - first), 2 * first) for first in range(0, channels, LANES)
    ]


def whiten_kernel(group, spectrum_ref, *refs):
    pieces, rows_ref = refs[:-1], refs[-1]
    windows, channels, columns = spectrum_ref.shape
    bins = columns // 2
    row = lax.broadcasted_iota(jnp.int32, (bins, 1), 0)
    count = jnp.minimum(row + 2, bins - 1) - jnp.maximum(row - 2, 0) + 1
    share = 1.0 / count.astype(jnp.float32)

    for first, width, lane in channel_blocks(channels):
        blocks = [
            spectrum_ref[w, first : first + width, :].astype(jnp.float32).T
            for w in range(windows)
        ]
        spectrum = jnp.concatenate(blocks, axis=1)
        cols = windows * width
        parts = spectrum.reshape(bins // group, 2, group, cols)
        power = (parts[:, 0] * parts[:, 0] + parts[:, 1] * parts[:, 1]).reshape(bins, cols)
        summed = power
        for step in (1, 2):
            summed = summed + jnp.where(row >= step, pltpu.roll(power, step, axis=0), 0.0)
            summed = summed + jnp.where(
                row < bins - step, pltpu.roll(power, bins - step, axis=0), 0.0
            )
        level = jnp.maximum(summed * share, 0.1)
        inverse = lax.rsqrt(level).reshape(bins // group, 1, group, cols)
        whitened = (parts * inverse).astype(jnp.bfloat16)
        rows_ref[..., lane : lane + cols] = whitened.reshape(rows_ref.shape[:-1] + (cols,))

    if len(pieces) == 1:
        pieces[0][...] = rows_ref[...]
    else:
        for which, piece in enumerate(pieces):
            piece[...] = rows_ref[:, which]


def swap_halves(tile):
    return pltpu.roll(tile, LANES // 2, axis=1)


def outer_kernel(bins, scale, which, own_ref, other_ref, *refs):
    out_ref, right, left, slots, sems = refs[-5:]
    half = LANES // 2
    channels = out_ref.shape[2]
    full = channels // LANES
    step = now = pl.program_id(0)
    steps = bins
    depth_of_slots, cuts = sems.shape[:2]
    size = channels // cuts

    def copy(when, cut, part):
        slot = lax.rem(when, depth_of_slots)
        at = pl.ds(cut * size, size)
        return pltpu.make_async_copy(
            slots.at[slot, part, at], out_ref.at[part, which * bins + when, at], sems.at[slot, cut, part]
        )

    def wait_for(when):
        for cut in range(cuts):
            for part in range(2):
                copy(when, cut, part).wait()

    @pl.when(step == 0)
    def _():
        me = lax.axis_index("chan")
        rows = own_ref.shape[0] * own_ref.shape[1]
        own, other = (
            ref[...].astype(jnp.float32).reshape(rows, ref.shape[2]) for ref in (own_ref, other_ref)
        )
        block0 = jnp.where(me == 0, own, other)
        block1 = jnp.where(me == 0, other, own)
        row = lax.broadcasted_iota(jnp.int32, (rows, 1), 0)
        first_part = (row // bins) % 2 == 0
        low = lax.broadcasted_iota(jnp.int32, (rows, LANES), 1) < half

        def tiles_of(block, w):
            tiles = [
                block[:, (2 * j + w) * LANES : (2 * j + w + 1) * LANES] for j in range(full)
            ]
            last = block[:, 2 * full * LANES :]
            turned = swap_halves(last)
            both = jnp.where(low, last, turned) if w == 0 else jnp.where(low, turned, last)
            return tiles, both

        for w in range(2):
            at = pl.ds(w * rows, rows)
            tiles, last0 = tiles_of(block0, w)
            tiles1, last1 = tiles_of(block1, w)
            turned = [swap_halves(tile) for tile in tiles1]
            chain = [last0] + turned + [last1]
            tiles = tiles + [
                jnp.where(low, chain[j], chain[j + 1]) for j in range(len(chain) - 1)
            ]
            for j, tile in enumerate(tiles):
                rotated = jnp.where(
                    first_part,
                    -pltpu.roll(tile, rows - bins, axis=0),
                    pltpu.roll(tile, bins, axis=0),
                )
                right[at, j * LANES : (j + 1) * LANES] = tile.astype(jnp.bfloat16)
                right[at, 2 * channels + j * LANES : 2 * channels + (j + 1) * LANES] = (
                    rotated.astype(jnp.bfloat16)
                )
        scaled = own * scale
        for j in range(full):
            for w in range(2):
                lanes = (2 * j + w) * LANES
                left[j * LANES : (j + 1) * LANES, w * rows : (w + 1) * rows] = scaled[
                    :, lanes : lanes + LANES
                ].T
        last = scaled[:, 2 * full * LANES :].T
        for w in range(2):
            left[full * LANES :, w * rows : (w + 1) * rows] = last[w * half : (w + 1) * half]

    depth = left.shape[1]
    lane = lax.broadcasted_iota(jnp.int32, (1, depth), 1)
    chosen = jnp.where((lane & (bins - 1)) == step, left[...], 0.0).astype(jnp.bfloat16)
    @pl.when(now >= depth_of_slots)
    def _():
        wait_for(now - depth_of_slots)

    slot = lax.rem(now, depth_of_slots)

    whole = 2 * channels // (2 * LANES) * (2 * LANES)
    starts = [0, whole, 4 * channels - whole, 4 * channels]
    left_over = 2 * channels - whole

    def multiply(first, last):
        return jnp.dot(
            chosen, right[:, first:last], preferred_element_type=jnp.float32
        ).astype(jnp.bfloat16)

    def send(part):
        for cut in range(cuts):
            copy(now, cut, part).start()

    slots[slot, 0, :, :whole] = multiply(*starts[:2])
    if left_over:
        both = multiply(*starts[1:3])
        slots[slot, 0, :, whole:] = both[:, :left_over]
        slots[slot, 1, :, :left_over] = both[:, left_over:]
    send(0)
    slots[slot, 1, :, left_over:] = multiply(*starts[2:])
    send(1)

    @pl.when(now == steps - 1)
    def _():
        for back in reversed(range(depth_of_slots)):
            wait_for(now - back)


def copy_kernel(in_ref, out_ref):
    out_ref[...] = in_ref[...]


def swap(value):
    return lax.ppermute(value, "chan", [(0, 1), (1, 0)])


def local(samples):
    local_channels, local_windows, length = samples.shape
    devices = lax.axis_size("freq")
    local_bins = BINS // devices
    windows = local_windows * devices
    bins = min(local_bins, 128 // (2 * devices))
    groups = local_bins // bins
    aligned = bins % 8 == 0
    group = bins if aligned else BINS
    table = jnp.asarray(bin_table(length, BINS, group))
    lanes = local_windows * local_channels
    vmem = pl.BlockSpec(memory_space=pltpu.VMEM)
    memory = pl.BlockSpec(memory_space=pl.ANY)
    if aligned:
        rows = (devices, groups, 2 * bins, lanes)
        shapes = [(devices, 2 * bins, lanes)] * groups
    else:
        rows = (2 * BINS, lanes)
        shapes = [rows]
    with jax.named_scope("table"):
        table = pl.pallas_call(
            copy_kernel,
            out_shape=jax.ShapeDtypeStruct(table.shape, table.dtype),
            in_specs=[vmem],
            out_specs=vmem,
            compiler_params=pltpu.CompilerParams(vmem_limit_bytes=8 * MIB),
        )(table)
    spectrum = jnp.einsum("cws,sj->wcj", samples, table, preferred_element_type=jnp.float32)
    spectrum = spectrum.astype(jnp.bfloat16)
    with jax.named_scope("whiten"):
        whitened = pl.pallas_call(
            functools.partial(whiten_kernel, group),
            out_shape=[jax.ShapeDtypeStruct(shape, jnp.bfloat16) for shape in shapes],
            in_specs=[vmem],
            out_specs=[vmem] * len(shapes),
            scratch_shapes=[pltpu.VMEM(rows, jnp.bfloat16)],
            compiler_params=pltpu.CompilerParams(vmem_limit_bytes=16 * MIB),
            cost_estimate=pl.CostEstimate(
                flops=40 * BINS * lanes, bytes_accessed=12 * BINS * lanes, transcendentals=BINS * lanes
            ),
        )(spectrum)
    if not aligned:
        rows = whitened[0].reshape(2, devices, groups, bins, lanes).transpose(2, 1, 0, 3, 4)
        whitened = rows.reshape(groups, devices, 2 * bins, lanes)
    sources = [
        lax.all_to_all(whitened[g], "freq", split_axis=0, concat_axis=0, tiled=True)
        for g in range(groups)
    ]
    if not aligned:
        sources = [own.reshape(1, devices * 2 * bins, lanes) for own in sources]
    depth = local_windows * devices * 2 * bins
    out = None
    for g in range(groups):
        own = sources[g]
        if out is not None:
            own, out = lax.optimization_barrier((own, out))
        operands = [own, swap(own)]
        specs = [vmem] * len(operands)
        aliases = {}
        if out is not None:
            aliases = {len(operands): 0}
            operands, specs = [*operands, out], [*specs, memory]
        with jax.named_scope("outer_products"):
            out = pl.pallas_call(
                functools.partial(outer_kernel, bins, 1.0 / windows, g),
                out_shape=jax.ShapeDtypeStruct(
                    (2, local_bins, local_channels, 2 * local_channels), jnp.bfloat16
                ),
                grid=(bins,),
                in_specs=specs,
                out_specs=memory,
                input_output_aliases=aliases,
                scratch_shapes=[
                    pltpu.VMEM((depth, 4 * local_channels), jnp.bfloat16),
                    pltpu.VMEM((local_channels, depth), jnp.float32),
                    pltpu.VMEM((3, 2, local_channels, 2 * local_channels), jnp.bfloat16),
                    pltpu.SemaphoreType.DMA((3, CUTS, 2)),
                ],
                compiler_params=pltpu.CompilerParams(vmem_limit_bytes=32 * MIB),
                cost_estimate=pl.CostEstimate(
                    flops=8 * bins * depth * local_channels * local_channels,
                    bytes_accessed=8 * bins * local_channels * local_channels,
                    transcendentals=0,
                ),
            )(*operands)
    return jnp.transpose(out, (0, 1, 3, 2))


def solution(mesh):
    placed = (P("chan", ("hours", "freq"), None),)
    return jax.shard_map(
        local,
        mesh=mesh,
        in_specs=placed,
        out_specs=P(None, ("hours", "freq"), None, "chan"),
        check_vma=False,
    )
```

```python
import functools
import math

import jax
import jax.numpy as jnp
import ml_dtypes
import numpy as np
from jax import lax
from jax.experimental import pallas as pl
from jax.experimental.pallas import tpu as pltpu
from jax.sharding import PartitionSpec as P

BINS = 128
LANES = 128
MIB = 1024 * 1024


def bin_table(length, bins, group):
    position = np.arange(length)[None, :]
    number = np.arange(1, bins + 1)[:, None]
    phase = (position * number % length).astype(np.float32) * np.float32(2.0 * math.pi / length)
    taper = np.float32(0.5) - np.float32(0.5) * np.cos(
        position.astype(np.float32) * np.float32(2.0 * math.pi / length)
    )
    factor = np.float32(math.sqrt(8.0 / (3.0 * length)))
    table = np.stack([taper * np.cos(phase), -(taper * np.sin(phase))]) * factor
    table = table.reshape(2, bins // group, group, length).transpose(3, 1, 0, 2)
    return table.reshape(length, 2 * bins).astype(ml_dtypes.bfloat16)


def channel_blocks(channels):
    return [
        (first, min(LANES, channels - first), 2 * first) for first in range(0, channels, LANES)
    ]


def whiten_kernel(group, masks, spectrum_ref, *refs):
    pieces, rows_ref = refs[:-1], refs[-1]
    windows, channels, columns = spectrum_ref.shape
    bins = columns // 2
    row = lax.broadcasted_iota(jnp.int32, (bins, 1), 0)
    count = jnp.minimum(row + 2, bins - 1) - jnp.maximum(row - 2, 0) + 1
    share = 1.0 / count.astype(jnp.float32)

    for first, width, lane in channel_blocks(channels):
        blocks = [
            spectrum_ref[w, first : first + width, :].astype(jnp.float32).T
            for w in range(windows)
        ]
        spectrum = jnp.concatenate(blocks, axis=1)
        cols = windows * width
        parts = spectrum.reshape(bins // group, 2, group, cols)
        power = (parts[:, 0] * parts[:, 0] + parts[:, 1] * parts[:, 1]).reshape(bins, cols)
        summed = power
        for step in (1, 2):
            summed = summed + jnp.where(row >= step, pltpu.roll(power, step, axis=0), 0.0)
            summed = summed + jnp.where(
                row < bins - step, pltpu.roll(power, bins - step, axis=0), 0.0
            )
        level = jnp.maximum(summed * share, 0.1)
        inverse = lax.rsqrt(level).reshape(bins // group, 1, group, cols)
        whitened = (parts * inverse).astype(jnp.bfloat16)
        rows_ref[..., lane : lane + cols] = whitened.reshape(rows_ref.shape[:-1] + (cols,))

    if len(pieces) == 1:
        pieces[0][...] = rows_ref[...]
    else:
        me = lax.axis_index("freq")
        for mask, piece in zip(masks, pieces):
            piece[...] = rows_ref[me ^ mask]


def swap_halves(tile):
    return pltpu.roll(tile, LANES // 2, axis=1)


def split_rows(tile, bins, sets):
    rows, lanes = tile.shape
    if sets == 1:
        first_part = (lax.broadcasted_iota(jnp.int32, (rows, 1), 0) // bins) % 2 == 0
        rotated = jnp.where(
            first_part, -pltpu.roll(tile, rows - bins, axis=0), pltpu.roll(tile, bins, axis=0)
        )
        return [(tile, rotated)]
    parts = tile.reshape(rows // (2 * bins), 2, bins, lanes)
    real, imag = parts[:, 0], parts[:, 1]
    within = bins // sets
    low = lax.broadcasted_iota(jnp.int32, real.shape, 1) < within
    turned_real, turned_imag = (pltpu.roll(part, within, axis=1) for part in (real, imag))
    found = [
        (jnp.where(low, real, turned_imag), jnp.where(low, -imag, turned_real)),
        (jnp.where(low, turned_real, imag), jnp.where(low, -turned_imag, real)),
    ]
    return [tuple(part.reshape(rows // sets, lanes) for part in pair) for pair in found]


def outer_kernel(bins, sets, scale, *refs):
    out_ref, right, left, slots, sems = refs[-5:]
    count = (len(refs) - 5) // 2
    own_refs, other_refs = refs[:count], refs[count:-5]
    half = LANES // 2
    channels = out_ref.shape[2]
    full = channels // LANES
    step = pl.program_id(1)
    now = pl.program_id(0) * bins + step
    steps = pl.num_programs(0) * bins
    depth_of_slots, cuts = sems.shape[:2]
    size = channels // cuts

    def copy(when, cut, part):
        slot = lax.rem(when, depth_of_slots)
        at = pl.ds(cut * size, size)
        return pltpu.make_async_copy(
            slots.at[slot, part, at], out_ref.at[part, when, at], sems.at[slot, cut, part]
        )

    def wait_for(when):
        for cut in range(cuts):
            for part in range(2):
                copy(when, cut, part).wait()

    @pl.when(step == 0)
    def _():
        me = lax.axis_index("chan")
        which = pl.program_id(0)
        own = jnp.concatenate([ref[which].astype(jnp.float32) for ref in own_refs])
        other = jnp.concatenate([ref[which].astype(jnp.float32) for ref in other_refs])
        rows = own.shape[0]
        block0 = jnp.where(me == 0, own, other)
        block1 = jnp.where(me == 0, other, own)
        low = lax.broadcasted_iota(jnp.int32, (rows, LANES), 1) < half

        def tiles_of(block, w):
            tiles = [
                block[:, (2 * j + w) * LANES : (2 * j + w + 1) * LANES] for j in range(full)
            ]
            last = block[:, 2 * full * LANES :]
            turned = swap_halves(last)
            both = jnp.where(low, last, turned) if w == 0 else jnp.where(low, turned, last)
            return tiles, both

        share = rows // sets
        for w in range(2):
            at = pl.ds(w * share, share)
            tiles, last0 = tiles_of(block0, w)
            tiles1, last1 = tiles_of(block1, w)
            turned = [swap_halves(tile) for tile in tiles1]
            chain = [last0] + turned + [last1]
            tiles = tiles + [
                jnp.where(low, chain[j], chain[j + 1]) for j in range(len(chain) - 1)
            ]
            for j, tile in enumerate(tiles):
                lanes = slice(j * LANES, (j + 1) * LANES)
                lanes_imag = slice(2 * channels + j * LANES, 2 * channels + (j + 1) * LANES)
                for q, (plain, rotated) in enumerate(split_rows(tile, bins, sets)):
                    right[q, at, lanes] = plain.astype(jnp.bfloat16)
                    right[q, at, lanes_imag] = rotated.astype(jnp.bfloat16)
        scaled = own * scale
        for j in range(full + 1):
            block = scaled[:, 2 * j * LANES : (2 * j + 2) * LANES]
            if j < full:
                windows = [block[:, :LANES], block[:, LANES:]]
            else:
                windows = [block, swap_halves(block)]
            kept = min(LANES, channels - j * LANES)
            pieces = [split_rows(window, bins, sets) for window in windows]
            for q in range(sets):
                turned = jnp.concatenate([piece[q][0] for piece in pieces]).T
                left[q, j * LANES : j * LANES + kept] = turned[:kept]

    depth = left.shape[2]
    within = bins // sets
    lane = lax.broadcasted_iota(jnp.int32, (1, depth), 1)
    taken = (lane & (within - 1)) == (step & (within - 1))
    chosen = jnp.where(taken, left[step // within], 0.0).astype(jnp.bfloat16)
    weights = right.at[step // within]

    @pl.when(now >= depth_of_slots)
    def _():
        wait_for(now - depth_of_slots)

    slot = lax.rem(now, depth_of_slots)

    whole = 2 * channels // (2 * LANES) * (2 * LANES)
    starts = [0, whole, 4 * channels - whole, 4 * channels]
    left_over = 2 * channels - whole

    def multiply(first, last):
        return jnp.dot(
            chosen, weights[:, first:last], preferred_element_type=jnp.float32
        ).astype(jnp.bfloat16)

    def send(part):
        for cut in range(cuts):
            copy(now, cut, part).start()

    slots[slot, 0, :, :whole] = multiply(*starts[:2])
    if left_over:
        both = multiply(*starts[1:3])
        slots[slot, 0, :, whole:] = both[:, :left_over]
        slots[slot, 1, :, :left_over] = both[:, left_over:]
    send(0)
    slots[slot, 1, :, left_over:] = multiply(*starts[2:])
    send(1)

    @pl.when(now == steps - 1)
    def _():
        for back in reversed(range(depth_of_slots)):
            wait_for(now - back)


def copy_kernel(in_ref, out_ref):
    out_ref[...] = in_ref[...]


def exchange(value, mask):
    pairs = [(source, source ^ mask) for source in range(lax.axis_size("freq"))]
    return lax.ppermute(value, "freq", pairs) if mask else value


def swap(value):
    return lax.ppermute(value, "chan", [(0, 1), (1, 0)])


def local(samples):
    local_channels, local_windows, length = samples.shape
    devices = lax.axis_size("freq")
    local_bins = BINS // devices
    windows = local_windows * devices
    bins = min(local_bins, 128 // (2 * devices))
    groups = local_bins // bins
    aligned = bins == 8
    group = bins if aligned else BINS
    table = jnp.asarray(bin_table(length, BINS, group))
    lanes = local_windows * local_channels
    vmem = pl.BlockSpec(memory_space=pltpu.VMEM)
    memory = pl.BlockSpec(memory_space=pl.ANY)
    masks = [1, 2, *range(devices - 1, 2, -1), 0] if aligned else [0]
    pieces = len(masks)
    rows = (devices, groups, 2 * bins, lanes) if aligned else (2 * BINS, lanes)
    piece = rows[1:] if aligned else rows
    with jax.named_scope("table"):
        table = pl.pallas_call(
            copy_kernel,
            out_shape=jax.ShapeDtypeStruct(table.shape, table.dtype),
            in_specs=[vmem],
            out_specs=vmem,
            compiler_params=pltpu.CompilerParams(vmem_limit_bytes=8 * MIB),
        )(table)
    spectrum = jnp.einsum("cws,sj->wcj", samples, table, preferred_element_type=jnp.float32)
    spectrum = spectrum.astype(jnp.bfloat16)
    with jax.named_scope("whiten"):
        whitened = pl.pallas_call(
            functools.partial(whiten_kernel, group, masks),
            out_shape=[jax.ShapeDtypeStruct(piece, jnp.bfloat16)] * pieces,
            in_specs=[vmem],
            out_specs=[vmem] * pieces,
            scratch_shapes=[pltpu.VMEM(rows, jnp.bfloat16)],
            compiler_params=pltpu.CompilerParams(vmem_limit_bytes=16 * MIB),
            cost_estimate=pl.CostEstimate(
                flops=40 * BINS * lanes, bytes_accessed=12 * BINS * lanes, transcendentals=BINS * lanes
            ),
        )(spectrum)
    if aligned:
        own = [exchange(value, mask) for mask, value in zip(masks, whitened)]
    else:
        rows = whitened[0].reshape(2, devices, groups, bins, lanes).transpose(1, 2, 0, 3, 4)
        rows = rows.reshape(devices, groups, 2 * bins, lanes)
        rows = lax.all_to_all(rows, "freq", split_axis=0, concat_axis=0, tiled=True)
        own = [rows.transpose(1, 0, 2, 3).reshape(groups, devices * 2 * bins, lanes)]
    other = [swap(value) for value in own]
    sets = 2 if aligned else 1
    depth = local_windows * devices * 2 * bins // sets
    with jax.named_scope("outer_products"):
        out = pl.pallas_call(
            functools.partial(outer_kernel, bins, sets, 1.0 / windows),
            out_shape=jax.ShapeDtypeStruct(
                (2, local_bins, local_channels, 2 * local_channels), jnp.bfloat16
            ),
            grid=(groups, bins),
            in_specs=[vmem] * (2 * pieces),
            out_specs=memory,
            scratch_shapes=[
                pltpu.VMEM((sets, depth, 4 * local_channels), jnp.bfloat16),
                pltpu.VMEM((sets, local_channels, depth), jnp.float32),
                pltpu.VMEM((3, 2, local_channels, 2 * local_channels), jnp.bfloat16),
                pltpu.SemaphoreType.DMA((3, 2, 2)),
            ],
            compiler_params=pltpu.CompilerParams(vmem_limit_bytes=32 * MIB),
            cost_estimate=pl.CostEstimate(
                flops=8 * local_bins * depth * local_channels * local_channels,
                bytes_accessed=8 * local_bins * local_channels * local_channels,
                transcendentals=0,
            ),
        )(*own, *other)
    return jnp.transpose(out, (0, 1, 3, 2))


def solution(mesh):
    placed = (P("chan", ("hours", "freq"), None),)
    return jax.shard_map(
        local,
        mesh=mesh,
        in_specs=placed,
        out_specs=P(None, ("hours", "freq"), None, "chan"),
        check_vma=False,
    )
```

```python
import functools
import math

import jax
import jax.numpy as jnp
import ml_dtypes
import numpy as np
from jax import lax
from jax.experimental import pallas as pl
from jax.experimental.pallas import tpu as pltpu
from jax.sharding import PartitionSpec as P

BINS = 128
LANES = 128
MIB = 1024 * 1024


def bin_table(length, bins, group):
    position = np.arange(length)[None, :]
    number = np.arange(1, bins + 1)[:, None]
    phase = (position * number % length).astype(np.float32) * np.float32(2.0 * math.pi / length)
    taper = np.float32(0.5) - np.float32(0.5) * np.cos(
        position.astype(np.float32) * np.float32(2.0 * math.pi / length)
    )
    factor = np.float32(math.sqrt(8.0 / (3.0 * length)))
    table = np.stack([taper * np.cos(phase), -(taper * np.sin(phase))]) * factor
    table = table.reshape(2, bins // group, group, length).transpose(3, 1, 0, 2)
    return table.reshape(length, 2 * bins).astype(ml_dtypes.bfloat16)


def channel_blocks(channels):
    return [
        (first, min(LANES, channels - first), 2 * first) for first in range(0, channels, LANES)
    ]


def whiten_kernel(group, masks, spectrum_ref, *refs):
    pieces, rows_ref = refs[:-1], refs[-1]
    windows, channels, columns = spectrum_ref.shape
    bins = columns // 2
    row = lax.broadcasted_iota(jnp.int32, (bins, 1), 0)
    count = jnp.minimum(row + 2, bins - 1) - jnp.maximum(row - 2, 0) + 1
    share = 1.0 / count.astype(jnp.float32)

    for first, width, lane in channel_blocks(channels):
        blocks = [
            spectrum_ref[w, first : first + width, :].astype(jnp.float32).T
            for w in range(windows)
        ]
        spectrum = jnp.concatenate(blocks, axis=1)
        cols = windows * width
        parts = spectrum.reshape(bins // group, 2, group, cols)
        power = (parts[:, 0] * parts[:, 0] + parts[:, 1] * parts[:, 1]).reshape(bins, cols)
        summed = power
        for step in (1, 2):
            summed = summed + jnp.where(row >= step, pltpu.roll(power, step, axis=0), 0.0)
            summed = summed + jnp.where(
                row < bins - step, pltpu.roll(power, bins - step, axis=0), 0.0
            )
        level = jnp.maximum(summed * share, 0.1)
        inverse = lax.rsqrt(level).reshape(bins // group, 1, group, cols)
        whitened = (parts * inverse).astype(jnp.bfloat16)
        rows_ref[..., lane : lane + cols] = whitened.reshape(rows_ref.shape[:-1] + (cols,))

    if len(pieces) == 1:
        pieces[0][...] = rows_ref[...]
    else:
        me = lax.axis_index("freq")
        for mask, piece in zip(masks, pieces):
            piece[...] = rows_ref[me ^ mask]


def swap_halves(tile):
    return pltpu.roll(tile, LANES // 2, axis=1)


def rows_of_set(tile, bins, sets, q):
    rows, lanes = tile.shape
    if sets == 1:
        first_part = (lax.broadcasted_iota(jnp.int32, (rows, 1), 0) // bins) % 2 == 0
        rotated = jnp.where(
            first_part, -pltpu.roll(tile, rows - bins, axis=0), pltpu.roll(tile, bins, axis=0)
        )
        return tile, rotated
    parts = tile.reshape(rows // (2 * bins), 2, bins, lanes)
    real, imag = parts[:, 0], parts[:, 1]
    within = bins // sets
    low = lax.broadcasted_iota(jnp.int32, real.shape, 1) < within
    turned_real, turned_imag = (pltpu.roll(part, within, axis=1) for part in (real, imag))
    if q == 0:
        found = jnp.where(low, real, turned_imag), jnp.where(low, -imag, turned_real)
    else:
        found = jnp.where(low, turned_real, imag), jnp.where(low, -turned_imag, real)
    return tuple(part.reshape(rows // sets, lanes) for part in found)


def outer_kernel(bins, sets, scale, *refs):
    out_ref, right, left, slots, sems = refs[-5:]
    count = (len(refs) - 5) // 2
    own_refs, other_refs = refs[:count], refs[count:-5]
    half = LANES // 2
    channels = out_ref.shape[2]
    full = channels // LANES
    step = pl.program_id(1)
    now = pl.program_id(0) * bins + step
    steps = pl.num_programs(0) * bins
    depth_of_slots, cuts = sems.shape[:2]
    size = channels // cuts

    def copy(when, cut, part):
        slot = lax.rem(when, depth_of_slots)
        at = pl.ds(cut * size, size)
        return pltpu.make_async_copy(
            slots.at[slot, part, at], out_ref.at[part, when, at], sems.at[slot, cut, part]
        )

    def wait_for(when):
        for cut in range(cuts):
            for part in range(2):
                copy(when, cut, part).wait()

    def prepare(q):
        me = lax.axis_index("chan")
        which = pl.program_id(0)
        own = jnp.concatenate([ref[which].astype(jnp.float32) for ref in own_refs])
        other = jnp.concatenate([ref[which].astype(jnp.float32) for ref in other_refs])
        rows = own.shape[0]
        block0 = jnp.where(me == 0, own, other)
        block1 = jnp.where(me == 0, other, own)
        low = lax.broadcasted_iota(jnp.int32, (rows, LANES), 1) < half

        def tiles_of(block, w):
            tiles = [
                block[:, (2 * j + w) * LANES : (2 * j + w + 1) * LANES] for j in range(full)
            ]
            last = block[:, 2 * full * LANES :]
            turned = swap_halves(last)
            both = jnp.where(low, last, turned) if w == 0 else jnp.where(low, turned, last)
            return tiles, both

        share = rows // sets
        for w in range(2):
            at = pl.ds(w * share, share)
            tiles, last0 = tiles_of(block0, w)
            tiles1, last1 = tiles_of(block1, w)
            turned = [swap_halves(tile) for tile in tiles1]
            chain = [last0] + turned + [last1]
            tiles = tiles + [
                jnp.where(low, chain[j], chain[j + 1]) for j in range(len(chain) - 1)
            ]
            for j, tile in enumerate(tiles):
                lanes = slice(j * LANES, (j + 1) * LANES)
                lanes_imag = slice(2 * channels + j * LANES, 2 * channels + (j + 1) * LANES)
                plain, rotated = rows_of_set(tile, bins, sets, q)
                right[q, at, lanes] = plain.astype(jnp.bfloat16)
                right[q, at, lanes_imag] = rotated.astype(jnp.bfloat16)
        scaled = own * scale
        for j in range(full + 1):
            block = scaled[:, 2 * j * LANES : (2 * j + 2) * LANES]
            if j < full:
                windows = [block[:, :LANES], block[:, LANES:]]
            else:
                windows = [block, swap_halves(block)]
            kept = min(LANES, channels - j * LANES)
            pieces = [rows_of_set(window, bins, sets, q)[0] for window in windows]
            left[q, j * LANES : j * LANES + kept] = jnp.concatenate(pieces).T[:kept]

    for q in range(sets):
        pl.when(step == q * (bins // sets))(functools.partial(prepare, q))

    depth = left.shape[2]
    within = bins // sets
    lane = lax.broadcasted_iota(jnp.int32, (1, depth), 1)
    taken = (lane & (within - 1)) == (step & (within - 1))
    chosen = jnp.where(taken, left[step // within], 0.0).astype(jnp.bfloat16)
    weights = right.at[step // within]

    @pl.when(now >= depth_of_slots)
    def _():
        wait_for(now - depth_of_slots)

    slot = lax.rem(now, depth_of_slots)

    whole = 2 * channels // (2 * LANES) * (2 * LANES)
    starts = [0, whole, 4 * channels - whole, 4 * channels]
    left_over = 2 * channels - whole

    def multiply(first, last):
        return jnp.dot(
            chosen, weights[:, first:last], preferred_element_type=jnp.float32
        ).astype(jnp.bfloat16)

    def send(part):
        for cut in range(cuts):
            copy(now, cut, part).start()

    slots[slot, 0, :, :whole] = multiply(*starts[:2])
    if left_over:
        both = multiply(*starts[1:3])
        slots[slot, 0, :, whole:] = both[:, :left_over]
        slots[slot, 1, :, :left_over] = both[:, left_over:]
    send(0)
    slots[slot, 1, :, left_over:] = multiply(*starts[2:])
    send(1)

    @pl.when(now == steps - 1)
    def _():
        for back in reversed(range(depth_of_slots)):
            wait_for(now - back)


def copy_kernel(in_ref, out_ref):
    out_ref[...] = in_ref[...]


def exchange(value, mask):
    pairs = [(source, source ^ mask) for source in range(lax.axis_size("freq"))]
    return lax.ppermute(value, "freq", pairs) if mask else value


def swap(value):
    return lax.ppermute(value, "chan", [(0, 1), (1, 0)])


def local(samples):
    local_channels, local_windows, length = samples.shape
    devices = lax.axis_size("freq")
    local_bins = BINS // devices
    windows = local_windows * devices
    bins = min(local_bins, 128 // (2 * devices))
    groups = local_bins // bins
    aligned = bins == 8
    group = bins if aligned else BINS
    table = jnp.asarray(bin_table(length, BINS, group))
    lanes = local_windows * local_channels
    vmem = pl.BlockSpec(memory_space=pltpu.VMEM)
    memory = pl.BlockSpec(memory_space=pl.ANY)
    masks = [*range(devices - 1, devices // 2 - 1, -1), *range(1, devices // 2), 0]
    masks = masks if aligned else [0]
    pieces = len(masks)
    rows = (devices, groups, 2 * bins, lanes) if aligned else (2 * BINS, lanes)
    piece = rows[1:] if aligned else rows
    with jax.named_scope("table"):
        table = pl.pallas_call(
            copy_kernel,
            out_shape=jax.ShapeDtypeStruct(table.shape, table.dtype),
            in_specs=[vmem],
            out_specs=vmem,
            compiler_params=pltpu.CompilerParams(vmem_limit_bytes=8 * MIB),
        )(table)
    spectrum = jnp.einsum("cws,sj->wcj", samples, table, preferred_element_type=jnp.float32)
    spectrum = spectrum.astype(jnp.bfloat16)
    with jax.named_scope("whiten"):
        whitened = pl.pallas_call(
            functools.partial(whiten_kernel, group, masks),
            out_shape=[jax.ShapeDtypeStruct(piece, jnp.bfloat16)] * pieces,
            in_specs=[vmem],
            out_specs=[vmem] * pieces,
            scratch_shapes=[pltpu.VMEM(rows, jnp.bfloat16)],
            compiler_params=pltpu.CompilerParams(vmem_limit_bytes=16 * MIB),
            cost_estimate=pl.CostEstimate(
                flops=40 * BINS * lanes, bytes_accessed=12 * BINS * lanes, transcendentals=BINS * lanes
            ),
        )(spectrum)
    if aligned:
        own = [exchange(value, mask) for mask, value in zip(masks, whitened)]
    else:
        rows = whitened[0].reshape(2, devices, groups, bins, lanes).transpose(1, 2, 0, 3, 4)
        rows = rows.reshape(devices, groups, 2 * bins, lanes)
        rows = lax.all_to_all(rows, "freq", split_axis=0, concat_axis=0, tiled=True)
        own = [rows.transpose(1, 0, 2, 3).reshape(groups, devices * 2 * bins, lanes)]
    other = [swap(value) for value in own]
    sets = 2 if aligned else 1
    depth = local_windows * devices * 2 * bins // sets
    with jax.named_scope("outer_products"):
        out = pl.pallas_call(
            functools.partial(outer_kernel, bins, sets, 1.0 / windows),
            out_shape=jax.ShapeDtypeStruct(
                (2, local_bins, local_channels, 2 * local_channels), jnp.bfloat16
            ),
            grid=(groups, bins),
            in_specs=[vmem] * (2 * pieces),
            out_specs=memory,
            scratch_shapes=[
                pltpu.VMEM((sets, depth, 4 * local_channels), jnp.bfloat16),
                pltpu.VMEM((sets, local_channels, depth), jnp.float32),
                pltpu.VMEM((3, 2, local_channels, 2 * local_channels), jnp.bfloat16),
                pltpu.SemaphoreType.DMA((3, 1, 2)),
            ],
            compiler_params=pltpu.CompilerParams(vmem_limit_bytes=32 * MIB),
            cost_estimate=pl.CostEstimate(
                flops=8 * local_bins * depth * local_channels * local_channels,
                bytes_accessed=8 * local_bins * local_channels * local_channels,
                transcendentals=0,
            ),
        )(*own, *other)
    return jnp.transpose(out, (0, 1, 3, 2))


def solution(mesh):
    placed = (P("chan", ("hours", "freq"), None),)
    return jax.shard_map(
        local,
        mesh=mesh,
        in_specs=placed,
        out_specs=P(None, ("hours", "freq"), None, "chan"),
        check_vma=False,
    )
```

```python
import functools
import math

import jax
import jax.numpy as jnp
import ml_dtypes
import numpy as np
from jax import lax
from jax.experimental import pallas as pl
from jax.experimental.pallas import tpu as pltpu
from jax.sharding import PartitionSpec as P

BINS = 128
LANES = 128
MIB = 1024 * 1024


def bin_table(length, bins, group):
    position = np.arange(length)[None, :]
    number = np.arange(1, bins + 1)[:, None]
    phase = (position * number % length).astype(np.float32) * np.float32(2.0 * math.pi / length)
    taper = np.float32(0.5) - np.float32(0.5) * np.cos(
        position.astype(np.float32) * np.float32(2.0 * math.pi / length)
    )
    factor = np.float32(math.sqrt(8.0 / (3.0 * length)))
    table = np.stack([taper * np.cos(phase), -(taper * np.sin(phase))]) * factor
    table = table.reshape(2, bins // group, group, length).transpose(3, 1, 0, 2)
    return table.reshape(length, 2 * bins).astype(ml_dtypes.bfloat16)


def channel_blocks(channels):
    return [
        (first, min(LANES, channels - first), 2 * first) for first in range(0, channels, LANES)
    ]


def whiten_kernel(group, masks, spectrum_ref, *refs):
    pieces, rows_ref = refs[:-1], refs[-1]
    windows, channels, columns = spectrum_ref.shape
    bins = columns // 2
    row = lax.broadcasted_iota(jnp.int32, (bins, 1), 0)
    count = jnp.minimum(row + 2, bins - 1) - jnp.maximum(row - 2, 0) + 1
    share = 1.0 / count.astype(jnp.float32)

    for first, width, lane in channel_blocks(channels):
        blocks = [
            spectrum_ref[w, first : first + width, :].astype(jnp.float32).T
            for w in range(windows)
        ]
        spectrum = jnp.concatenate(blocks, axis=1)
        cols = windows * width
        parts = spectrum.reshape(bins // group, 2, group, cols)
        power = (parts[:, 0] * parts[:, 0] + parts[:, 1] * parts[:, 1]).reshape(bins, cols)
        summed = power
        for step in (1, 2):
            summed = summed + jnp.where(row >= step, pltpu.roll(power, step, axis=0), 0.0)
            summed = summed + jnp.where(
                row < bins - step, pltpu.roll(power, bins - step, axis=0), 0.0
            )
        level = jnp.maximum(summed * share, 0.1)
        inverse = lax.rsqrt(level).reshape(bins // group, 1, group, cols)
        whitened = (parts * inverse).astype(jnp.bfloat16)
        rows_ref[..., lane : lane + cols] = whitened.reshape(rows_ref.shape[:-1] + (cols,))

    if len(pieces) == 1:
        pieces[0][...] = rows_ref[...]
    else:
        me = lax.axis_index("freq")
        for mask, piece in zip(masks, pieces):
            piece[...] = rows_ref[me ^ mask]


def swap_halves(tile):
    return pltpu.roll(tile, LANES // 2, axis=1)


def rows_of_set(tile, bins, sets, q):
    rows, lanes = tile.shape
    if sets == 1:
        first_part = (lax.broadcasted_iota(jnp.int32, (rows, 1), 0) // bins) % 2 == 0
        rotated = jnp.where(
            first_part, -pltpu.roll(tile, rows - bins, axis=0), pltpu.roll(tile, bins, axis=0)
        )
        return tile, rotated
    parts = tile.reshape(rows // (2 * bins), 2, bins, lanes)
    real, imag = parts[:, 0], parts[:, 1]
    within = bins // sets
    low = lax.broadcasted_iota(jnp.int32, real.shape, 1) < within
    turned_real, turned_imag = (pltpu.roll(part, within, axis=1) for part in (real, imag))
    if q == 0:
        found = jnp.where(low, real, turned_imag), jnp.where(low, -imag, turned_real)
    else:
        found = jnp.where(low, turned_real, imag), jnp.where(low, -turned_imag, real)
    return tuple(part.reshape(rows // sets, lanes) for part in found)


def outer_kernel(bins, sets, scale, *refs):
    out_ref, right, left, slots, sems = refs[-5:]
    count = (len(refs) - 5) // 2
    own_refs, other_refs = refs[:count], refs[count:-5]
    half = LANES // 2
    channels = out_ref.shape[2]
    full = channels // LANES
    part, step = pl.program_id(1), pl.program_id(2)
    now = (pl.program_id(0) * 2 + part) * bins + step
    steps = pl.num_programs(0) * 2 * bins
    depth_of_slots, cuts = sems.shape
    size = channels // cuts

    def copy(when, cut):
        slot = lax.rem(when, depth_of_slots)
        at = pl.ds(cut * size, size)
        into, run = lax.rem(when // bins, 2), when // (2 * bins)
        return pltpu.make_async_copy(
            slots.at[slot, at],
            out_ref.at[into, run * bins + lax.rem(when, bins), at],
            sems.at[slot, cut],
        )

    def wait_for(when):
        for cut in range(cuts):
            copy(when, cut).wait()

    def prepare(q):
        me = lax.axis_index("chan")
        which = pl.program_id(0)
        own = jnp.concatenate([ref[which].astype(jnp.float32) for ref in own_refs])
        other = jnp.concatenate([ref[which].astype(jnp.float32) for ref in other_refs])
        rows = own.shape[0]
        block0 = jnp.where(me == 0, own, other)
        block1 = jnp.where(me == 0, other, own)
        low = lax.broadcasted_iota(jnp.int32, (rows, LANES), 1) < half

        def tiles_of(block, w):
            tiles = [
                block[:, (2 * j + w) * LANES : (2 * j + w + 1) * LANES] for j in range(full)
            ]
            last = block[:, 2 * full * LANES :]
            turned = swap_halves(last)
            both = jnp.where(low, last, turned) if w == 0 else jnp.where(low, turned, last)
            return tiles, both

        share = rows // sets
        for w in range(2):
            at = pl.ds(w * share, share)
            tiles, last0 = tiles_of(block0, w)
            tiles1, last1 = tiles_of(block1, w)
            turned = [swap_halves(tile) for tile in tiles1]
            chain = [last0] + turned + [last1]
            tiles = tiles + [
                jnp.where(low, chain[j], chain[j + 1]) for j in range(len(chain) - 1)
            ]
            for j, tile in enumerate(tiles):
                lanes = slice(j * LANES, (j + 1) * LANES)
                plain, rotated = rows_of_set(tile, bins, sets, q)
                right[0, q, at, lanes] = plain.astype(jnp.bfloat16)
                right[1, q, at, lanes] = rotated.astype(jnp.bfloat16)
        scaled = own * scale
        for j in range(full + 1):
            block = scaled[:, 2 * j * LANES : (2 * j + 2) * LANES]
            if j < full:
                windows = [block[:, :LANES], block[:, LANES:]]
            else:
                windows = [block, swap_halves(block)]
            kept = min(LANES, channels - j * LANES)
            pieces = [rows_of_set(window, bins, sets, q)[0] for window in windows]
            left[q, j * LANES : j * LANES + kept] = jnp.concatenate(pieces).T[:kept]

    for q in range(sets):
        pl.when((part == 0) & (step == q * (bins // sets)))(functools.partial(prepare, q))

    depth = left.shape[2]
    within = bins // sets
    lane = lax.broadcasted_iota(jnp.int32, (1, depth), 1)
    taken = (lane & (within - 1)) == (step & (within - 1))
    chosen = jnp.where(taken, left[step // within], 0.0).astype(jnp.bfloat16)
    weights = right.at[part, step // within]

    @pl.when(now >= depth_of_slots)
    def _():
        wait_for(now - depth_of_slots)

    slot = lax.rem(now, depth_of_slots)

    for cut in range(cuts):
        at = slice(cut * size, (cut + 1) * size)
        product = jnp.dot(chosen[at], weights[...], preferred_element_type=jnp.float32)
        slots[slot, at] = product.astype(jnp.bfloat16)
        copy(now, cut).start()

    @pl.when(now == steps - 1)
    def _():
        for back in reversed(range(depth_of_slots)):
            wait_for(now - back)


def copy_kernel(in_ref, out_ref):
    out_ref[...] = in_ref[...]


def exchange(value, mask):
    pairs = [(source, source ^ mask) for source in range(lax.axis_size("freq"))]
    return lax.ppermute(value, "freq", pairs) if mask else value


def swap(value):
    return lax.ppermute(value, "chan", [(0, 1), (1, 0)])


def local(samples):
    local_channels, local_windows, length = samples.shape
    devices = lax.axis_size("freq")
    local_bins = BINS // devices
    windows = local_windows * devices
    bins = min(local_bins, 128 // (2 * devices))
    groups = local_bins // bins
    aligned = bins == 8
    group = bins if aligned else BINS
    table = jnp.asarray(bin_table(length, BINS, group))
    lanes = local_windows * local_channels
    vmem = pl.BlockSpec(memory_space=pltpu.VMEM)
    memory = pl.BlockSpec(memory_space=pl.ANY)
    masks = [devices - 1, 1, 2, *range(devices - 2, 2, -1), 0] if aligned else [0]
    pieces = len(masks)
    rows = (devices, groups, 2 * bins, lanes) if aligned else (2 * BINS, lanes)
    piece = rows[1:] if aligned else rows
    with jax.named_scope("table"):
        table = pl.pallas_call(
            copy_kernel,
            out_shape=jax.ShapeDtypeStruct(table.shape, table.dtype),
            in_specs=[vmem],
            out_specs=vmem,
            compiler_params=pltpu.CompilerParams(vmem_limit_bytes=8 * MIB),
        )(table)
    spectrum = jnp.einsum("cws,sj->wcj", samples, table, preferred_element_type=jnp.float32)
    spectrum = spectrum.astype(jnp.bfloat16)
    with jax.named_scope("whiten"):
        whitened = pl.pallas_call(
            functools.partial(whiten_kernel, group, masks),
            out_shape=[jax.ShapeDtypeStruct(piece, jnp.bfloat16)] * pieces,
            in_specs=[vmem],
            out_specs=[vmem] * pieces,
            scratch_shapes=[pltpu.VMEM(rows, jnp.bfloat16)],
            compiler_params=pltpu.CompilerParams(vmem_limit_bytes=16 * MIB),
            cost_estimate=pl.CostEstimate(
                flops=40 * BINS * lanes, bytes_accessed=12 * BINS * lanes, transcendentals=BINS * lanes
            ),
        )(spectrum)
    if aligned:
        own = [exchange(value, mask) for mask, value in zip(masks, whitened)]
    else:
        rows = whitened[0].reshape(2, devices, groups, bins, lanes).transpose(1, 2, 0, 3, 4)
        rows = rows.reshape(devices, groups, 2 * bins, lanes)
        rows = lax.all_to_all(rows, "freq", split_axis=0, concat_axis=0, tiled=True)
        own = [rows.transpose(1, 0, 2, 3).reshape(groups, devices * 2 * bins, lanes)]
    other = [swap(value) for value in own]
    sets = 2 if aligned else 1
    depth = local_windows * devices * 2 * bins // sets
    with jax.named_scope("outer_products"):
        out = pl.pallas_call(
            functools.partial(outer_kernel, bins, sets, 1.0 / windows),
            out_shape=jax.ShapeDtypeStruct(
                (2, local_bins, local_channels, 2 * local_channels), jnp.bfloat16
            ),
            grid=(groups, 2, bins),
            in_specs=[vmem] * (2 * pieces),
            out_specs=memory,
            scratch_shapes=[
                pltpu.VMEM((2, sets, depth, 2 * local_channels), jnp.bfloat16),
                pltpu.VMEM((sets, local_channels, depth), jnp.float32),
                pltpu.VMEM((4, local_channels, 2 * local_channels), jnp.bfloat16),
                pltpu.SemaphoreType.DMA((4, 2)),
            ],
            compiler_params=pltpu.CompilerParams(vmem_limit_bytes=32 * MIB),
            cost_estimate=pl.CostEstimate(
                flops=8 * local_bins * depth * local_channels * local_channels,
                bytes_accessed=8 * local_bins * local_channels * local_channels,
                transcendentals=0,
            ),
        )(*own, *other)
    return jnp.transpose(out, (0, 1, 3, 2))


def solution(mesh):
    placed = (P("chan", ("hours", "freq"), None),)
    return jax.shard_map(
        local,
        mesh=mesh,
        in_specs=placed,
        out_specs=P(None, ("hours", "freq"), None, "chan"),
        check_vma=False,
    )
```

```python
import functools
import math

import jax
import jax.numpy as jnp
import ml_dtypes
import numpy as np
from jax import lax
from jax.experimental import pallas as pl
from jax.experimental.pallas import tpu as pltpu
from jax.sharding import PartitionSpec as P

BINS = 128
LANES = 128
ROWS = 96
COLUMNS = 512
MIB = 1024 * 1024


def bin_table(length, bins, group):
    position = np.arange(length)[None, :]
    number = np.arange(1, bins + 1)[:, None]
    phase = (position * number % length).astype(np.float32) * np.float32(2.0 * math.pi / length)
    taper = np.float32(0.5) - np.float32(0.5) * np.cos(
        position.astype(np.float32) * np.float32(2.0 * math.pi / length)
    )
    factor = np.float32(math.sqrt(8.0 / (3.0 * length)))
    table = np.stack([taper * np.cos(phase), -(taper * np.sin(phase))]) * factor
    table = table.reshape(2, bins // group, group, length).transpose(3, 1, 0, 2)
    return table.reshape(length, 2 * bins).astype(ml_dtypes.bfloat16)


def channel_blocks(channels):
    return [
        (first, min(LANES, channels - first), 2 * first) for first in range(0, channels, LANES)
    ]


def whiten_kernel(group, masks, spectrum_ref, *refs):
    pieces, rows_ref = refs[:-1], refs[-1]
    windows, channels, columns = spectrum_ref.shape
    bins = columns // 2
    row = lax.broadcasted_iota(jnp.int32, (bins, 1), 0)
    count = jnp.minimum(row + 2, bins - 1) - jnp.maximum(row - 2, 0) + 1
    share = 1.0 / count.astype(jnp.float32)

    for first, width, lane in channel_blocks(channels):
        blocks = [
            spectrum_ref[w, first : first + width, :].astype(jnp.float32).T
            for w in range(windows)
        ]
        spectrum = jnp.concatenate(blocks, axis=1)
        cols = windows * width
        parts = spectrum.reshape(bins // group, 2, group, cols)
        power = (parts[:, 0] * parts[:, 0] + parts[:, 1] * parts[:, 1]).reshape(bins, cols)
        summed = power
        for step in (1, 2):
            summed = summed + jnp.where(row >= step, pltpu.roll(power, step, axis=0), 0.0)
            summed = summed + jnp.where(
                row < bins - step, pltpu.roll(power, bins - step, axis=0), 0.0
            )
        level = jnp.maximum(summed * share, 0.1)
        inverse = lax.rsqrt(level).reshape(bins // group, 1, group, cols)
        whitened = (parts * inverse).astype(jnp.bfloat16)
        rows_ref[..., lane : lane + cols] = whitened.reshape(rows_ref.shape[:-1] + (cols,))

    if len(pieces) == 1:
        pieces[0][...] = rows_ref[...]
    else:
        me = lax.axis_index("freq")
        for mask, piece in zip(masks, pieces):
            piece[...] = rows_ref[me ^ mask]


def swap_halves(tile):
    return pltpu.roll(tile, LANES // 2, axis=1)


def rows_of_set(tile, bins, sets, q):
    rows, lanes = tile.shape
    if sets == 1:
        first_part = (lax.broadcasted_iota(jnp.int32, (rows, 1), 0) // bins) % 2 == 0
        rotated = jnp.where(
            first_part, -pltpu.roll(tile, rows - bins, axis=0), pltpu.roll(tile, bins, axis=0)
        )
        return tile, rotated
    parts = tile.reshape(rows // (2 * bins), 2, bins, lanes)
    real, imag = parts[:, 0], parts[:, 1]
    within = bins // sets
    low = lax.broadcasted_iota(jnp.int32, real.shape, 1) < within
    turned_real, turned_imag = (pltpu.roll(part, within, axis=1) for part in (real, imag))
    if q == 0:
        found = jnp.where(low, real, turned_imag), jnp.where(low, -imag, turned_real)
    else:
        found = jnp.where(low, turned_real, imag), jnp.where(low, -turned_imag, real)
    return tuple(part.reshape(rows // sets, lanes) for part in found)


def outer_kernel(bins, sets, scale, *refs):
    out_ref, right, left, slots, sems = refs[-5:]
    count = (len(refs) - 5) // 2
    own_refs, other_refs = refs[:count], refs[count:-5]
    half = LANES // 2
    channels = out_ref.shape[2]
    full = channels // LANES
    step = pl.program_id(1)
    now = pl.program_id(0) * bins + step
    steps = pl.num_programs(0) * bins
    depth_of_slots, cuts = sems.shape[:2]
    size = channels // cuts

    def copy(when, cut, part):
        slot = lax.rem(when, depth_of_slots)
        at = pl.ds(cut * size, size)
        return pltpu.make_async_copy(
            slots.at[slot, part, at], out_ref.at[part, when, at], sems.at[slot, cut, part]
        )

    def wait_for(when):
        for cut in range(cuts):
            for part in range(2):
                copy(when, cut, part).wait()

    def prepare(q):
        me = lax.axis_index("chan")
        which = pl.program_id(0)
        own = jnp.concatenate([ref[which].astype(jnp.float32) for ref in own_refs])
        other = jnp.concatenate([ref[which].astype(jnp.float32) for ref in other_refs])
        rows = own.shape[0]
        block0 = jnp.where(me == 0, own, other)
        block1 = jnp.where(me == 0, other, own)
        low = lax.broadcasted_iota(jnp.int32, (rows, LANES), 1) < half

        def tiles_of(block, w):
            tiles = [
                block[:, (2 * j + w) * LANES : (2 * j + w + 1) * LANES] for j in range(full)
            ]
            last = block[:, 2 * full * LANES :]
            turned = swap_halves(last)
            both = jnp.where(low, last, turned) if w == 0 else jnp.where(low, turned, last)
            return tiles, both

        share = rows // sets
        for w in range(2):
            at = pl.ds(w * share, share)
            tiles, last0 = tiles_of(block0, w)
            tiles1, last1 = tiles_of(block1, w)
            turned = [swap_halves(tile) for tile in tiles1]
            chain = [last0] + turned + [last1]
            tiles = tiles + [
                jnp.where(low, chain[j], chain[j + 1]) for j in range(len(chain) - 1)
            ]
            for j, tile in enumerate(tiles):
                lanes = slice(j * LANES, (j + 1) * LANES)
                lanes_imag = slice(2 * channels + j * LANES, 2 * channels + (j + 1) * LANES)
                plain, rotated = rows_of_set(tile, bins, sets, q)
                right[q, at, lanes] = plain.astype(jnp.bfloat16)
                right[q, at, lanes_imag] = rotated.astype(jnp.bfloat16)
        scaled = own * scale
        for j in range(full + 1):
            block = scaled[:, 2 * j * LANES : (2 * j + 2) * LANES]
            if j < full:
                windows = [block[:, :LANES], block[:, LANES:]]
            else:
                windows = [block, swap_halves(block)]
            kept = min(LANES, channels - j * LANES)
            pieces = [rows_of_set(window, bins, sets, q)[0] for window in windows]
            left[q, j * LANES : j * LANES + kept] = jnp.concatenate(pieces).T[:kept]

    for q in range(sets):
        pl.when(step == q * (bins // sets))(functools.partial(prepare, q))

    depth = left.shape[2]
    within = bins // sets
    lane = lax.broadcasted_iota(jnp.int32, (1, depth), 1)
    taken = (lane & (within - 1)) == (step & (within - 1))
    chosen = jnp.where(taken, left[step // within], 0.0).astype(jnp.bfloat16)
    weights = right.at[step // within]

    @pl.when(now >= depth_of_slots)
    def _():
        wait_for(now - depth_of_slots)

    slot = lax.rem(now, depth_of_slots)

    for cut in range(cuts):
        for first in range(cut * size, (cut + 1) * size, ROWS):
            at = slice(first, first + ROWS)
            for lane in range(0, 4 * channels, COLUMNS):
                last = min(lane + COLUMNS, 4 * channels)
                product = jnp.dot(
                    chosen[at], weights[:, lane:last], preferred_element_type=jnp.float32
                ).astype(jnp.bfloat16)
                middle = min(max(lane, 2 * channels), last)
                if lane < middle:
                    slots[slot, 0, at, lane:middle] = product[:, : middle - lane]
                if middle < last:
                    begin, end = middle - 2 * channels, last - 2 * channels
                    slots[slot, 1, at, begin:end] = product[:, middle - lane :]
        for part in range(2):
            copy(now, cut, part).start()

    @pl.when(now == steps - 1)
    def _():
        for back in reversed(range(depth_of_slots)):
            wait_for(now - back)


def copy_kernel(in_ref, out_ref):
    out_ref[...] = in_ref[...]


def exchange(value, mask):
    pairs = [(source, source ^ mask) for source in range(lax.axis_size("freq"))]
    return lax.ppermute(value, "freq", pairs) if mask else value


def swap(value):
    return lax.ppermute(value, "chan", [(0, 1), (1, 0)])


def local(samples):
    local_channels, local_windows, length = samples.shape
    devices = lax.axis_size("freq")
    local_bins = BINS // devices
    windows = local_windows * devices
    bins = min(local_bins, 128 // (2 * devices))
    groups = local_bins // bins
    aligned = bins == 8
    group = bins if aligned else BINS
    table = jnp.asarray(bin_table(length, BINS, group))
    lanes = local_windows * local_channels
    vmem = pl.BlockSpec(memory_space=pltpu.VMEM)
    memory = pl.BlockSpec(memory_space=pl.ANY)
    masks = [devices - 1, 1, 2, *range(devices - 2, 2, -1), 0] if aligned else [0]
    pieces = len(masks)
    rows = (devices, groups, 2 * bins, lanes) if aligned else (2 * BINS, lanes)
    piece = rows[1:] if aligned else rows
    with jax.named_scope("table"):
        table = pl.pallas_call(
            copy_kernel,
            out_shape=jax.ShapeDtypeStruct(table.shape, table.dtype),
            in_specs=[vmem],
            out_specs=vmem,
            compiler_params=pltpu.CompilerParams(vmem_limit_bytes=8 * MIB),
        )(table)
    spectrum = jnp.einsum("cws,sj->wcj", samples, table, preferred_element_type=jnp.float32)
    spectrum = spectrum.astype(jnp.bfloat16)
    with jax.named_scope("whiten"):
        whitened = pl.pallas_call(
            functools.partial(whiten_kernel, group, masks),
            out_shape=[jax.ShapeDtypeStruct(piece, jnp.bfloat16)] * pieces,
            in_specs=[vmem],
            out_specs=[vmem] * pieces,
            scratch_shapes=[pltpu.VMEM(rows, jnp.bfloat16)],
            compiler_params=pltpu.CompilerParams(vmem_limit_bytes=16 * MIB),
            cost_estimate=pl.CostEstimate(
                flops=40 * BINS * lanes, bytes_accessed=12 * BINS * lanes, transcendentals=BINS * lanes
            ),
        )(spectrum)
    if aligned:
        own = [exchange(value, mask) for mask, value in zip(masks, whitened)]
    else:
        rows = whitened[0].reshape(2, devices, groups, bins, lanes).transpose(1, 2, 0, 3, 4)
        rows = rows.reshape(devices, groups, 2 * bins, lanes)
        rows = lax.all_to_all(rows, "freq", split_axis=0, concat_axis=0, tiled=True)
        own = [rows.transpose(1, 0, 2, 3).reshape(groups, devices * 2 * bins, lanes)]
    other = [swap(value) for value in own]
    sets = 2 if aligned else 1
    depth = local_windows * devices * 2 * bins // sets
    with jax.named_scope("outer_products"):
        out = pl.pallas_call(
            functools.partial(outer_kernel, bins, sets, 1.0 / windows),
            out_shape=jax.ShapeDtypeStruct(
                (2, local_bins, local_channels, 2 * local_channels), jnp.bfloat16
            ),
            grid=(groups, bins),
            in_specs=[vmem] * (2 * pieces),
            out_specs=memory,
            scratch_shapes=[
                pltpu.VMEM((sets, depth, 4 * local_channels), jnp.bfloat16),
                pltpu.VMEM((sets, local_channels, depth), jnp.float32),
                pltpu.VMEM((3, 2, local_channels, 2 * local_channels), jnp.bfloat16),
                pltpu.SemaphoreType.DMA((3, 2, 2)),
            ],
            compiler_params=pltpu.CompilerParams(vmem_limit_bytes=32 * MIB),
            cost_estimate=pl.CostEstimate(
                flops=8 * local_bins * depth * local_channels * local_channels,
                bytes_accessed=8 * local_bins * local_channels * local_channels,
                transcendentals=0,
            ),
        )(*own, *other)
    return jnp.transpose(out, (0, 1, 3, 2))


def solution(mesh):
    placed = (P("chan", ("hours", "freq"), None),)
    return jax.shard_map(
        local,
        mesh=mesh,
        in_specs=placed,
        out_specs=P(None, ("hours", "freq"), None, "chan"),
        check_vma=False,
    )
```

```python
import functools
import math

import jax
import jax.numpy as jnp
import ml_dtypes
import numpy as np
from jax import lax
from jax.experimental import pallas as pl
from jax.experimental.pallas import tpu as pltpu
from jax.sharding import PartitionSpec as P

BINS = 128
LANES = 128
MIB = 1024 * 1024


def bin_table(length, bins, group):
    position = np.arange(length)[None, :]
    number = np.arange(1, bins + 1)[:, None]
    phase = (position * number % length).astype(np.float32) * np.float32(2.0 * math.pi / length)
    taper = np.float32(0.5) - np.float32(0.5) * np.cos(
        position.astype(np.float32) * np.float32(2.0 * math.pi / length)
    )
    factor = np.float32(math.sqrt(8.0 / (3.0 * length)))
    table = np.stack([taper * np.cos(phase), -(taper * np.sin(phase))]) * factor
    table = table.reshape(2, bins // group, group, length).transpose(3, 1, 0, 2)
    return table.reshape(length, 2 * bins).astype(ml_dtypes.bfloat16)


def channel_blocks(channels):
    return [
        (first, min(LANES, channels - first), 2 * first) for first in range(0, channels, LANES)
    ]


def whiten_kernel(group, masks, spectrum_ref, *refs):
    pieces, rows_ref = refs[:-1], refs[-1]
    windows, channels, columns = spectrum_ref.shape
    bins = columns // 2
    row = lax.broadcasted_iota(jnp.int32, (bins, 1), 0)
    count = jnp.minimum(row + 2, bins - 1) - jnp.maximum(row - 2, 0) + 1
    share = 1.0 / count.astype(jnp.float32)

    for first, width, lane in channel_blocks(channels):
        blocks = [
            spectrum_ref[w, first : first + width, :].astype(jnp.float32).T
            for w in range(windows)
        ]
        spectrum = jnp.concatenate(blocks, axis=1)
        cols = windows * width
        parts = spectrum.reshape(bins // group, 2, group, cols)
        power = (parts[:, 0] * parts[:, 0] + parts[:, 1] * parts[:, 1]).reshape(bins, cols)
        summed = power
        for step in (1, 2):
            summed = summed + jnp.where(row >= step, pltpu.roll(power, step, axis=0), 0.0)
            summed = summed + jnp.where(
                row < bins - step, pltpu.roll(power, bins - step, axis=0), 0.0
            )
        level = jnp.maximum(summed * share, 0.1)
        inverse = lax.rsqrt(level).reshape(bins // group, 1, group, cols)
        whitened = (parts * inverse).astype(jnp.bfloat16)
        rows_ref[..., lane : lane + cols] = whitened.reshape(rows_ref.shape[:-1] + (cols,))

    if len(pieces) == 1:
        pieces[0][...] = rows_ref[...]
    else:
        me = lax.axis_index("freq")
        for mask, piece in zip(masks, pieces):
            piece[...] = rows_ref[me ^ mask]


def swap_halves(tile):
    return pltpu.roll(tile, LANES // 2, axis=1)


def rows_of_set(tile, bins, sets, q):
    rows, lanes = tile.shape
    if sets == 1:
        first_part = (lax.broadcasted_iota(jnp.int32, (rows, 1), 0) // bins) % 2 == 0
        rotated = jnp.where(
            first_part, -pltpu.roll(tile, rows - bins, axis=0), pltpu.roll(tile, bins, axis=0)
        )
        return tile, rotated
    parts = tile.reshape(rows // (2 * bins), 2, bins, lanes)
    real, imag = parts[:, 0], parts[:, 1]
    within = bins // sets
    low = lax.broadcasted_iota(jnp.int32, real.shape, 1) < within
    turned_real, turned_imag = (pltpu.roll(part, within, axis=1) for part in (real, imag))
    if q == 0:
        found = jnp.where(low, real, turned_imag), jnp.where(low, -imag, turned_real)
    else:
        found = jnp.where(low, turned_real, imag), jnp.where(low, -turned_imag, real)
    return tuple(part.reshape(rows // sets, lanes) for part in found)


def outer_kernel(bins, sets, scale, *refs):
    out_ref, right, left, slots, sems = refs[-5:]
    count = (len(refs) - 5) // 2
    own_refs, other_refs = refs[:count], refs[count:-5]
    half = LANES // 2
    channels = out_ref.shape[2]
    full = channels // LANES
    step = pl.program_id(1)
    now = pl.program_id(0) * bins + step
    steps = pl.num_programs(0) * bins
    depth_of_slots, cuts = sems.shape[:2]
    size = channels // cuts

    def copy(when, cut, part):
        slot = lax.rem(when, depth_of_slots)
        at = pl.ds(cut * size, size)
        return pltpu.make_async_copy(
            slots.at[slot, part, at], out_ref.at[part, when, at], sems.at[slot, cut, part]
        )

    def wait_for(when):
        for cut in range(cuts):
            for part in range(2):
                copy(when, cut, part).wait()

    def prepare(q):
        me = lax.axis_index("chan")
        which = pl.program_id(0)
        own = jnp.concatenate([ref[which].astype(jnp.float32) for ref in own_refs])
        other = jnp.concatenate([ref[which].astype(jnp.float32) for ref in other_refs])
        rows = own.shape[0]
        block0 = jnp.where(me == 0, own, other)
        block1 = jnp.where(me == 0, other, own)
        low = lax.broadcasted_iota(jnp.int32, (rows, LANES), 1) < half

        def tiles_of(block, w):
            tiles = [
                block[:, (2 * j + w) * LANES : (2 * j + w + 1) * LANES] for j in range(full)
            ]
            last = block[:, 2 * full * LANES :]
            turned = swap_halves(last)
            both = jnp.where(low, last, turned) if w == 0 else jnp.where(low, turned, last)
            return tiles, both

        share = rows // sets
        for w in range(2):
            at = pl.ds(w * share, share)
            tiles, last0 = tiles_of(block0, w)
            tiles1, last1 = tiles_of(block1, w)
            turned = [swap_halves(tile) for tile in tiles1]
            chain = [last0] + turned + [last1]
            tiles = tiles + [
                jnp.where(low, chain[j], chain[j + 1]) for j in range(len(chain) - 1)
            ]
            for j, tile in enumerate(tiles):
                lanes = slice(j * LANES, (j + 1) * LANES)
                lanes_imag = slice(2 * channels + j * LANES, 2 * channels + (j + 1) * LANES)
                plain, rotated = rows_of_set(tile, bins, sets, q)
                right[q, at, lanes] = plain.astype(jnp.bfloat16)
                right[q, at, lanes_imag] = rotated.astype(jnp.bfloat16)
        scaled = own * scale
        for j in range(full + 1):
            block = scaled[:, 2 * j * LANES : (2 * j + 2) * LANES]
            if j < full:
                windows = [block[:, :LANES], block[:, LANES:]]
            else:
                windows = [block, swap_halves(block)]
            kept = min(LANES, channels - j * LANES)
            pieces = [rows_of_set(window, bins, sets, q)[0] for window in windows]
            left[q, j * LANES : j * LANES + kept] = jnp.concatenate(pieces).T[:kept]

    for q in range(sets):
        pl.when(step == q * (bins // sets))(functools.partial(prepare, q))

    depth = left.shape[2]
    within = bins // sets
    lane = lax.broadcasted_iota(jnp.int32, (1, depth), 1)
    taken = (lane & (within - 1)) == (step & (within - 1))
    chosen = jnp.where(taken, left[step // within], 0.0).astype(jnp.bfloat16)
    weights = right.at[step // within]

    @pl.when(now >= depth_of_slots)
    def _():
        wait_for(now - depth_of_slots)

    slot = lax.rem(now, depth_of_slots)

    whole = 2 * channels // (2 * LANES) * (2 * LANES)
    starts = [0, whole, 4 * channels - whole, 4 * channels]
    left_over = 2 * channels - whole

    def multiply(first, last):
        return jnp.dot(
            chosen, weights[:, first:last], preferred_element_type=jnp.float32
        ).astype(jnp.bfloat16)

    def send(part):
        for cut in range(cuts):
            copy(now, cut, part).start(priority=cut)

    slots[slot, 0, :, :whole] = multiply(*starts[:2])
    if left_over:
        both = multiply(*starts[1:3])
        slots[slot, 0, :, whole:] = both[:, :left_over]
        slots[slot, 1, :, :left_over] = both[:, left_over:]
    send(0)
    slots[slot, 1, :, left_over:] = multiply(*starts[2:])
    send(1)

    @pl.when(now == steps - 1)
    def _():
        for back in reversed(range(depth_of_slots)):
            wait_for(now - back)


def copy_kernel(in_ref, out_ref):
    out_ref[...] = in_ref[...]


def exchange(value, mask):
    pairs = [(source, source ^ mask) for source in range(lax.axis_size("freq"))]
    return lax.ppermute(value, "freq", pairs) if mask else value


def swap(value):
    return lax.ppermute(value, "chan", [(0, 1), (1, 0)])


def local(samples):
    local_channels, local_windows, length = samples.shape
    devices = lax.axis_size("freq")
    local_bins = BINS // devices
    windows = local_windows * devices
    bins = min(local_bins, 128 // (2 * devices))
    groups = local_bins // bins
    aligned = bins == 8
    group = bins if aligned else BINS
    table = jnp.asarray(bin_table(length, BINS, group))
    lanes = local_windows * local_channels
    vmem = pl.BlockSpec(memory_space=pltpu.VMEM)
    memory = pl.BlockSpec(memory_space=pl.ANY)
    masks = [devices - 1, 1, 2, *range(devices - 2, 2, -1), 0] if aligned else [0]
    pieces = len(masks)
    rows = (devices, groups, 2 * bins, lanes) if aligned else (2 * BINS, lanes)
    piece = rows[1:] if aligned else rows
    with jax.named_scope("table"):
        table = pl.pallas_call(
            copy_kernel,
            out_shape=jax.ShapeDtypeStruct(table.shape, table.dtype),
            in_specs=[vmem],
            out_specs=vmem,
            compiler_params=pltpu.CompilerParams(vmem_limit_bytes=8 * MIB),
        )(table)
    spectrum = jnp.einsum("cws,sj->wcj", samples, table, preferred_element_type=jnp.float32)
    spectrum = spectrum.astype(jnp.bfloat16)
    with jax.named_scope("whiten"):
        whitened = pl.pallas_call(
            functools.partial(whiten_kernel, group, masks),
            out_shape=[jax.ShapeDtypeStruct(piece, jnp.bfloat16)] * pieces,
            in_specs=[vmem],
            out_specs=[vmem] * pieces,
            scratch_shapes=[pltpu.VMEM(rows, jnp.bfloat16)],
            compiler_params=pltpu.CompilerParams(vmem_limit_bytes=16 * MIB),
            cost_estimate=pl.CostEstimate(
                flops=40 * BINS * lanes, bytes_accessed=12 * BINS * lanes, transcendentals=BINS * lanes
            ),
        )(spectrum)
    if aligned:
        own = [exchange(value, mask) for mask, value in zip(masks, whitened)]
    else:
        rows = whitened[0].reshape(2, devices, groups, bins, lanes).transpose(1, 2, 0, 3, 4)
        rows = rows.reshape(devices, groups, 2 * bins, lanes)
        rows = lax.all_to_all(rows, "freq", split_axis=0, concat_axis=0, tiled=True)
        own = [rows.transpose(1, 0, 2, 3).reshape(groups, devices * 2 * bins, lanes)]
    other = [swap(value) for value in own]
    sets = 2 if aligned else 1
    depth = local_windows * devices * 2 * bins // sets
    with jax.named_scope("outer_products"):
        out = pl.pallas_call(
            functools.partial(outer_kernel, bins, sets, 1.0 / windows),
            out_shape=jax.ShapeDtypeStruct(
                (2, local_bins, local_channels, 2 * local_channels), jnp.bfloat16
            ),
            grid=(groups, bins),
            in_specs=[vmem] * (2 * pieces),
            out_specs=memory,
            scratch_shapes=[
                pltpu.VMEM((sets, depth, 4 * local_channels), jnp.bfloat16),
                pltpu.VMEM((sets, local_channels, depth), jnp.float32),
                pltpu.VMEM((3, 2, local_channels, 2 * local_channels), jnp.bfloat16),
                pltpu.SemaphoreType.DMA((3, 2, 2)),
            ],
            compiler_params=pltpu.CompilerParams(vmem_limit_bytes=32 * MIB),
            cost_estimate=pl.CostEstimate(
                flops=8 * local_bins * depth * local_channels * local_channels,
                bytes_accessed=8 * local_bins * local_channels * local_channels,
                transcendentals=0,
            ),
        )(*own, *other)
    return jnp.transpose(out, (0, 1, 3, 2))


def solution(mesh):
    placed = (P("chan", ("hours", "freq"), None),)
    return jax.shard_map(
        local,
        mesh=mesh,
        in_specs=placed,
        out_specs=P(None, ("hours", "freq"), None, "chan"),
        check_vma=False,
    )
```

```python
import functools
import math

import jax
import jax.numpy as jnp
import ml_dtypes
import numpy as np
from jax import lax
from jax.experimental import pallas as pl
from jax.experimental.pallas import tpu as pltpu
from jax.sharding import PartitionSpec as P

BINS = 128
LANES = 128
MIB = 1024 * 1024


def bin_table(length, bins, group):
    position = np.arange(length)[None, :]
    number = np.arange(1, bins + 1)[:, None]
    phase = (position * number % length).astype(np.float32) * np.float32(2.0 * math.pi / length)
    taper = np.float32(0.5) - np.float32(0.5) * np.cos(
        position.astype(np.float32) * np.float32(2.0 * math.pi / length)
    )
    factor = np.float32(math.sqrt(8.0 / (3.0 * length)))
    table = np.stack([taper * np.cos(phase), -(taper * np.sin(phase))]) * factor
    table = table.reshape(2, bins // group, group, length).transpose(3, 1, 0, 2)
    return table.reshape(length, 2 * bins).astype(ml_dtypes.bfloat16)


def channel_blocks(channels):
    return [
        (first, min(LANES, channels - first), 2 * first) for first in range(0, channels, LANES)
    ]


def whiten_kernel(group, masks, spectrum_ref, *refs):
    pieces, rows_ref = refs[:-1], refs[-1]
    windows, channels, columns = spectrum_ref.shape
    bins = columns // 2
    row = lax.broadcasted_iota(jnp.int32, (bins, 1), 0)
    count = jnp.minimum(row + 2, bins - 1) - jnp.maximum(row - 2, 0) + 1
    share = 1.0 / count.astype(jnp.float32)

    for first, width, lane in channel_blocks(channels):
        blocks = [
            spectrum_ref[w, first : first + width, :].astype(jnp.float32).T
            for w in range(windows)
        ]
        spectrum = jnp.concatenate(blocks, axis=1)
        cols = windows * width
        parts = spectrum.reshape(bins // group, 2, group, cols)
        power = (parts[:, 0] * parts[:, 0] + parts[:, 1] * parts[:, 1]).reshape(bins, cols)
        summed = power
        for step in (1, 2):
            summed = summed + jnp.where(row >= step, pltpu.roll(power, step, axis=0), 0.0)
            summed = summed + jnp.where(
                row < bins - step, pltpu.roll(power, bins - step, axis=0), 0.0
            )
        level = jnp.maximum(summed * share, 0.1)
        inverse = lax.rsqrt(level).reshape(bins // group, 1, group, cols)
        whitened = (parts * inverse).astype(jnp.bfloat16)
        rows_ref[..., lane : lane + cols] = whitened.reshape(rows_ref.shape[:-1] + (cols,))

    if len(pieces) == 1:
        pieces[0][...] = rows_ref[...]
    else:
        me = lax.axis_index("freq")
        for mask, piece in zip(masks, pieces):
            piece[...] = rows_ref[me ^ mask]


def swap_halves(tile):
    return pltpu.roll(tile, LANES // 2, axis=1)


def rows_of_set(tile, bins, sets, q):
    rows, lanes = tile.shape
    if sets == 1:
        first_part = (lax.broadcasted_iota(jnp.int32, (rows, 1), 0) // bins) % 2 == 0
        rotated = jnp.where(
            first_part, -pltpu.roll(tile, rows - bins, axis=0), pltpu.roll(tile, bins, axis=0)
        )
        return tile, rotated
    parts = tile.reshape(rows // (2 * bins), 2, bins, lanes)
    real, imag = parts[:, 0], parts[:, 1]
    within = bins // sets
    low = lax.broadcasted_iota(jnp.int32, real.shape, 1) < within
    turned_real, turned_imag = (pltpu.roll(part, within, axis=1) for part in (real, imag))
    if q == 0:
        found = jnp.where(low, real, turned_imag), jnp.where(low, -imag, turned_real)
    else:
        found = jnp.where(low, turned_real, imag), jnp.where(low, -turned_imag, real)
    return tuple(part.reshape(rows // sets, lanes) for part in found)


def outer_kernel(bins, sets, scale, *refs):
    out_ref, right, left, slots, sems = refs[-5:]
    count = (len(refs) - 5) // 2
    own_refs, other_refs = refs[:count], refs[count:-5]
    half = LANES // 2
    channels = out_ref.shape[2]
    full = channels // LANES
    which, chosen_set = pl.program_id(0), pl.program_id(1)
    now = which * sets + chosen_set
    steps = pl.num_programs(0) * sets
    within = bins // sets
    cuts = sems.shape[2]
    size = channels // cuts

    def copy(when, bin_of_set, cut, part):
        side = lax.rem(when, 2)
        at = pl.ds(cut * size, size)
        return pltpu.make_async_copy(
            slots.at[side, bin_of_set, part, at],
            out_ref.at[part, when * within + bin_of_set, at],
            sems.at[side, bin_of_set, cut, part],
        )

    def wait_for(when):
        for bin_of_set in range(within):
            for cut in range(cuts):
                for part in range(2):
                    copy(when, bin_of_set, cut, part).wait()

    def prepare(q):
        me = lax.axis_index("chan")
        own = jnp.concatenate([ref[which].astype(jnp.float32) for ref in own_refs])
        other = jnp.concatenate([ref[which].astype(jnp.float32) for ref in other_refs])
        rows = own.shape[0]
        block0 = jnp.where(me == 0, own, other)
        block1 = jnp.where(me == 0, other, own)
        low = lax.broadcasted_iota(jnp.int32, (rows, LANES), 1) < half

        def tiles_of(block, w):
            tiles = [
                block[:, (2 * j + w) * LANES : (2 * j + w + 1) * LANES] for j in range(full)
            ]
            last = block[:, 2 * full * LANES :]
            turned = swap_halves(last)
            both = jnp.where(low, last, turned) if w == 0 else jnp.where(low, turned, last)
            return tiles, both

        share = rows // sets
        for w in range(2):
            at = pl.ds(w * share, share)
            tiles, last0 = tiles_of(block0, w)
            tiles1, last1 = tiles_of(block1, w)
            turned = [swap_halves(tile) for tile in tiles1]
            chain = [last0] + turned + [last1]
            tiles = tiles + [
                jnp.where(low, chain[j], chain[j + 1]) for j in range(len(chain) - 1)
            ]
            for j, tile in enumerate(tiles):
                lanes = slice(j * LANES, (j + 1) * LANES)
                lanes_imag = slice(2 * channels + j * LANES, 2 * channels + (j + 1) * LANES)
                plain, rotated = rows_of_set(tile, bins, sets, q)
                right[q, at, lanes] = plain.astype(jnp.bfloat16)
                right[q, at, lanes_imag] = rotated.astype(jnp.bfloat16)
        scaled = own * scale
        for j in range(full + 1):
            block = scaled[:, 2 * j * LANES : (2 * j + 2) * LANES]
            if j < full:
                windows = [block[:, :LANES], block[:, LANES:]]
            else:
                windows = [block, swap_halves(block)]
            kept = min(LANES, channels - j * LANES)
            pieces = [rows_of_set(window, bins, sets, q)[0] for window in windows]
            left[q, j * LANES : j * LANES + kept] = jnp.concatenate(pieces).T[:kept]

    for q in range(sets):
        pl.when(chosen_set == q)(functools.partial(prepare, q))

    @pl.when(now >= 2)
    def _():
        wait_for(now - 2)

    depth = left.shape[2]
    lane = lax.broadcasted_iota(jnp.int32, (1, depth), 1) & (within - 1)
    weights = right.at[chosen_set]
    side = lax.rem(now, 2)
    whole = 2 * channels // (2 * LANES) * (2 * LANES)
    starts = [0, whole, 4 * channels - whole, 4 * channels]
    left_over = 2 * channels - whole

    for k in range(within):
        chosen = jnp.where(lane == k, left[chosen_set], 0.0).astype(jnp.bfloat16)

        def multiply(first, last):
            return jnp.dot(
                chosen, weights[:, first:last], preferred_element_type=jnp.float32
            ).astype(jnp.bfloat16)

        def send(part):
            for cut in range(cuts):
                copy(now, k, cut, part).start()

        slots[side, k, 0, :, :whole] = multiply(*starts[:2])
        if left_over:
            both = multiply(*starts[1:3])
            slots[side, k, 0, :, whole:] = both[:, :left_over]
            slots[side, k, 1, :, :left_over] = both[:, left_over:]
        send(0)
        slots[side, k, 1, :, left_over:] = multiply(*starts[2:])
        send(1)

    @pl.when(now == steps - 1)
    def _():
        wait_for(now - 1)
        wait_for(now)


def copy_kernel(in_ref, out_ref):
    out_ref[...] = in_ref[...]


def exchange(value, mask):
    pairs = [(source, source ^ mask) for source in range(lax.axis_size("freq"))]
    return lax.ppermute(value, "freq", pairs) if mask else value


def swap(value):
    return lax.ppermute(value, "chan", [(0, 1), (1, 0)])


def local(samples):
    local_channels, local_windows, length = samples.shape
    devices = lax.axis_size("freq")
    local_bins = BINS // devices
    windows = local_windows * devices
    bins = min(local_bins, 128 // (2 * devices))
    groups = local_bins // bins
    aligned = bins == 8
    group = bins if aligned else BINS
    table = jnp.asarray(bin_table(length, BINS, group))
    lanes = local_windows * local_channels
    vmem = pl.BlockSpec(memory_space=pltpu.VMEM)
    memory = pl.BlockSpec(memory_space=pl.ANY)
    masks = [devices - 1, 1, 2, *range(devices - 2, 2, -1), 0] if aligned else [0]
    pieces = len(masks)
    rows = (devices, groups, 2 * bins, lanes) if aligned else (2 * BINS, lanes)
    piece = rows[1:] if aligned else rows
    with jax.named_scope("table"):
        table = pl.pallas_call(
            copy_kernel,
            out_shape=jax.ShapeDtypeStruct(table.shape, table.dtype),
            in_specs=[vmem],
            out_specs=vmem,
            compiler_params=pltpu.CompilerParams(vmem_limit_bytes=8 * MIB),
        )(table)
    spectrum = jnp.einsum("cws,sj->wcj", samples, table, preferred_element_type=jnp.float32)
    spectrum = spectrum.astype(jnp.bfloat16)
    with jax.named_scope("whiten"):
        whitened = pl.pallas_call(
            functools.partial(whiten_kernel, group, masks),
            out_shape=[jax.ShapeDtypeStruct(piece, jnp.bfloat16)] * pieces,
            in_specs=[vmem],
            out_specs=[vmem] * pieces,
            scratch_shapes=[pltpu.VMEM(rows, jnp.bfloat16)],
            compiler_params=pltpu.CompilerParams(vmem_limit_bytes=16 * MIB),
            cost_estimate=pl.CostEstimate(
                flops=40 * BINS * lanes, bytes_accessed=12 * BINS * lanes, transcendentals=BINS * lanes
            ),
        )(spectrum)
    if aligned:
        own = [exchange(value, mask) for mask, value in zip(masks, whitened)]
    else:
        rows = whitened[0].reshape(2, devices, groups, bins, lanes).transpose(1, 2, 0, 3, 4)
        rows = rows.reshape(devices, groups, 2 * bins, lanes)
        rows = lax.all_to_all(rows, "freq", split_axis=0, concat_axis=0, tiled=True)
        own = [rows.transpose(1, 0, 2, 3).reshape(groups, devices * 2 * bins, lanes)]
    other = [swap(value) for value in own]
    sets = 2 if aligned else 1
    depth = local_windows * devices * 2 * bins // sets
    with jax.named_scope("outer_products"):
        out = pl.pallas_call(
            functools.partial(outer_kernel, bins, sets, 1.0 / windows),
            out_shape=jax.ShapeDtypeStruct(
                (2, local_bins, local_channels, 2 * local_channels), jnp.bfloat16
            ),
            grid=(groups, sets),
            in_specs=[vmem] * (2 * pieces),
            out_specs=memory,
            scratch_shapes=[
                pltpu.VMEM((sets, depth, 4 * local_channels), jnp.bfloat16),
                pltpu.VMEM((sets, local_channels, depth), jnp.float32),
                pltpu.VMEM((2, bins // sets, 2, local_channels, 2 * local_channels), jnp.bfloat16),
                pltpu.SemaphoreType.DMA((2, bins // sets, 2, 2)),
            ],
            compiler_params=pltpu.CompilerParams(vmem_limit_bytes=48 * MIB),
            cost_estimate=pl.CostEstimate(
                flops=8 * local_bins * depth * local_channels * local_channels,
                bytes_accessed=8 * local_bins * local_channels * local_channels,
                transcendentals=0,
            ),
        )(*own, *other)
    return jnp.transpose(out, (0, 1, 3, 2))


def solution(mesh):
    placed = (P("chan", ("hours", "freq"), None),)
    return jax.shard_map(
        local,
        mesh=mesh,
        in_specs=placed,
        out_specs=P(None, ("hours", "freq"), None, "chan"),
        check_vma=False,
    )
```

```python
import functools
import math

import jax
import jax.numpy as jnp
import ml_dtypes
import numpy as np
from jax import lax
from jax.experimental import pallas as pl
from jax.experimental.pallas import tpu as pltpu
from jax.sharding import PartitionSpec as P

BINS = 128
LANES = 128
MIB = 1024 * 1024


def bin_table(length, bins, group):
    position = np.arange(length)[None, :]
    number = np.arange(1, bins + 1)[:, None]
    phase = (position * number % length).astype(np.float32) * np.float32(2.0 * math.pi / length)
    taper = np.float32(0.5) - np.float32(0.5) * np.cos(
        position.astype(np.float32) * np.float32(2.0 * math.pi / length)
    )
    factor = np.float32(math.sqrt(8.0 / (3.0 * length)))
    table = np.stack([taper * np.cos(phase), -(taper * np.sin(phase))]) * factor
    table = table.reshape(2, bins // group, group, length).transpose(3, 1, 0, 2)
    return table.reshape(length, 2 * bins).astype(ml_dtypes.bfloat16)


def channel_blocks(channels):
    return [
        (first, min(LANES, channels - first), 2 * first) for first in range(0, channels, LANES)
    ]


def whiten_kernel(group, masks, spectrum_ref, *refs):
    pieces, rows_ref = refs[:-1], refs[-1]
    windows, channels, columns = spectrum_ref.shape
    bins = columns // 2
    row = lax.broadcasted_iota(jnp.int32, (bins, 1), 0)
    count = jnp.minimum(row + 2, bins - 1) - jnp.maximum(row - 2, 0) + 1
    share = 1.0 / count.astype(jnp.float32)

    for first, width, lane in channel_blocks(channels):
        blocks = [
            spectrum_ref[w, first : first + width, :].astype(jnp.float32).T
            for w in range(windows)
        ]
        spectrum = jnp.concatenate(blocks, axis=1)
        cols = windows * width
        parts = spectrum.reshape(bins // group, 2, group, cols)
        power = (parts[:, 0] * parts[:, 0] + parts[:, 1] * parts[:, 1]).reshape(bins, cols)
        summed = power
        for step in (1, 2):
            summed = summed + jnp.where(row >= step, pltpu.roll(power, step, axis=0), 0.0)
            summed = summed + jnp.where(
                row < bins - step, pltpu.roll(power, bins - step, axis=0), 0.0
            )
        level = jnp.maximum(summed * share, 0.1)
        inverse = lax.rsqrt(level).reshape(bins // group, 1, group, cols)
        whitened = (parts * inverse).astype(jnp.bfloat16)
        rows_ref[..., lane : lane + cols] = whitened.reshape(rows_ref.shape[:-1] + (cols,))

    if len(pieces) == 1:
        pieces[0][...] = rows_ref[...]
    else:
        me = lax.axis_index("freq")
        for mask, piece in zip(masks, pieces):
            piece[...] = rows_ref[me ^ mask]


def swap_halves(tile):
    return pltpu.roll(tile, LANES // 2, axis=1)


def rows_of_set(tile, bins, sets, q):
    if sets == 1:
        return tile
    rows, lanes = tile.shape
    parts = tile.reshape(rows // (2 * bins), 2, bins, lanes)
    real, imag = parts[:, 0], parts[:, 1]
    within = bins // sets
    low = lax.broadcasted_iota(jnp.int32, real.shape, 1) < within
    if q == 0:
        found = jnp.where(low, real, pltpu.roll(imag, within, axis=1))
    else:
        found = jnp.where(low, pltpu.roll(real, within, axis=1), imag)
    return found.reshape(rows // sets, lanes)


def rotate(tile, within):
    rows, lanes = tile.shape
    if 2 * within == 8:
        pairs = tile.reshape(rows // 8, 8, lanes)
        low = lax.broadcasted_iota(jnp.int32, pairs.shape, 1) < within
        turned = pltpu.roll(pairs, within, axis=1)
        return jnp.where(low, -turned, turned).reshape(rows, lanes)
    first_part = (lax.broadcasted_iota(jnp.int32, (rows, 1), 0) // within) % 2 == 0
    return jnp.where(
        first_part, -pltpu.roll(tile, rows - within, axis=0), pltpu.roll(tile, within, axis=0)
    )


def outer_kernel(bins, sets, scale, *refs):
    out_ref, right, left, slots, sems = refs[-5:]
    count = (len(refs) - 5) // 2
    own_refs, other_refs = refs[:count], refs[count:-5]
    half = LANES // 2
    channels = out_ref.shape[2]
    full = channels // LANES
    which = pl.program_id(0)
    within = bins // sets
    cuts = sems.shape[2]
    size = channels // cuts

    def copy(group, q, k, cut, part):
        at = pl.ds(cut * size, size)
        return pltpu.make_async_copy(
            slots.at[q, k, part, at],
            out_ref.at[part, group * bins + q * within + k, at],
            sems.at[q, k, cut, part],
        )

    def wait_for(group, q):
        for k in range(within):
            for cut in range(cuts):
                for part in range(2):
                    copy(group, q, k, cut, part).wait()

    def prepare(q):
        me = lax.axis_index("chan")
        own = jnp.concatenate([ref[which].astype(jnp.float32) for ref in own_refs])
        other = jnp.concatenate([ref[which].astype(jnp.float32) for ref in other_refs])
        rows = own.shape[0]
        block0 = jnp.where(me == 0, own, other)
        block1 = jnp.where(me == 0, other, own)
        low = lax.broadcasted_iota(jnp.int32, (rows, LANES), 1) < half

        def tiles_of(block, w):
            tiles = [
                block[:, (2 * j + w) * LANES : (2 * j + w + 1) * LANES] for j in range(full)
            ]
            last = block[:, 2 * full * LANES :]
            turned = swap_halves(last)
            both = jnp.where(low, last, turned) if w == 0 else jnp.where(low, turned, last)
            return tiles, both

        share = rows // sets
        for w in range(2):
            at = pl.ds(w * share, share)
            tiles, last0 = tiles_of(block0, w)
            tiles1, last1 = tiles_of(block1, w)
            turned = [swap_halves(tile) for tile in tiles1]
            chain = [last0] + turned + [last1]
            tiles = tiles + [
                jnp.where(low, chain[j], chain[j + 1]) for j in range(len(chain) - 1)
            ]
            for j, tile in enumerate(tiles):
                lanes = slice(j * LANES, (j + 1) * LANES)
                right[q, at, lanes] = rows_of_set(tile, bins, sets, q).astype(jnp.bfloat16)
        scaled = own * scale
        for j in range(full + 1):
            block = scaled[:, 2 * j * LANES : (2 * j + 2) * LANES]
            if j < full:
                windows = [block[:, :LANES], block[:, LANES:]]
            else:
                windows = [block, swap_halves(block)]
            kept = min(LANES, channels - j * LANES)
            pieces = [rows_of_set(window, bins, sets, q) for window in windows]
            left[q, j * LANES : j * LANES + kept] = jnp.concatenate(pieces).T[:kept]

    def prepare_rotated(q, first, last):
        for lane in range(first, last, LANES):
            plain = right[q, :, lane : lane + LANES].astype(jnp.float32)
            at = slice(2 * channels + lane, 2 * channels + lane + LANES)
            right[q, :, at] = rotate(plain, within).astype(jnp.bfloat16)

    depth = left.shape[2]
    lane = lax.broadcasted_iota(jnp.int32, (1, depth), 1) & (within - 1)
    whole = 2 * channels // (2 * LANES) * (2 * LANES)
    starts = [0, whole, 4 * channels - whole, 4 * channels]
    left_over = 2 * channels - whole

    for q in range(sets):
        pl.when(which >= 1)(functools.partial(wait_for, which - 1, q))
        prepare(q)
        prepare_rotated(q, 0, left_over)
        for k in range(within):
            chosen = jnp.where(lane == k, left[q], 0.0).astype(jnp.bfloat16)

            def multiply(first, last):
                return jnp.dot(
                    chosen, right[q, :, first:last], preferred_element_type=jnp.float32
                ).astype(jnp.bfloat16)

            def send(part):
                for cut in range(cuts):
                    copy(which, q, k, cut, part).start()

            slots[q, k, 0, :, :whole] = multiply(*starts[:2])
            if left_over:
                both = multiply(*starts[1:3])
                slots[q, k, 0, :, whole:] = both[:, :left_over]
                slots[q, k, 1, :, :left_over] = both[:, left_over:]
            send(0)
            if k == 0:
                prepare_rotated(q, left_over, 2 * channels)
            slots[q, k, 1, :, left_over:] = multiply(*starts[2:])
            send(1)

    @pl.when(which == pl.num_programs(0) - 1)
    def _():
        for q in range(sets):
            wait_for(which, q)


def copy_kernel(in_ref, out_ref):
    out_ref[...] = in_ref[...]


def exchange(value, mask):
    pairs = [(source, source ^ mask) for source in range(lax.axis_size("freq"))]
    return lax.ppermute(value, "freq", pairs) if mask else value


def swap(value):
    return lax.ppermute(value, "chan", [(0, 1), (1, 0)])


def local(samples):
    local_channels, local_windows, length = samples.shape
    devices = lax.axis_size("freq")
    local_bins = BINS // devices
    windows = local_windows * devices
    bins = min(local_bins, 128 // (2 * devices))
    groups = local_bins // bins
    aligned = bins == 8
    group = bins if aligned else BINS
    table = jnp.asarray(bin_table(length, BINS, group))
    lanes = local_windows * local_channels
    vmem = pl.BlockSpec(memory_space=pltpu.VMEM)
    memory = pl.BlockSpec(memory_space=pl.ANY)
    masks = [devices - 1, 1, 2, 3, *range(devices - 2, 3, -1), 0] if aligned else [0]
    pieces = len(masks)
    rows = (devices, groups, 2 * bins, lanes) if aligned else (2 * BINS, lanes)
    piece = rows[1:] if aligned else rows
    with jax.named_scope("table"):
        table = pl.pallas_call(
            copy_kernel,
            out_shape=jax.ShapeDtypeStruct(table.shape, table.dtype),
            in_specs=[vmem],
            out_specs=vmem,
            compiler_params=pltpu.CompilerParams(vmem_limit_bytes=8 * MIB),
        )(table)
    spectrum = jnp.einsum("cws,sj->wcj", samples, table, preferred_element_type=jnp.float32)
    spectrum = spectrum.astype(jnp.bfloat16)
    with jax.named_scope("whiten"):
        whitened = pl.pallas_call(
            functools.partial(whiten_kernel, group, masks),
            out_shape=[jax.ShapeDtypeStruct(piece, jnp.bfloat16)] * pieces,
            in_specs=[vmem],
            out_specs=[vmem] * pieces,
            scratch_shapes=[pltpu.VMEM(rows, jnp.bfloat16)],
            compiler_params=pltpu.CompilerParams(vmem_limit_bytes=16 * MIB),
            cost_estimate=pl.CostEstimate(
                flops=40 * BINS * lanes, bytes_accessed=12 * BINS * lanes, transcendentals=BINS * lanes
            ),
        )(spectrum)
    if aligned:
        own = [exchange(value, mask) for mask, value in zip(masks, whitened)]
    else:
        rows = whitened[0].reshape(2, devices, groups, bins, lanes).transpose(1, 2, 0, 3, 4)
        rows = rows.reshape(devices, groups, 2 * bins, lanes)
        rows = lax.all_to_all(rows, "freq", split_axis=0, concat_axis=0, tiled=True)
        own = [rows.transpose(1, 0, 2, 3).reshape(groups, devices * 2 * bins, lanes)]
    other = [swap(value) for value in own]
    sets = 2 if aligned else 1
    depth = local_windows * devices * 2 * bins // sets
    with jax.named_scope("outer_products"):
        out = pl.pallas_call(
            functools.partial(outer_kernel, bins, sets, 1.0 / windows),
            out_shape=jax.ShapeDtypeStruct(
                (2, local_bins, local_channels, 2 * local_channels), jnp.bfloat16
            ),
            grid=(groups,),
            in_specs=[vmem] * (2 * pieces),
            out_specs=memory,
            scratch_shapes=[
                pltpu.VMEM((sets, depth, 4 * local_channels), jnp.bfloat16),
                pltpu.VMEM((sets, local_channels, depth), jnp.float32),
                pltpu.VMEM((sets, bins // sets, 2, local_channels, 2 * local_channels), jnp.bfloat16),
                pltpu.SemaphoreType.DMA((sets, bins // sets, 2, 2)),
            ],
            compiler_params=pltpu.CompilerParams(vmem_limit_bytes=48 * MIB),
            cost_estimate=pl.CostEstimate(
                flops=8 * local_bins * depth * local_channels * local_channels,
                bytes_accessed=8 * local_bins * local_channels * local_channels,
                transcendentals=0,
            ),
        )(*own, *other)
    return jnp.transpose(out, (0, 1, 3, 2))


def solution(mesh):
    placed = (P("chan", ("hours", "freq"), None),)
    return jax.shard_map(
        local,
        mesh=mesh,
        in_specs=placed,
        out_specs=P(None, ("hours", "freq"), None, "chan"),
        check_vma=False,
    )
```

```python
import functools
import math

import jax
import jax.numpy as jnp
import ml_dtypes
import numpy as np
from jax import lax
from jax.experimental import pallas as pl
from jax.experimental.pallas import tpu as pltpu
from jax.sharding import PartitionSpec as P

BINS = 128
LANES = 128
MIB = 1024 * 1024


def bin_table(length, bins, group):
    position = np.arange(length)[None, :]
    number = np.arange(1, bins + 1)[:, None]
    phase = (position * number % length).astype(np.float32) * np.float32(2.0 * math.pi / length)
    taper = np.float32(0.5) - np.float32(0.5) * np.cos(
        position.astype(np.float32) * np.float32(2.0 * math.pi / length)
    )
    factor = np.float32(math.sqrt(8.0 / (3.0 * length)))
    table = np.stack([taper * np.cos(phase), -(taper * np.sin(phase))]) * factor
    table = table.reshape(2, bins // group, group, length).transpose(3, 1, 0, 2)
    return table.reshape(length, 2 * bins).astype(ml_dtypes.bfloat16)


def channel_blocks(channels):
    return [
        (first, min(LANES, channels - first), 2 * first) for first in range(0, channels, LANES)
    ]


def whiten_kernel(group, masks, spectrum_ref, *refs):
    pieces, rows_ref = refs[:-1], refs[-1]
    windows, channels, columns = spectrum_ref.shape
    bins = columns // 2
    row = lax.broadcasted_iota(jnp.int32, (bins, 1), 0)
    count = jnp.minimum(row + 2, bins - 1) - jnp.maximum(row - 2, 0) + 1
    share = 1.0 / count.astype(jnp.float32)

    for first, width, lane in channel_blocks(channels):
        blocks = [
            spectrum_ref[w, first : first + width, :].astype(jnp.float32).T
            for w in range(windows)
        ]
        spectrum = jnp.concatenate(blocks, axis=1)
        cols = windows * width
        parts = spectrum.reshape(bins // group, 2, group, cols)
        power = (parts[:, 0] * parts[:, 0] + parts[:, 1] * parts[:, 1]).reshape(bins, cols)
        summed = power
        for step in (1, 2):
            summed = summed + jnp.where(row >= step, pltpu.roll(power, step, axis=0), 0.0)
            summed = summed + jnp.where(
                row < bins - step, pltpu.roll(power, bins - step, axis=0), 0.0
            )
        level = jnp.maximum(summed * share, 0.1)
        inverse = lax.rsqrt(level).reshape(bins // group, 1, group, cols)
        whitened = (parts * inverse).astype(jnp.bfloat16)
        rows_ref[..., lane : lane + cols] = whitened.reshape(rows_ref.shape[:-1] + (cols,))

    if len(pieces) == 1:
        pieces[0][...] = rows_ref[...]
    else:
        me = lax.axis_index("freq")
        for mask, piece in zip(masks, pieces):
            piece[...] = rows_ref[me ^ mask]


def swap_halves(tile):
    return pltpu.roll(tile, LANES // 2, axis=1)


def rows_of_set(tile, bins, sets, q):
    if sets == 1:
        return tile
    rows, lanes = tile.shape
    parts = tile.reshape(rows // (2 * bins), 2, bins, lanes)
    real, imag = parts[:, 0], parts[:, 1]
    within = bins // sets
    low = lax.broadcasted_iota(jnp.int32, real.shape, 1) < within
    if q == 0:
        found = jnp.where(low, real, pltpu.roll(imag, within, axis=1))
    else:
        found = jnp.where(low, pltpu.roll(real, within, axis=1), imag)
    return found.reshape(rows // sets, lanes)


def rotate(tile, within):
    rows, lanes = tile.shape
    if 2 * within == 8:
        pairs = tile.reshape(rows // 8, 8, lanes)
        low = lax.broadcasted_iota(jnp.int32, pairs.shape, 1) < within
        turned = pltpu.roll(pairs, within, axis=1)
        return jnp.where(low, -turned, turned).reshape(rows, lanes)
    first_part = (lax.broadcasted_iota(jnp.int32, (rows, 1), 0) // within) % 2 == 0
    return jnp.where(
        first_part, -pltpu.roll(tile, rows - within, axis=0), pltpu.roll(tile, within, axis=0)
    )


def outer_kernel(bins, sets, scale, *refs):
    out_ref, right, left, slots, sems = refs[-5:]
    count = (len(refs) - 5) // 2
    own_refs, other_refs = refs[:count], refs[count:-5]
    half = LANES // 2
    channels = out_ref.shape[2]
    full = channels // LANES
    which = pl.program_id(0)
    within = bins // sets
    cuts = sems.shape[2]
    size = channels // cuts

    def copy(group, q, k, cut, part):
        at = pl.ds(cut * size, size)
        return pltpu.make_async_copy(
            slots.at[q, k, part, at],
            out_ref.at[part, group * bins + q * within + k, at],
            sems.at[q, k, cut, part],
        )

    def wait_for(group, q):
        for k in range(within):
            for cut in range(cuts):
                for part in range(2):
                    copy(group, q, k, cut, part).wait()

    def prepare(q):
        me = lax.axis_index("chan")
        own = jnp.concatenate([ref[which].astype(jnp.float32) for ref in own_refs])
        other = jnp.concatenate([ref[which].astype(jnp.float32) for ref in other_refs])
        rows = own.shape[0]
        block0 = jnp.where(me == 0, own, other)
        block1 = jnp.where(me == 0, other, own)
        low = lax.broadcasted_iota(jnp.int32, (rows, LANES), 1) < half

        def tiles_of(block, w):
            tiles = [
                block[:, (2 * j + w) * LANES : (2 * j + w + 1) * LANES] for j in range(full)
            ]
            last = block[:, 2 * full * LANES :]
            turned = swap_halves(last)
            both = jnp.where(low, last, turned) if w == 0 else jnp.where(low, turned, last)
            return tiles, both

        share = rows // sets
        for w in range(2):
            at = pl.ds(w * share, share)
            tiles, last0 = tiles_of(block0, w)
            tiles1, last1 = tiles_of(block1, w)
            turned = [swap_halves(tile) for tile in tiles1]
            chain = [last0] + turned + [last1]
            tiles = tiles + [
                jnp.where(low, chain[j], chain[j + 1]) for j in range(len(chain) - 1)
            ]
            for j, tile in enumerate(tiles):
                lanes = slice(j * LANES, (j + 1) * LANES)
                right[q, at, lanes] = rows_of_set(tile, bins, sets, q).astype(jnp.bfloat16)
        scaled = own * scale
        for j in range(full + 1):
            block = scaled[:, 2 * j * LANES : (2 * j + 2) * LANES]
            if j < full:
                windows = [block[:, :LANES], block[:, LANES:]]
            else:
                windows = [block, swap_halves(block)]
            kept = min(LANES, channels - j * LANES)
            pieces = [rows_of_set(window, bins, sets, q) for window in windows]
            left[q, j * LANES : j * LANES + kept] = jnp.concatenate(pieces).T[:kept]

    def prepare_rotated(q, first, last):
        for lane in range(first, last, LANES):
            plain = right[q, :, lane : lane + LANES].astype(jnp.float32)
            at = slice(2 * channels + lane, 2 * channels + lane + LANES)
            right[q, :, at] = rotate(plain, within).astype(jnp.bfloat16)

    depth = left.shape[2]
    lane = lax.broadcasted_iota(jnp.int32, (1, depth), 1) & (within - 1)
    whole = 2 * channels // (2 * LANES) * (2 * LANES)
    starts = [0, whole, 4 * channels - whole, 4 * channels]
    left_over = 2 * channels - whole

    for q in range(sets):
        pl.when(which >= 1)(functools.partial(wait_for, which - 1, q))
        prepare(q)
        prepare_rotated(q, 0, left_over)
        for k in range(within):
            chosen = jnp.where(lane == k, left[q], 0.0).astype(jnp.bfloat16)

            def multiply(first, last):
                return jnp.dot(
                    chosen, right[q, :, first:last], preferred_element_type=jnp.float32
                ).astype(jnp.bfloat16)

            def send(part):
                for cut in range(cuts):
                    copy(which, q, k, cut, part).start()

            slots[q, k, 0, :, :whole] = multiply(*starts[:2])
            if left_over:
                both = multiply(*starts[1:3])
                slots[q, k, 0, :, whole:] = both[:, :left_over]
                slots[q, k, 1, :, :left_over] = both[:, left_over:]
            send(0)
            if k == 0:
                prepare_rotated(q, left_over, 2 * channels)
            slots[q, k, 1, :, left_over:] = multiply(*starts[2:])
            send(1)

    @pl.when(which == pl.num_programs(0) - 1)
    def _():
        for q in range(sets):
            wait_for(which, q)


def copy_kernel(in_ref, out_ref):
    out_ref[...] = in_ref[...]


def exchange(value, mask):
    pairs = [(source, source ^ mask) for source in range(lax.axis_size("freq"))]
    return lax.ppermute(value, "freq", pairs) if mask else value


def swap(value):
    return lax.ppermute(value, "chan", [(0, 1), (1, 0)])


def local(samples):
    local_channels, local_windows, length = samples.shape
    devices = lax.axis_size("freq")
    local_bins = BINS // devices
    windows = local_windows * devices
    bins = min(local_bins, 128 // (2 * devices))
    groups = local_bins // bins
    aligned = bins == 8
    group = bins if aligned else BINS
    table = jnp.asarray(bin_table(length, BINS, group))
    lanes = local_windows * local_channels
    vmem = pl.BlockSpec(memory_space=pltpu.VMEM)
    memory = pl.BlockSpec(memory_space=pl.ANY)
    masks = [devices - 1, 1, 2, *range(devices - 2, 2, -1), 0] if aligned else [0]
    pieces = len(masks)
    rows = (devices, groups, 2 * bins, lanes) if aligned else (2 * BINS, lanes)
    piece = rows[1:] if aligned else rows
    with jax.named_scope("table"):
        table = pl.pallas_call(
            copy_kernel,
            out_shape=jax.ShapeDtypeStruct(table.shape, table.dtype),
            in_specs=[vmem],
            out_specs=vmem,
            compiler_params=pltpu.CompilerParams(vmem_limit_bytes=8 * MIB),
        )(table)
    spectrum = jnp.einsum("cws,sj->wcj", samples, table, preferred_element_type=jnp.float32)
    spectrum = spectrum.astype(jnp.bfloat16)
    with jax.named_scope("whiten"):
        whitened = pl.pallas_call(
            functools.partial(whiten_kernel, group, masks),
            out_shape=[jax.ShapeDtypeStruct(piece, jnp.bfloat16)] * pieces,
            in_specs=[vmem],
            out_specs=[vmem] * pieces,
            scratch_shapes=[pltpu.VMEM(rows, jnp.bfloat16)],
            compiler_params=pltpu.CompilerParams(vmem_limit_bytes=16 * MIB),
            cost_estimate=pl.CostEstimate(
                flops=40 * BINS * lanes, bytes_accessed=12 * BINS * lanes, transcendentals=BINS * lanes
            ),
        )(spectrum)
    if aligned:
        own = [exchange(value, mask) for mask, value in zip(masks, whitened)]
    else:
        rows = whitened[0].reshape(2, devices, groups, bins, lanes).transpose(1, 2, 0, 3, 4)
        rows = rows.reshape(devices, groups, 2 * bins, lanes)
        rows = lax.all_to_all(rows, "freq", split_axis=0, concat_axis=0, tiled=True)
        own = [rows.transpose(1, 0, 2, 3).reshape(groups, devices * 2 * bins, lanes)]
    other = [swap(value) for value in own]
    sets = 2 if aligned else 1
    depth = local_windows * devices * 2 * bins // sets
    with jax.named_scope("outer_products"):
        out = pl.pallas_call(
            functools.partial(outer_kernel, bins, sets, 1.0 / windows),
            out_shape=jax.ShapeDtypeStruct(
                (2, local_bins, local_channels, 2 * local_channels), jnp.bfloat16
            ),
            grid=(groups,),
            in_specs=[vmem] * (2 * pieces),
            out_specs=memory,
            scratch_shapes=[
                pltpu.VMEM((sets, depth, 4 * local_channels), jnp.bfloat16),
                pltpu.VMEM((sets, local_channels, depth), jnp.float32),
                pltpu.VMEM((sets, bins // sets, 2, local_channels, 2 * local_channels), jnp.bfloat16),
                pltpu.SemaphoreType.DMA((sets, bins // sets, 2, 2)),
            ],
            compiler_params=pltpu.CompilerParams(vmem_limit_bytes=48 * MIB),
            cost_estimate=pl.CostEstimate(
                flops=8 * local_bins * depth * local_channels * local_channels,
                bytes_accessed=8 * local_bins * local_channels * local_channels,
                transcendentals=0,
            ),
        )(*own, *other)
    return jnp.transpose(out, (0, 1, 3, 2))


def solution(mesh):
    placed = (P("chan", ("hours", "freq"), None),)
    return jax.shard_map(
        local,
        mesh=mesh,
        in_specs=placed,
        out_specs=P(None, ("hours", "freq"), None, "chan"),
        check_vma=False,
    )
```

```python
import functools
import math

import jax
import jax.numpy as jnp
import ml_dtypes
import numpy as np
from jax import lax
from jax.experimental import pallas as pl
from jax.experimental.pallas import tpu as pltpu
from jax.sharding import PartitionSpec as P

BINS = 128
LANES = 128
MIB = 1024 * 1024


def bin_table(length, bins, group):
    position = np.arange(length)[None, :]
    number = np.arange(1, bins + 1)[:, None]
    phase = (position * number % length).astype(np.float32) * np.float32(2.0 * math.pi / length)
    taper = np.float32(0.5) - np.float32(0.5) * np.cos(
        position.astype(np.float32) * np.float32(2.0 * math.pi / length)
    )
    factor = np.float32(math.sqrt(8.0 / (3.0 * length)))
    table = np.stack([taper * np.cos(phase), -(taper * np.sin(phase))]) * factor
    table = table.reshape(2, bins // group, group, length).transpose(3, 1, 0, 2)
    return table.reshape(length, 2 * bins).astype(ml_dtypes.bfloat16)


def channel_blocks(channels):
    return [
        (first, min(LANES, channels - first), 2 * first) for first in range(0, channels, LANES)
    ]


def whiten_kernel(group, masks, spectrum_ref, *refs):
    pieces, rows_ref = refs[:-1], refs[-1]
    windows, channels, columns = spectrum_ref.shape
    bins = columns // 2
    row = lax.broadcasted_iota(jnp.int32, (bins, 1), 0)
    count = jnp.minimum(row + 2, bins - 1) - jnp.maximum(row - 2, 0) + 1
    share = 1.0 / count.astype(jnp.float32)

    for first, width, lane in channel_blocks(channels):
        blocks = [
            spectrum_ref[w, first : first + width, :].astype(jnp.float32).T
            for w in range(windows)
        ]
        spectrum = jnp.concatenate(blocks, axis=1)
        cols = windows * width
        parts = spectrum.reshape(bins // group, 2, group, cols)
        power = (parts[:, 0] * parts[:, 0] + parts[:, 1] * parts[:, 1]).reshape(bins, cols)
        summed = power
        for step in (1, 2):
            summed = summed + jnp.where(row >= step, pltpu.roll(power, step, axis=0), 0.0)
            summed = summed + jnp.where(
                row < bins - step, pltpu.roll(power, bins - step, axis=0), 0.0
            )
        level = jnp.maximum(summed * share, 0.1)
        inverse = lax.rsqrt(level).reshape(bins // group, 1, group, cols)
        whitened = (parts * inverse).astype(jnp.bfloat16)
        rows_ref[..., lane : lane + cols] = whitened.reshape(rows_ref.shape[:-1] + (cols,))

    if len(pieces) == 1:
        pieces[0][...] = rows_ref[...]
    else:
        me = lax.axis_index("freq")
        for mask, piece in zip(masks, pieces):
            piece[...] = rows_ref[me ^ mask]


def swap_halves(tile):
    return pltpu.roll(tile, LANES // 2, axis=1)


def rows_of_set(tile, bins, sets, q):
    if sets == 1:
        return tile
    rows, lanes = tile.shape
    parts = tile.reshape(rows // (2 * bins), 2, bins, lanes)
    real, imag = parts[:, 0], parts[:, 1]
    within = bins // sets
    low = lax.broadcasted_iota(jnp.int32, real.shape, 1) < within
    if q == 0:
        found = jnp.where(low, real, pltpu.roll(imag, within, axis=1))
    else:
        found = jnp.where(low, pltpu.roll(real, within, axis=1), imag)
    return found.reshape(rows // sets, lanes)


def rotate(tile, within):
    rows, lanes = tile.shape
    if 2 * within == 8:
        pairs = tile.reshape(rows // 8, 8, lanes)
        low = lax.broadcasted_iota(jnp.int32, pairs.shape, 1) < within
        turned = pltpu.roll(pairs, within, axis=1)
        return jnp.where(low, -turned, turned).reshape(rows, lanes)
    first_part = (lax.broadcasted_iota(jnp.int32, (rows, 1), 0) // within) % 2 == 0
    return jnp.where(
        first_part, -pltpu.roll(tile, rows - within, axis=0), pltpu.roll(tile, within, axis=0)
    )


def outer_kernel(bins, sets, scale, *refs):
    out_ref, right, left, slots, sems = refs[-5:]
    count = (len(refs) - 5) // 2
    own_refs, other_refs = refs[:count], refs[count:-5]
    half = LANES // 2
    channels = out_ref.shape[2]
    full = channels // LANES
    which = pl.program_id(0)
    within = bins // sets
    cuts = sems.shape[2]
    size = channels // cuts

    def copy(group, q, k, cut, part):
        at = pl.ds(cut * size, size)
        return pltpu.make_async_copy(
            slots.at[q, k, part, at],
            out_ref.at[part, group * bins + q * within + k, at],
            sems.at[q, k, cut, part],
        )

    def wait_for(group, q):
        for k in range(within):
            for cut in range(cuts):
                for part in range(2):
                    copy(group, q, k, cut, part).wait()

    def prepare(q):
        me = lax.axis_index("chan")
        own = jnp.concatenate([ref[which].astype(jnp.float32) for ref in own_refs])
        other = jnp.concatenate([ref[which].astype(jnp.float32) for ref in other_refs])
        rows = own.shape[0]
        block0 = jnp.where(me == 0, own, other)
        block1 = jnp.where(me == 0, other, own)
        low = lax.broadcasted_iota(jnp.int32, (rows, LANES), 1) < half

        def tiles_of(block, w):
            tiles = [
                block[:, (2 * j + w) * LANES : (2 * j + w + 1) * LANES] for j in range(full)
            ]
            last = block[:, 2 * full * LANES :]
            turned = swap_halves(last)
            both = jnp.where(low, last, turned) if w == 0 else jnp.where(low, turned, last)
            return tiles, both

        share = rows // sets
        for w in range(2):
            at = pl.ds(w * share, share)
            tiles, last0 = tiles_of(block0, w)
            tiles1, last1 = tiles_of(block1, w)
            turned = [swap_halves(tile) for tile in tiles1]
            chain = [last0] + turned + [last1]
            tiles = tiles + [
                jnp.where(low, chain[j], chain[j + 1]) for j in range(len(chain) - 1)
            ]
            for j, tile in enumerate(tiles):
                lanes = slice(j * LANES, (j + 1) * LANES)
                right[q, at, lanes] = rows_of_set(tile, bins, sets, q).astype(jnp.bfloat16)
        scaled = own * scale
        for j in range(full + 1):
            block = scaled[:, 2 * j * LANES : (2 * j + 2) * LANES]
            if j < full:
                windows = [block[:, :LANES], block[:, LANES:]]
            else:
                windows = [block, swap_halves(block)]
            kept = min(LANES, channels - j * LANES)
            pieces = [rows_of_set(window, bins, sets, q) for window in windows]
            left[q, j * LANES : j * LANES + kept] = jnp.concatenate(pieces).T[:kept]

    def prepare_rotated(q, first, last):
        for lane in range(first, last, LANES):
            plain = right[q, :, lane : lane + LANES].astype(jnp.float32)
            at = slice(2 * channels + lane, 2 * channels + lane + LANES)
            right[q, :, at] = rotate(plain, within).astype(jnp.bfloat16)

    depth = left.shape[2]
    lane = lax.broadcasted_iota(jnp.int32, (1, depth), 1) & (within - 1)
    whole = 2 * channels // (2 * LANES) * (2 * LANES)
    starts = [0, whole, 4 * channels - whole, 4 * channels]
    left_over = 2 * channels - whole

    for q in range(sets):
        pl.when(which >= 1)(functools.partial(wait_for, which - 1, q))
        prepare(q)
        prepare_rotated(q, 0, left_over)
        for k in range(within):
            chosen = jnp.where(lane == k, left[q], 0.0).astype(jnp.bfloat16)

            def multiply(first, last):
                return jnp.dot(
                    chosen, right[q, :, first:last], preferred_element_type=jnp.float32
                ).astype(jnp.bfloat16)

            def send(part):
                for cut in range(cuts):
                    copy(which, q, k, cut, part).start()

            slots[q, k, 0, :, :whole] = multiply(*starts[:2])
            if left_over:
                both = multiply(*starts[1:3])
                slots[q, k, 0, :, whole:] = both[:, :left_over]
                slots[q, k, 1, :, :left_over] = both[:, left_over:]
            send(0)
            if k == 0:
                prepare_rotated(q, left_over, 2 * channels)
            slots[q, k, 1, :, left_over:] = multiply(*starts[2:])
            send(1)

    @pl.when(which == pl.num_programs(0) - 1)
    def _():
        for q in range(sets):
            wait_for(which, q)


def copy_kernel(in_ref, out_ref):
    out_ref[...] = in_ref[...]


def exchange(value, mask):
    pairs = [(source, source ^ mask) for source in range(lax.axis_size("freq"))]
    return lax.ppermute(value, "freq", pairs) if mask else value


def swap(value):
    return lax.ppermute(value, "chan", [(0, 1), (1, 0)])


def local(samples):
    local_channels, local_windows, length = samples.shape
    devices = lax.axis_size("freq")
    local_bins = BINS // devices
    windows = local_windows * devices
    bins = min(local_bins, 128 // (2 * devices))
    groups = local_bins // bins
    aligned = bins == 8
    group = bins if aligned else BINS
    table = jnp.asarray(bin_table(length, BINS, group))
    lanes = local_windows * local_channels
    vmem = pl.BlockSpec(memory_space=pltpu.VMEM)
    memory = pl.BlockSpec(memory_space=pl.ANY)
    masks = [*range(devices - 1, devices - 3, -1), 1, 2, *range(devices - 3, 2, -1), 0]
    masks = masks if aligned else [0]
    pieces = len(masks)
    rows = (devices, groups, 2 * bins, lanes) if aligned else (2 * BINS, lanes)
    piece = rows[1:] if aligned else rows
    with jax.named_scope("table"):
        table = pl.pallas_call(
            copy_kernel,
            out_shape=jax.ShapeDtypeStruct(table.shape, table.dtype),
            in_specs=[vmem],
            out_specs=vmem,
            compiler_params=pltpu.CompilerParams(vmem_limit_bytes=8 * MIB),
        )(table)
    spectrum = jnp.einsum("cws,sj->wcj", samples, table, preferred_element_type=jnp.float32)
    spectrum = spectrum.astype(jnp.bfloat16)
    with jax.named_scope("whiten"):
        whitened = pl.pallas_call(
            functools.partial(whiten_kernel, group, masks),
            out_shape=[jax.ShapeDtypeStruct(piece, jnp.bfloat16)] * pieces,
            in_specs=[vmem],
            out_specs=[vmem] * pieces,
            scratch_shapes=[pltpu.VMEM(rows, jnp.bfloat16)],
            compiler_params=pltpu.CompilerParams(vmem_limit_bytes=16 * MIB),
            cost_estimate=pl.CostEstimate(
                flops=40 * BINS * lanes, bytes_accessed=12 * BINS * lanes, transcendentals=BINS * lanes
            ),
        )(spectrum)
    if aligned:
        own = [exchange(value, mask) for mask, value in zip(masks, whitened)]
    else:
        rows = whitened[0].reshape(2, devices, groups, bins, lanes).transpose(1, 2, 0, 3, 4)
        rows = rows.reshape(devices, groups, 2 * bins, lanes)
        rows = lax.all_to_all(rows, "freq", split_axis=0, concat_axis=0, tiled=True)
        own = [rows.transpose(1, 0, 2, 3).reshape(groups, devices * 2 * bins, lanes)]
    other = [swap(value) for value in own]
    sets = 2 if aligned else 1
    depth = local_windows * devices * 2 * bins // sets
    with jax.named_scope("outer_products"):
        out = pl.pallas_call(
            functools.partial(outer_kernel, bins, sets, 1.0 / windows),
            out_shape=jax.ShapeDtypeStruct(
                (2, local_bins, local_channels, 2 * local_channels), jnp.bfloat16
            ),
            grid=(groups,),
            in_specs=[vmem] * (2 * pieces),
            out_specs=memory,
            scratch_shapes=[
                pltpu.VMEM((sets, depth, 4 * local_channels), jnp.bfloat16),
                pltpu.VMEM((sets, local_channels, depth), jnp.float32),
                pltpu.VMEM((sets, bins // sets, 2, local_channels, 2 * local_channels), jnp.bfloat16),
                pltpu.SemaphoreType.DMA((sets, bins // sets, 2, 2)),
            ],
            compiler_params=pltpu.CompilerParams(vmem_limit_bytes=48 * MIB),
            cost_estimate=pl.CostEstimate(
                flops=8 * local_bins * depth * local_channels * local_channels,
                bytes_accessed=8 * local_bins * local_channels * local_channels,
                transcendentals=0,
            ),
        )(*own, *other)
    return jnp.transpose(out, (0, 1, 3, 2))


def solution(mesh):
    placed = (P("chan", ("hours", "freq"), None),)
    return jax.shard_map(
        local,
        mesh=mesh,
        in_specs=placed,
        out_specs=P(None, ("hours", "freq"), None, "chan"),
        check_vma=False,
    )
```

```python
import functools
import math

import jax
import jax.numpy as jnp
import ml_dtypes
import numpy as np
from jax import lax
from jax.experimental import pallas as pl
from jax.experimental.pallas import tpu as pltpu
from jax.sharding import PartitionSpec as P

BINS = 128
LANES = 128
MIB = 1024 * 1024


def bin_table(length, bins, group):
    position = np.arange(length)[None, :]
    number = np.arange(1, bins + 1)[:, None]
    phase = (position * number % length).astype(np.float32) * np.float32(2.0 * math.pi / length)
    taper = np.float32(0.5) - np.float32(0.5) * np.cos(
        position.astype(np.float32) * np.float32(2.0 * math.pi / length)
    )
    factor = np.float32(math.sqrt(8.0 / (3.0 * length)))
    table = np.stack([taper * np.cos(phase), -(taper * np.sin(phase))]) * factor
    table = table.reshape(2, bins // group, group, length).transpose(3, 1, 0, 2)
    return table.reshape(length, 2 * bins).astype(ml_dtypes.bfloat16)


def channel_blocks(channels):
    return [
        (first, min(LANES, channels - first), 2 * first) for first in range(0, channels, LANES)
    ]


def whiten_kernel(group, masks, spectrum_ref, *refs):
    pieces, rows_ref = refs[:-1], refs[-1]
    windows, channels, columns = spectrum_ref.shape
    bins = columns // 2
    row = lax.broadcasted_iota(jnp.int32, (bins, 1), 0)
    count = jnp.minimum(row + 2, bins - 1) - jnp.maximum(row - 2, 0) + 1
    share = 1.0 / count.astype(jnp.float32)

    for first, width, lane in channel_blocks(channels):
        blocks = [
            spectrum_ref[w, first : first + width, :].astype(jnp.float32).T
            for w in range(windows)
        ]
        spectrum = jnp.concatenate(blocks, axis=1)
        cols = windows * width
        parts = spectrum.reshape(bins // group, 2, group, cols)
        power = (parts[:, 0] * parts[:, 0] + parts[:, 1] * parts[:, 1]).reshape(bins, cols)
        summed = power
        for step in (1, 2):
            summed = summed + jnp.where(row >= step, pltpu.roll(power, step, axis=0), 0.0)
            summed = summed + jnp.where(
                row < bins - step, pltpu.roll(power, bins - step, axis=0), 0.0
            )
        level = jnp.maximum(summed * share, 0.1)
        inverse = lax.rsqrt(level).reshape(bins // group, 1, group, cols)
        whitened = (parts * inverse).astype(jnp.bfloat16)
        rows_ref[..., lane : lane + cols] = whitened.reshape(rows_ref.shape[:-1] + (cols,))

    if len(pieces) == 1:
        pieces[0][...] = rows_ref[...]
    else:
        me = lax.axis_index("freq")
        for mask, piece in zip(masks, pieces):
            piece[...] = rows_ref[me ^ mask]


def swap_halves(tile):
    return pltpu.roll(tile, LANES // 2, axis=1)


def rows_of_set(tile, bins, sets, q):
    if sets == 1:
        return tile
    rows, lanes = tile.shape
    parts = tile.reshape(rows // (2 * bins), 2, bins, lanes)
    real, imag = parts[:, 0], parts[:, 1]
    within = bins // sets
    low = lax.broadcasted_iota(jnp.int32, real.shape, 1) < within
    if q == 0:
        found = jnp.where(low, real, pltpu.roll(imag, within, axis=1))
    else:
        found = jnp.where(low, pltpu.roll(real, within, axis=1), imag)
    return found.reshape(rows // sets, lanes)


def rotate(tile, within):
    rows, lanes = tile.shape
    if 2 * within == 8:
        pairs = tile.reshape(rows // 8, 8, lanes)
        low = lax.broadcasted_iota(jnp.int32, pairs.shape, 1) < within
        turned = pltpu.roll(pairs, within, axis=1)
        return jnp.where(low, -turned, turned).reshape(rows, lanes)
    first_part = (lax.broadcasted_iota(jnp.int32, (rows, 1), 0) // within) % 2 == 0
    return jnp.where(
        first_part, -pltpu.roll(tile, rows - within, axis=0), pltpu.roll(tile, within, axis=0)
    )


def outer_kernel(bins, sets, scale, *refs):
    out_ref, right, left, slots, sems = refs[-5:]
    count = (len(refs) - 5) // 2
    own_refs, other_refs = refs[:count], refs[count:-5]
    half = LANES // 2
    channels = out_ref.shape[2]
    full = channels // LANES
    which = pl.program_id(0)
    within = bins // sets
    cuts = sems.shape[2]
    size = channels // cuts

    def copy(group, q, k, cut, part):
        at = pl.ds(cut * size, size)
        return pltpu.make_async_copy(
            slots.at[q, k, part, at],
            out_ref.at[part, group * bins + q * within + k, at],
            sems.at[q, k, cut, part],
        )

    def wait_for(group, q):
        for k in range(within):
            for cut in range(cuts):
                for part in range(2):
                    copy(group, q, k, cut, part).wait()

    def prepare(q):
        me = lax.axis_index("chan")
        own = jnp.concatenate([ref[which].astype(jnp.float32) for ref in own_refs])
        other = jnp.concatenate([ref[which].astype(jnp.float32) for ref in other_refs])
        rows = own.shape[0]
        block0 = jnp.where(me == 0, own, other)
        block1 = jnp.where(me == 0, other, own)
        low = lax.broadcasted_iota(jnp.int32, (rows, LANES), 1) < half

        def tiles_of(block, w):
            tiles = [
                block[:, (2 * j + w) * LANES : (2 * j + w + 1) * LANES] for j in range(full)
            ]
            last = block[:, 2 * full * LANES :]
            turned = swap_halves(last)
            both = jnp.where(low, last, turned) if w == 0 else jnp.where(low, turned, last)
            return tiles, both

        share = rows // sets
        for w in range(2):
            at = pl.ds(w * share, share)
            tiles, last0 = tiles_of(block0, w)
            tiles1, last1 = tiles_of(block1, w)
            turned = [swap_halves(tile) for tile in tiles1]
            chain = [last0] + turned + [last1]
            tiles = tiles + [
                jnp.where(low, chain[j], chain[j + 1]) for j in range(len(chain) - 1)
            ]
            for j, tile in enumerate(tiles):
                lanes = slice(j * LANES, (j + 1) * LANES)
                right[q, at, lanes] = rows_of_set(tile, bins, sets, q).astype(jnp.bfloat16)
        scaled = own * scale
        for j in range(full + 1):
            block = scaled[:, 2 * j * LANES : (2 * j + 2) * LANES]
            if j < full:
                windows = [block[:, :LANES], block[:, LANES:]]
            else:
                windows = [block, swap_halves(block)]
            kept = min(LANES, channels - j * LANES)
            pieces = [rows_of_set(window, bins, sets, q) for window in windows]
            left[q, j * LANES : j * LANES + kept] = jnp.concatenate(pieces).T[:kept]

    def prepare_rotated(q, first, last):
        for lane in range(first, last, LANES):
            plain = right[q, :, lane : lane + LANES].astype(jnp.float32)
            at = slice(2 * channels + lane, 2 * channels + lane + LANES)
            right[q, :, at] = rotate(plain, within).astype(jnp.bfloat16)

    depth = left.shape[2]
    lane = lax.broadcasted_iota(jnp.int32, (1, depth), 1) & (within - 1)
    whole = 2 * channels // (2 * LANES) * (2 * LANES)
    starts = [0, whole, 4 * channels - whole, 4 * channels]
    left_over = 2 * channels - whole

    for q in range(sets):
        pl.when(which >= 1)(functools.partial(wait_for, which - 1, q))
        prepare(q)
        prepare_rotated(q, 0, left_over)
        for k in range(within):
            chosen = jnp.where(lane == k, left[q], 0.0).astype(jnp.bfloat16)

            def multiply(first, last):
                return jnp.dot(
                    chosen, right[q, :, first:last], preferred_element_type=jnp.float32
                ).astype(jnp.bfloat16)

            def send(part):
                for cut in range(cuts):
                    copy(which, q, k, cut, part).start()

            slots[q, k, 0, :, :whole] = multiply(*starts[:2])
            if left_over:
                both = multiply(*starts[1:3])
                slots[q, k, 0, :, whole:] = both[:, :left_over]
                slots[q, k, 1, :, :left_over] = both[:, left_over:]
            send(0)
            if k == 0:
                prepare_rotated(q, left_over, 2 * channels)
            slots[q, k, 1, :, left_over:] = multiply(*starts[2:])
            send(1)

    @pl.when(which == pl.num_programs(0) - 1)
    def _():
        for q in range(sets):
            wait_for(which, q)


def copy_kernel(in_ref, out_ref):
    out_ref[...] = in_ref[...]


def exchange(value, mask):
    pairs = [(source, source ^ mask) for source in range(lax.axis_size("freq"))]
    return lax.ppermute(value, "freq", pairs) if mask else value


def swap(value):
    return lax.ppermute(value, "chan", [(0, 1), (1, 0)])


def local(samples):
    local_channels, local_windows, length = samples.shape
    devices = lax.axis_size("freq")
    local_bins = BINS // devices
    windows = local_windows * devices
    bins = min(local_bins, 128 // (2 * devices))
    groups = local_bins // bins
    aligned = bins == 8
    group = bins if aligned else BINS
    table = jnp.asarray(bin_table(length, BINS, group))
    lanes = local_windows * local_channels
    vmem = pl.BlockSpec(memory_space=pltpu.VMEM)
    memory = pl.BlockSpec(memory_space=pl.ANY)
    masks = [*range(devices - 1, devices - 3, -1), 1, 2, devices - 3, 3]
    masks = [*masks, *(mask for mask in range(devices - 4, 3, -1)), 0]
    masks = masks if aligned else [0]
    pieces = len(masks)
    rows = (devices, groups, 2 * bins, lanes) if aligned else (2 * BINS, lanes)
    piece = rows[1:] if aligned else rows
    with jax.named_scope("table"):
        table = pl.pallas_call(
            copy_kernel,
            out_shape=jax.ShapeDtypeStruct(table.shape, table.dtype),
            in_specs=[vmem],
            out_specs=vmem,
            compiler_params=pltpu.CompilerParams(vmem_limit_bytes=8 * MIB),
        )(table)
    spectrum = jnp.einsum("cws,sj->wcj", samples, table, preferred_element_type=jnp.float32)
    spectrum = spectrum.astype(jnp.bfloat16)
    with jax.named_scope("whiten"):
        whitened = pl.pallas_call(
            functools.partial(whiten_kernel, group, masks),
            out_shape=[jax.ShapeDtypeStruct(piece, jnp.bfloat16)] * pieces,
            in_specs=[vmem],
            out_specs=[vmem] * pieces,
            scratch_shapes=[pltpu.VMEM(rows, jnp.bfloat16)],
            compiler_params=pltpu.CompilerParams(vmem_limit_bytes=16 * MIB),
            cost_estimate=pl.CostEstimate(
                flops=40 * BINS * lanes, bytes_accessed=12 * BINS * lanes, transcendentals=BINS * lanes
            ),
        )(spectrum)
    if aligned:
        own = [exchange(value, mask) for mask, value in zip(masks, whitened)]
    else:
        rows = whitened[0].reshape(2, devices, groups, bins, lanes).transpose(1, 2, 0, 3, 4)
        rows = rows.reshape(devices, groups, 2 * bins, lanes)
        rows = lax.all_to_all(rows, "freq", split_axis=0, concat_axis=0, tiled=True)
        own = [rows.transpose(1, 0, 2, 3).reshape(groups, devices * 2 * bins, lanes)]
    other = [swap(value) for value in own]
    sets = 2 if aligned else 1
    depth = local_windows * devices * 2 * bins // sets
    with jax.named_scope("outer_products"):
        out = pl.pallas_call(
            functools.partial(outer_kernel, bins, sets, 1.0 / windows),
            out_shape=jax.ShapeDtypeStruct(
                (2, local_bins, local_channels, 2 * local_channels), jnp.bfloat16
            ),
            grid=(groups,),
            in_specs=[vmem] * (2 * pieces),
            out_specs=memory,
            scratch_shapes=[
                pltpu.VMEM((sets, depth, 4 * local_channels), jnp.bfloat16),
                pltpu.VMEM((sets, local_channels, depth), jnp.float32),
                pltpu.VMEM((sets, bins // sets, 2, local_channels, 2 * local_channels), jnp.bfloat16),
                pltpu.SemaphoreType.DMA((sets, bins // sets, 2, 2)),
            ],
            compiler_params=pltpu.CompilerParams(vmem_limit_bytes=48 * MIB),
            cost_estimate=pl.CostEstimate(
                flops=8 * local_bins * depth * local_channels * local_channels,
                bytes_accessed=8 * local_bins * local_channels * local_channels,
                transcendentals=0,
            ),
        )(*own, *other)
    return jnp.transpose(out, (0, 1, 3, 2))


def solution(mesh):
    placed = (P("chan", ("hours", "freq"), None),)
    return jax.shard_map(
        local,
        mesh=mesh,
        in_specs=placed,
        out_specs=P(None, ("hours", "freq"), None, "chan"),
        check_vma=False,
    )
```

```python
import functools
import math

import jax
import jax.numpy as jnp
import ml_dtypes
import numpy as np
from jax import lax
from jax.experimental import pallas as pl
from jax.experimental.pallas import tpu as pltpu
from jax.sharding import PartitionSpec as P

BINS = 128
LANES = 128
MIB = 1024 * 1024


def bin_table(length, bins, group):
    position = np.arange(length)[None, :]
    number = np.arange(1, bins + 1)[:, None]
    phase = (position * number % length).astype(np.float32) * np.float32(2.0 * math.pi / length)
    taper = np.float32(0.5) - np.float32(0.5) * np.cos(
        position.astype(np.float32) * np.float32(2.0 * math.pi / length)
    )
    factor = np.float32(math.sqrt(8.0 / (3.0 * length)))
    table = np.stack([taper * np.cos(phase), -(taper * np.sin(phase))]) * factor
    table = table.reshape(2, bins // group, group, length).transpose(3, 1, 0, 2)
    return table.reshape(length, 2 * bins).astype(ml_dtypes.bfloat16)


def channel_blocks(channels):
    return [
        (first, min(LANES, channels - first), 2 * first) for first in range(0, channels, LANES)
    ]


def whiten_kernel(group, masks, spectrum_ref, *refs):
    pieces, rows_ref = refs[:-1], refs[-1]
    windows, channels, columns = spectrum_ref.shape
    bins = columns // 2
    row = lax.broadcasted_iota(jnp.int32, (bins, 1), 0)
    count = jnp.minimum(row + 2, bins - 1) - jnp.maximum(row - 2, 0) + 1
    share = 1.0 / count.astype(jnp.float32)

    for first, width, lane in channel_blocks(channels):
        blocks = [
            spectrum_ref[w, first : first + width, :].astype(jnp.float32).T
            for w in range(windows)
        ]
        spectrum = jnp.concatenate(blocks, axis=1)
        cols = windows * width
        parts = spectrum.reshape(bins // group, 2, group, cols)
        power = (parts[:, 0] * parts[:, 0] + parts[:, 1] * parts[:, 1]).reshape(bins, cols)
        summed = power
        for step in (1, 2):
            summed = summed + jnp.where(row >= step, pltpu.roll(power, step, axis=0), 0.0)
            summed = summed + jnp.where(
                row < bins - step, pltpu.roll(power, bins - step, axis=0), 0.0
            )
        level = jnp.maximum(summed * share, 0.1)
        inverse = lax.rsqrt(level).reshape(bins // group, 1, group, cols)
        whitened = (parts * inverse).astype(jnp.bfloat16)
        rows_ref[..., lane : lane + cols] = whitened.reshape(rows_ref.shape[:-1] + (cols,))

    if len(pieces) == 1:
        pieces[0][...] = rows_ref[...]
    else:
        me = lax.axis_index("freq")
        for mask, piece in zip(masks, pieces):
            piece[...] = rows_ref[me ^ mask]


def swap_halves(tile):
    return pltpu.roll(tile, LANES // 2, axis=1)


def rows_of_set(tile, bins, sets, q):
    if sets == 1:
        return tile
    rows, lanes = tile.shape
    parts = tile.reshape(rows // (2 * bins), 2, bins, lanes)
    real, imag = parts[:, 0], parts[:, 1]
    within = bins // sets
    low = lax.broadcasted_iota(jnp.int32, real.shape, 1) < within
    if q == 0:
        found = jnp.where(low, real, pltpu.roll(imag, within, axis=1))
    else:
        found = jnp.where(low, pltpu.roll(real, within, axis=1), imag)
    return found.reshape(rows // sets, lanes)


def rotate(tile, within):
    rows, lanes = tile.shape
    if 2 * within == 8:
        pairs = tile.reshape(rows // 8, 8, lanes)
        low = lax.broadcasted_iota(jnp.int32, pairs.shape, 1) < within
        turned = pltpu.roll(pairs, within, axis=1)
        return jnp.where(low, -turned, turned).reshape(rows, lanes)
    first_part = (lax.broadcasted_iota(jnp.int32, (rows, 1), 0) // within) % 2 == 0
    return jnp.where(
        first_part, -pltpu.roll(tile, rows - within, axis=0), pltpu.roll(tile, within, axis=0)
    )


def outer_kernel(bins, sets, scale, *refs):
    out_ref, right, left, slots, sems = refs[-5:]
    count = (len(refs) - 5) // 2
    own_refs, other_refs = refs[:count], refs[count:-5]
    half = LANES // 2
    channels = out_ref.shape[2]
    full = channels // LANES
    which = pl.program_id(0)
    within = bins // sets
    cuts = sems.shape[2]
    size = channels // cuts

    def copy(group, q, k, cut, part):
        at = pl.ds(cut * size, size)
        return pltpu.make_async_copy(
            slots.at[q, k, part, at],
            out_ref.at[part, group * bins + q * within + k, at],
            sems.at[q, k, cut, part],
        )

    def wait_for(group, q):
        for k in range(within):
            for cut in range(cuts):
                for part in range(2):
                    copy(group, q, k, cut, part).wait()

    def prepare(q):
        me = lax.axis_index("chan")
        own = jnp.concatenate([ref[which].astype(jnp.float32) for ref in own_refs])
        other = jnp.concatenate([ref[which].astype(jnp.float32) for ref in other_refs])
        rows = own.shape[0]
        block0 = jnp.where(me == 0, own, other)
        block1 = jnp.where(me == 0, other, own)
        low = lax.broadcasted_iota(jnp.int32, (rows, LANES), 1) < half

        def tiles_of(block, w):
            tiles = [
                block[:, (2 * j + w) * LANES : (2 * j + w + 1) * LANES] for j in range(full)
            ]
            last = block[:, 2 * full * LANES :]
            turned = swap_halves(last)
            both = jnp.where(low, last, turned) if w == 0 else jnp.where(low, turned, last)
            return tiles, both

        share = rows // sets
        for w in range(2):
            at = pl.ds(w * share, share)
            tiles, last0 = tiles_of(block0, w)
            tiles1, last1 = tiles_of(block1, w)
            turned = [swap_halves(tile) for tile in tiles1]
            chain = [last0] + turned + [last1]
            tiles = tiles + [
                jnp.where(low, chain[j], chain[j + 1]) for j in range(len(chain) - 1)
            ]
            for j, tile in enumerate(tiles):
                lanes = slice(j * LANES, (j + 1) * LANES)
                right[q, at, lanes] = rows_of_set(tile, bins, sets, q).astype(jnp.bfloat16)
        scaled = own * scale
        for j in range(full + 1):
            block = scaled[:, 2 * j * LANES : (2 * j + 2) * LANES]
            if j < full:
                windows = [block[:, :LANES], block[:, LANES:]]
            else:
                windows = [block, swap_halves(block)]
            kept = min(LANES, channels - j * LANES)
            pieces = [rows_of_set(window, bins, sets, q) for window in windows]
            left[q, j * LANES : j * LANES + kept] = jnp.concatenate(pieces).T[:kept]

    def prepare_rotated(q, first, last):
        for lane in range(first, last, LANES):
            plain = right[q, :, lane : lane + LANES].astype(jnp.float32)
            at = slice(2 * channels + lane, 2 * channels + lane + LANES)
            right[q, :, at] = rotate(plain, within).astype(jnp.bfloat16)

    depth = left.shape[2]
    lane = lax.broadcasted_iota(jnp.int32, (1, depth), 1) & (within - 1)
    whole = 2 * channels // (2 * LANES) * (2 * LANES)
    starts = [0, whole, 4 * channels - whole, 4 * channels]
    left_over = 2 * channels - whole

    for q in range(sets):
        pl.when(which >= 1)(functools.partial(wait_for, which - 1, q))
        prepare(q)
        prepare_rotated(q, 0, left_over)
        for k in range(within):
            chosen = jnp.where(lane == k, left[q], 0.0).astype(jnp.bfloat16)

            def multiply(first, last):
                return jnp.dot(
                    chosen, right[q, :, first:last], preferred_element_type=jnp.float32
                ).astype(jnp.bfloat16)

            def send(part):
                for cut in range(cuts):
                    copy(which, q, k, cut, part).start()

            slots[q, k, 0, :, :whole] = multiply(*starts[:2])
            if left_over:
                both = multiply(*starts[1:3])
                slots[q, k, 0, :, whole:] = both[:, :left_over]
                slots[q, k, 1, :, :left_over] = both[:, left_over:]
            send(0)
            if k == 0:
                prepare_rotated(q, left_over, 2 * channels)
            slots[q, k, 1, :, left_over:] = multiply(*starts[2:])
            send(1)

    @pl.when(which == pl.num_programs(0) - 1)
    def _():
        for q in range(sets):
            wait_for(which, q)


def copy_kernel(in_ref, out_ref):
    out_ref[...] = in_ref[...]


def exchange(value, mask):
    pairs = [(source, source ^ mask) for source in range(lax.axis_size("freq"))]
    return lax.ppermute(value, "freq", pairs) if mask else value


def swap(value):
    return lax.ppermute(value, "chan", [(0, 1), (1, 0)])


def local(samples):
    local_channels, local_windows, length = samples.shape
    devices = lax.axis_size("freq")
    local_bins = BINS // devices
    windows = local_windows * devices
    bins = min(local_bins, 128 // (2 * devices))
    groups = local_bins // bins
    aligned = bins == 8
    group = bins if aligned else BINS
    table = jnp.asarray(bin_table(length, BINS, group))
    lanes = local_windows * local_channels
    vmem = pl.BlockSpec(memory_space=pltpu.VMEM)
    memory = pl.BlockSpec(memory_space=pl.ANY)
    masks = [*range(devices - 1, devices - 3, -1), 2, 3, devices - 3, 1]
    masks = [*masks, *(mask for mask in range(devices - 4, 3, -1)), 0]
    masks = masks if aligned else [0]
    pieces = len(masks)
    rows = (devices, groups, 2 * bins, lanes) if aligned else (2 * BINS, lanes)
    piece = rows[1:] if aligned else rows
    with jax.named_scope("table"):
        table = pl.pallas_call(
            copy_kernel,
            out_shape=jax.ShapeDtypeStruct(table.shape, table.dtype),
            in_specs=[vmem],
            out_specs=vmem,
            compiler_params=pltpu.CompilerParams(vmem_limit_bytes=8 * MIB),
        )(table)
    spectrum = jnp.einsum("cws,sj->wcj", samples, table, preferred_element_type=jnp.float32)
    spectrum = spectrum.astype(jnp.bfloat16)
    with jax.named_scope("whiten"):
        whitened = pl.pallas_call(
            functools.partial(whiten_kernel, group, masks),
            out_shape=[jax.ShapeDtypeStruct(piece, jnp.bfloat16)] * pieces,
            in_specs=[vmem],
            out_specs=[vmem] * pieces,
            scratch_shapes=[pltpu.VMEM(rows, jnp.bfloat16)],
            compiler_params=pltpu.CompilerParams(vmem_limit_bytes=16 * MIB),
            cost_estimate=pl.CostEstimate(
                flops=40 * BINS * lanes, bytes_accessed=12 * BINS * lanes, transcendentals=BINS * lanes
            ),
        )(spectrum)
    if aligned:
        own = [exchange(value, mask) for mask, value in zip(masks, whitened)]
    else:
        rows = whitened[0].reshape(2, devices, groups, bins, lanes).transpose(1, 2, 0, 3, 4)
        rows = rows.reshape(devices, groups, 2 * bins, lanes)
        rows = lax.all_to_all(rows, "freq", split_axis=0, concat_axis=0, tiled=True)
        own = [rows.transpose(1, 0, 2, 3).reshape(groups, devices * 2 * bins, lanes)]
    other = [swap(value) for value in own]
    sets = 2 if aligned else 1
    depth = local_windows * devices * 2 * bins // sets
    with jax.named_scope("outer_products"):
        out = pl.pallas_call(
            functools.partial(outer_kernel, bins, sets, 1.0 / windows),
            out_shape=jax.ShapeDtypeStruct(
                (2, local_bins, local_channels, 2 * local_channels), jnp.bfloat16
            ),
            grid=(groups,),
            in_specs=[vmem] * (2 * pieces),
            out_specs=memory,
            scratch_shapes=[
                pltpu.VMEM((sets, depth, 4 * local_channels), jnp.bfloat16),
                pltpu.VMEM((sets, local_channels, depth), jnp.float32),
                pltpu.VMEM((sets, bins // sets, 2, local_channels, 2 * local_channels), jnp.bfloat16),
                pltpu.SemaphoreType.DMA((sets, bins // sets, 2, 2)),
            ],
            compiler_params=pltpu.CompilerParams(vmem_limit_bytes=48 * MIB),
            cost_estimate=pl.CostEstimate(
                flops=8 * local_bins * depth * local_channels * local_channels,
                bytes_accessed=8 * local_bins * local_channels * local_channels,
                transcendentals=0,
            ),
        )(*own, *other)
    return jnp.transpose(out, (0, 1, 3, 2))


def solution(mesh):
    placed = (P("chan", ("hours", "freq"), None),)
    return jax.shard_map(
        local,
        mesh=mesh,
        in_specs=placed,
        out_specs=P(None, ("hours", "freq"), None, "chan"),
        check_vma=False,
    )
```
